32 devices in a mesh: row: 4 (over y, x), col: 8 (over z, core).
Axes of the slice: x: 2, y: 2, z: 4, core: 2. Of those that a mesh axis runs over, the one named last changes fastest.
Arguments:
- observed: float32 [4, 32768], P(None, ('row', 'col')), may hold values from -50 to 50
- tile_values: bfloat16 [128, 16, 256, 256], P('row', 'col'), may hold values from -3.203125 to 3.203125
- tile_cols: int32 [128, 16], P('row', 'col'), may hold values from 0 to 511
Outputs:
- solution: float32 [4, 1048576], P(None, ('col', 'row'))
- residual_ratio: float32 [4], replicated
The draws below stay inside these ranges and needn't reach their ends.
All inputs are finite; a program needn't handle non-finite values.
Results may differ from the reference program's by a relative error of at most 0.0021.
Values may be sent and summed in bfloat16 or wider, within the bound.
No kernel may reach another device: no remote copies, remote signals or barrier semaphores. Data moves between devices by JAX's collectives and lax.ppermute only.
A program may use at most 128 MiB of HBM per device.

```python
import math
import jax
import jax.numpy as jnp
from jax import lax

TS = 256
KR = 2
NRHS = 4
ITERS = 2
N = 1048576
CB = 512
M = 32768
GROUPS = 16
TILE_ROWS = 128


def rise_factor(count, top_value):
    position = jnp.arange(count, dtype=jnp.float32) / max(count - 1, 1)
    return top_value ** position


def draw_observed(key, part):
    key_base, key_rough = jax.random.split(key)
    tiles_along = M // TS
    roughness = jnp.exp(jax.random.uniform(key_rough, (tiles_along,), jnp.float32, 0.0, math.log(10.0 / 3.0)))
    base_values = jnp.clip(jax.random.normal(key_base, (NRHS, M), jnp.float32), -4.0, 4.0)
    trend = rise_factor(tiles_along, 3.0)
    scales = jnp.repeat(roughness * trend, TS)
    return base_values * scales[None, :]


def draw_tile_values(key, part):
    key_base, key_rough = jax.random.split(key)
    sigma = (GROUPS * TS) ** (-0.5)
    roughness = jnp.exp(jax.random.uniform(key_rough, (TILE_ROWS, GROUPS), jnp.float32, 0.0, math.log(10.0 / 3.0)))
    base_values = jnp.clip(jax.random.normal(key_base, (TILE_ROWS, GROUPS, TS, TS), jnp.float32), -4.0, 4.0)
    top_value = 3.0
    row_scale = rise_factor(TILE_ROWS, top_value)
    col_scale = jnp.repeat(rise_factor(GROUPS // KR, top_value), KR)
    scales = sigma * roughness * row_scale[:, None] * col_scale[None, :]
    return (base_values * scales[:, :, None, None]).astype(jnp.bfloat16)


def place_ends(result, stream_key, least, high):
    longest = result.shape.index(max(result.shape))
    spots = []
    for shift in (0, 1):
        where = [jax.random.randint(jax.random.fold_in(stream_key, axis), (), 0, length) for axis, length in enumerate(result.shape)]
        where[longest] = (where[longest] + shift) % result.shape[longest]
        spots.append(tuple(where))
    return result.at[spots[0]].set(least).at[spots[1]].set(high)


def setup_inputs(seed: int = 0) -> dict:
    keys = jax.random.split(jax.random.key(seed), 4)
    return {
        "observed": draw_observed(jax.random.fold_in(keys[3], 71), 0),
        "tile_values": draw_tile_values(jax.random.fold_in(keys[3], 71), 0),
        "tile_cols": place_ends(jax.random.randint(keys[2], (TILE_ROWS, GROUPS), 0, CB), jax.random.fold_in(keys[2], 1), 0, CB - 1).astype(jnp.int32),
    }


epsilon_sq = 1e-06
group_rows = 8

def column_index(tile_cols):
    offsets = jnp.arange(tile_cols.shape[1], dtype=jnp.int32) // KR * CB
    return (tile_cols + offsets[None, :]).astype(jnp.int32)

def forward_map(tiles_grouped, index_grouped, right_bf):
    panel = right_bf.astype(jnp.float32).reshape(NRHS, N // TS, TS)

    def one_group(inputs):
        block_tiles, block_index = inputs
        picked = panel[:, block_index]
        return jnp.einsum('rktj,nrkj->nrt', block_tiles.astype(jnp.float32), picked)
    pieces = lax.map(one_group, (tiles_grouped, index_grouped))
    return jnp.transpose(pieces, (1, 0, 2, 3)).reshape(NRHS, M)

def adjoint_map(tiles_grouped, index_grouped, left_bf):
    rows_grouped = jnp.transpose(left_bf.astype(jnp.float32).reshape(NRHS, TILE_ROWS // group_rows, group_rows, TS), (1, 0, 2, 3))

    def one_group(running, inputs):
        block_tiles, block_index, block_rows = inputs
        tile_terms = jnp.einsum('rktj,nrt->nrkj', block_tiles.astype(jnp.float32), block_rows)
        return (running.at[:, block_index].add(tile_terms), None)
    initial = jnp.zeros((NRHS, N // TS, TS), jnp.float32)
    running = lax.scan(one_group, initial, (tiles_grouped, index_grouped, rows_grouped))[0]
    return running.reshape(NRHS, N)

def lane_norms(values):
    return jnp.sqrt(lax.optimization_barrier(jnp.sum(values * values, axis=1)) + epsilon_sq)

def reference(observed, tile_values, tile_cols):
    columns = column_index(tile_cols)
    tiles_grouped = tile_values.reshape(TILE_ROWS // group_rows, group_rows, GROUPS, TS, TS)
    index_grouped = columns.reshape(TILE_ROWS // group_rows, group_rows, GROUPS)
    beta_norm = lane_norms(observed)
    first_beta = beta_norm
    left_vec = observed / beta_norm[:, None]
    right_raw = adjoint_map(tiles_grouped, index_grouped, observed.astype(jnp.bfloat16)) / beta_norm[:, None]
    alpha_norm = lane_norms(right_raw)
    right_vec = right_raw / alpha_norm[:, None]
    right_bf = right_raw.astype(jnp.bfloat16)
    phibar = beta_norm
    rhobar = alpha_norm
    direction = right_vec
    solution = jnp.zeros_like(right_vec)
    for iteration in range(ITERS):
        left_raw = forward_map(tiles_grouped, index_grouped, right_bf) / alpha_norm[:, None] - alpha_norm[:, None] * left_vec
        product = adjoint_map(tiles_grouped, index_grouped, left_raw.astype(jnp.bfloat16))
        beta_norm = lane_norms(left_raw)
        right_raw = product / beta_norm[:, None] - beta_norm[:, None] * right_vec
        alpha_norm = lane_norms(right_raw)
        left_vec = left_raw / beta_norm[:, None]
        right_vec = right_raw / alpha_norm[:, None]
        right_bf = right_raw.astype(jnp.bfloat16)
        rho_val = jnp.sqrt(rhobar * rhobar + beta_norm * beta_norm)
        cosine = rhobar / rho_val
        sine_val = beta_norm / rho_val
        theta_val = sine_val * alpha_norm
        rhobar = -cosine * alpha_norm
        phi_val = cosine * phibar
        phibar = sine_val * phibar
        solution = solution + (phi_val / rho_val)[:, None] * direction
        direction = right_vec - (theta_val / rho_val)[:, None] * direction
    return (solution, phibar / first_beta)
```

```python
import functools

import jax
import jax.numpy as jnp
from jax import lax
from jax.experimental import pallas as pl
from jax.experimental.pallas import tpu as pltpu
from jax.sharding import PartitionSpec as P

ITERS = 2
N = 1048576
epsilon_sq = 1e-06
LANES = 128
VMEM = pl.BlockSpec(memory_space=pltpu.VMEM)
SMEM = pl.BlockSpec(memory_space=pltpu.SMEM)
ANY = pl.BlockSpec(memory_space=pl.ANY)
PARAMS = pltpu.CompilerParams(vmem_limit_bytes=40 * 1024 * 1024)


def tree_sum(parts):
    while len(parts) > 1:
        parts = [parts[i] + parts[i + 1] for i in range(0, len(parts), 2)]
    return parts[0]


def lane_total(acc):
    rows = jnp.broadcast_to(jnp.sum(acc, axis=1, keepdims=True), acc.shape)
    return rows + pltpu.roll(rows, 4, 0)


def norm_of(acc):
    return jnp.sqrt(lane_total(acc) + epsilon_sq)


def low_half():
    return lax.broadcasted_iota(jnp.int32, (8, LANES), 0) < 4


def wide_to_block(wide, upper):
    first, second = wide[:, :LANES], wide[:, LANES:]
    if upper:
        return jnp.where(low_half(), pltpu.roll(first, 4, 0), second)
    return jnp.where(low_half(), first, pltpu.roll(second, 4, 0))


def write_payload(out_ref, blocks, acc):
    rows = out_ref.shape[0]
    first, second = [], []
    low = low_half()
    for q in range(0, len(blocks), 2):
        first.append(jnp.where(low, blocks[q], pltpu.roll(blocks[q + 1], 4, 0)))
        second.append(jnp.where(low, pltpu.roll(blocks[q], 4, 0), blocks[q + 1]))
    while len(first) * 8 < rows:
        first.append(jnp.zeros((8, LANES), jnp.float32))
        second.append(jnp.zeros((8, LANES), jnp.float32))
    out_ref[:, :LANES] = jnp.concatenate(first, axis=0).astype(jnp.bfloat16)
    out_ref[:, LANES : 2 * LANES] = jnp.concatenate(second, axis=0).astype(jnp.bfloat16)
    upper = acc.astype(jnp.bfloat16).astype(jnp.float32)
    pieces = [upper, acc - upper] + [jnp.zeros((8, LANES), jnp.float32)] * (rows // 8 - 2)
    out_ref[:, 2 * LANES :] = jnp.concatenate(pieces, axis=0).astype(jnp.bfloat16)


def read_squares(ref):
    both = ref[:, 2 * LANES :].astype(jnp.float32)
    return both[:8] + both[8:16]


def prepare_kernel(obs_ref, blocks_ref, payload_ref):
    obs = obs_ref[...]
    blocks = []
    for q in range(obs.shape[1] // (2 * LANES)):
        at = q * 2 * LANES
        blocks.append(jnp.concatenate([obs[:, at : at + LANES], obs[:, at + LANES : at + 2 * LANES]], axis=0))
    for q, block in enumerate(blocks):
        blocks_ref[q] = block
    write_payload(payload_ref, blocks, tree_sum([b * b for b in blocks]))


def fetch_tiles(tiles_ref, held, sems, me, shares):
    per_share = tiles_ref.shape[0] // shares
    copies = []
    for d in range(shares):
        start = jnp.bitwise_xor(me, d) * per_share
        copies.append(pltpu.make_async_copy(tiles_ref.at[pl.ds(start, per_share)], held.at[d], sems.at[d]))
        copies[-1].start()
    return copies


def adjoint_kernel(shares, pos_ref, tiles_ref, *refs):
    payloads = refs[:shares]
    out_ref, held, sems = refs[shares:]
    me = pos_ref[1]
    per_share, per_block = held.shape[1], held.shape[2]
    copies = fetch_tiles(tiles_ref, held, sems, me, shares)
    total = held.shape[0] * per_share * per_block
    out_ref[total] = tree_sum([read_squares(p) for p in payloads])
    for d in range(shares):
        copies[d].wait()
        rays = payloads[d][:, : 2 * LANES]
        base = jnp.bitwise_xor(me, d) * (per_share * per_block)
        for q in range(per_share):
            for k in range(per_block):
                wide = jnp.dot(rays, held[d, q, k], preferred_element_type=jnp.float32)
                at = 8 * (q // 2)
                out_ref[base + q * per_block + k] = wide_to_block(wide[at : at + 8], q % 2 == 1)


def voxel_kernel(shares, rows, first, pos_ref, cols_ref, tiles_ref, *refs):
    refs = list(refs)
    terms = [refs.pop(0) for _ in range(rows)]
    if not first:
        right_ref, alpha_ref = refs.pop(0), refs.pop(0)
    outs = [refs.pop(0) for _ in range(shares)]
    beta_ref, raw_ref, term_buf, held, term_sems, tile_sems = refs
    my_row, me = pos_ref[0], pos_ref[1]
    per_share, per_block = held.shape[1], held.shape[2]
    per_row = shares * per_share * per_block
    pitch = per_row + 1
    term_copies = []
    for d in range(rows):
        slot = jnp.bitwise_xor(my_row, d)
        term_copies.append(pltpu.make_async_copy(terms[d], term_buf.at[slot], term_sems.at[d]))
        term_copies[-1].start()
    copies = fetch_tiles(tiles_ref, held, tile_sems, me, shares)
    col_tiles = raw_ref.shape[0]
    chunk = 16
    zeros = jnp.zeros((chunk, 8, LANES), jnp.float32)

    @pl.loop(0, col_tiles // chunk)
    def _(step):
        raw_ref[pl.ds(step * chunk, chunk)] = zeros

    for copy in term_copies:
        copy.wait()
    beta = norm_of(tree_sum([term_buf[s, per_row] for s in range(rows)]))
    beta_ref[...] = beta
    unroll = 8
    for s in range(rows):
        col_base = jnp.bitwise_xor(my_row, s) * per_row

        @pl.loop(0, per_row // unroll)
        def _(step):
            for u in range(unroll):
                t = step * unroll + u
                col = cols_ref[col_base + t]
                raw_ref[col] = raw_ref[col] + term_buf[s, t]

    beta_inv = 1.0 / beta
    if not first:
        right_scale = beta / alpha_ref[...]

    def scale(step, acc):
        at = pl.ds(step * chunk, chunk)
        raw = raw_ref[at] * beta_inv
        if not first:
            raw = raw - right_ref[at] * right_scale
        raw_ref[at] = raw
        return acc + jnp.sum(raw * raw, axis=0)

    acc = lax.fori_loop(0, col_tiles // chunk, scale, jnp.zeros((8, LANES), jnp.float32))
    for d in range(shares):
        copies[d].wait()
        base = jnp.bitwise_xor(me, d) * (per_share * per_block)
        for q in range(per_share):
            wide = None
            for k in range(per_block):
                block = raw_ref[cols_ref[base + q * per_block + k]]
                lhs = jnp.concatenate([block, pltpu.roll(block, 4, 0)], axis=1).astype(jnp.bfloat16)
                part = lax.dot_general(
                    lhs, held[d, q, k], (((1,), (1,)), ((), ())), preferred_element_type=jnp.float32
                )
                wide = part if wide is None else wide + part
            outs[d][q] = wide_to_block(wide, False)
        outs[d][per_share] = acc


def ray_kernel(shares, *refs):
    parts = refs[:shares]
    left_ref, beta_ref, raw_ref, alpha_ref, payload_ref, acc_ref = refs[shares:]
    per_share = raw_ref.shape[0]
    alpha = norm_of(tree_sum([p[per_share] for p in parts]))
    alpha_ref[...] = alpha
    alpha_inv = 1.0 / alpha
    left_scale = alpha / beta_ref[...]
    blocks = []
    for q in range(per_share):
        total = tree_sum([p[q] for p in parts])
        blocks.append(total * alpha_inv - left_ref[q] * left_scale)
        raw_ref[q] = blocks[-1]
    acc = tree_sum([b * b for b in blocks])
    acc_ref[...] = acc
    write_payload(payload_ref, blocks, acc)


def final_kernel(rows, iters, pos_ref, *refs):
    refs = list(refs)
    last = [refs.pop(0) for _ in range(rows)]
    betas = [refs.pop(0) for _ in range(iters)]
    alphas = [refs.pop(0) for _ in range(iters)]
    raws = [refs.pop(0) for _ in range(iters)]
    out_ref, ratio_ref, held, sems = refs
    share = held.shape[1]
    start = pos_ref[0] * share
    copies = []
    for i in range(iters):
        copies.append(pltpu.make_async_copy(raws[i].at[pl.ds(start, share)], held.at[i], sems.at[i]))
        copies[-1].start()
    beta = [b[...] for b in betas] + [norm_of(tree_sum([p[...] for p in last]))]
    alpha = [a[...] for a in alphas]
    phibar, rhobar = beta[0], alpha[0]
    direction = [1.0 / alpha[0]] + [jnp.zeros_like(phibar)] * (iters - 1)
    weights = [jnp.zeros_like(phibar)] * iters
    for i in range(iters):
        rho = jnp.sqrt(rhobar * rhobar + beta[i + 1] * beta[i + 1])
        cosine, sine = rhobar / rho, beta[i + 1] / rho
        phi = cosine * phibar
        phibar = sine * phibar
        weights = [w + (phi / rho) * d for w, d in zip(weights, direction)]
        if i + 1 < iters:
            theta = sine * alpha[i + 1]
            rhobar = -cosine * alpha[i + 1]
            direction = [-(theta / rho) * d for d in direction]
            direction[i + 1] = direction[i + 1] + 1.0 / alpha[i + 1]
    ratio_ref[...] = phibar / beta[0]
    for copy in copies:
        copy.wait()
    unroll = 4

    @pl.loop(0, share // unroll)
    def _(step):
        for u in range(unroll):
            c = step * unroll + u
            block = held[0, c] * weights[0]
            for i in range(1, iters):
                block = block + held[i, c] * weights[i]
            at = pl.multiple_of(c * 2 * LANES, 2 * LANES)
            out_ref[:, pl.ds(at, LANES)] = block[:4]
            out_ref[:, pl.ds(at + LANES, LANES)] = block[4:]


def exchange(value, axis):
    size = lax.axis_size(axis)
    got = [value]
    for d in range(1, size):
        got.append(lax.ppermute(value, axis, [(i, i ^ d) for i in range(size)]))
    return got


def exchange_parts(values, axis):
    size = lax.axis_size(axis)
    got = [values[0]]
    for d in range(1, size):
        got.append(lax.ppermute(values[d], axis, [(i, i ^ d) for i in range(size)]))
    return got


def f32(*shape):
    return jax.ShapeDtypeStruct(shape, jnp.float32)


def local(observed, tile_values, tile_cols):
    row_tiles, per_block, tile_size = tile_values.shape[:3]
    rows, shares = lax.axis_size("row"), lax.axis_size("col")
    col_tiles = N // (tile_size * shares)
    per_share = row_tiles // shares
    terms = row_tiles * per_block
    payload = jax.ShapeDtypeStruct((max(16, 4 * per_share), 3 * LANES), jnp.bfloat16)
    pos = jnp.stack([lax.axis_index("row"), lax.axis_index("col")]).astype(jnp.int32)
    cols = jnp.concatenate(exchange(tile_cols.reshape(-1), "row"))
    held = pltpu.VMEM((shares, per_share, per_block, tile_size, tile_size), jnp.bfloat16)

    def adjoint(payloads):
        return pl.pallas_call(
            functools.partial(adjoint_kernel, shares),
            out_shape=f32(terms + 1, 8, LANES),
            in_specs=[SMEM, ANY] + [VMEM] * shares,
            out_specs=VMEM,
            scratch_shapes=[held, pltpu.SemaphoreType.DMA((shares,))],
            compiler_params=PARAMS,
            name="adjoint",
        )(pos, tile_values, *payloads)

    def voxel(term_list, previous):
        first = previous is None
        extra = [] if first else list(previous)
        outs = pl.pallas_call(
            functools.partial(voxel_kernel, shares, rows, first),
            out_shape=[f32(per_share + 1, 8, LANES)] * shares + [f32(8, LANES), f32(col_tiles, 8, LANES)],
            in_specs=[SMEM, SMEM, ANY] + [ANY] * rows + [VMEM] * len(extra),
            out_specs=[VMEM] * (shares + 2),
            scratch_shapes=[
                pltpu.VMEM((rows, terms + 1, 8, LANES), jnp.float32),
                held,
                pltpu.SemaphoreType.DMA((rows,)),
                pltpu.SemaphoreType.DMA((shares,)),
            ],
            compiler_params=PARAMS,
            name="voxel",
        )(pos, cols, tile_values, *term_list, *extra)
        return outs[:shares], outs[shares], outs[shares + 1]

    def ray(parts, left_raw, beta):
        return pl.pallas_call(
            functools.partial(ray_kernel, shares),
            out_shape=[f32(per_share, 8, LANES), f32(8, LANES), payload, f32(8, LANES)],
            in_specs=[VMEM] * (shares + 2),
            out_specs=[VMEM] * 4,
            compiler_params=PARAMS,
            name="ray",
        )(*parts, left_raw, beta)

    left_raw, message = pl.pallas_call(
        prepare_kernel,
        out_shape=[f32(per_share, 8, LANES), payload],
        in_specs=[VMEM],
        out_specs=[VMEM, VMEM],
        compiler_params=PARAMS,
        name="prepare",
    )(observed)
    betas, alphas, raws = [], [], []
    previous = None
    for iteration in range(ITERS + 1):
        summed = exchange(adjoint(exchange(message, "col")), "row")
        parts, beta, right_raw = voxel(summed, previous)
        if iteration == ITERS:
            break
        left_raw, alpha, message, squares = ray(exchange_parts(parts, "col"), left_raw, beta)
        betas.append(beta)
        alphas.append(alpha)
        raws.append(right_raw)
        previous = (right_raw, alpha)
    last = exchange(tree_sum(exchange(squares, "col")), "row")
    share = col_tiles // rows
    result, ratio = pl.pallas_call(
        functools.partial(final_kernel, rows, ITERS),
        out_shape=[f32(4, share * tile_size), f32(8, LANES)],
        in_specs=[SMEM] + [VMEM] * (rows + 2 * ITERS) + [ANY] * ITERS,
        out_specs=[VMEM, VMEM],
        scratch_shapes=[pltpu.VMEM((ITERS, share, 8, LANES), jnp.float32), pltpu.SemaphoreType.DMA((ITERS,))],
        compiler_params=PARAMS,
        name="final",
    )(pos, *last, *betas, *alphas, *raws)
    return result, ratio[:4, 0]


def solution(mesh):
    in_specs = (P(None, ("row", "col")), P("row", "col", None, None), P("row", "col"))
    out_specs = (P(None, ("col", "row")), P())
    return jax.shard_map(local, mesh=mesh, in_specs=in_specs, out_specs=out_specs, check_vma=False)
```

```python
import functools

import jax
import jax.numpy as jnp
from jax import lax
from jax.experimental import pallas as pl
from jax.experimental.pallas import tpu as pltpu
from jax.sharding import PartitionSpec as P

ITERS = 2
N = 1048576
epsilon_sq = 1e-06
LANES = 128
VMEM = pl.BlockSpec(memory_space=pltpu.VMEM)
SMEM = pl.BlockSpec(memory_space=pltpu.SMEM)
ANY = pl.BlockSpec(memory_space=pl.ANY)
PARAMS = pltpu.CompilerParams(vmem_limit_bytes=32 * 1024 * 1024)


def tree_sum(parts):
    while len(parts) > 1:
        parts = [parts[i] + parts[i + 1] for i in range(0, len(parts), 2)]
    return parts[0]


def lane_total(acc):
    rows = jnp.broadcast_to(jnp.sum(acc, axis=1, keepdims=True), acc.shape)
    return rows + pltpu.roll(rows, 4, 0)


def norm_of(acc):
    return jnp.sqrt(lane_total(acc) + epsilon_sq)


def low_half():
    return lax.broadcasted_iota(jnp.int32, (8, LANES), 0) < 4


def wide_to_block(wide, upper):
    first, second = wide[:, :LANES], wide[:, LANES:]
    if upper:
        return jnp.where(low_half(), pltpu.roll(first, 4, 0), second)
    return jnp.where(low_half(), first, pltpu.roll(second, 4, 0))


def write_payload(out_ref, blocks, acc):
    rows = out_ref.shape[0]
    first, second = [], []
    low = low_half()
    for q in range(0, len(blocks), 2):
        first.append(jnp.where(low, blocks[q], pltpu.roll(blocks[q + 1], 4, 0)))
        second.append(jnp.where(low, pltpu.roll(blocks[q], 4, 0), blocks[q + 1]))
    while len(first) * 8 < rows:
        first.append(jnp.zeros((8, LANES), jnp.float32))
        second.append(jnp.zeros((8, LANES), jnp.float32))
    out_ref[:, :LANES] = jnp.concatenate(first, axis=0).astype(jnp.bfloat16)
    out_ref[:, LANES : 2 * LANES] = jnp.concatenate(second, axis=0).astype(jnp.bfloat16)
    upper = acc.astype(jnp.bfloat16).astype(jnp.float32)
    pieces = [upper, acc - upper] + [jnp.zeros((8, LANES), jnp.float32)] * (rows // 8 - 2)
    out_ref[:, 2 * LANES :] = jnp.concatenate(pieces, axis=0).astype(jnp.bfloat16)


def read_squares(ref):
    both = ref[:, 2 * LANES :].astype(jnp.float32)
    return both[:8] + both[8:16]


def prepare_kernel(obs_ref, blocks_ref, payload_ref):
    obs = obs_ref[...]
    blocks = []
    for q in range(obs.shape[1] // (2 * LANES)):
        at = q * 2 * LANES
        blocks.append(jnp.concatenate([obs[:, at : at + LANES], obs[:, at + LANES : at + 2 * LANES]], axis=0))
    for q, block in enumerate(blocks):
        blocks_ref[q] = block
    squares = tree_sum([b * b for b in blocks])
    for c in range(payload_ref.shape[0]):
        write_payload(payload_ref.at[c], blocks, squares)


def adjoint_kernel(cols_ref, tiles_ref, payload_ref, out_ref):
    row_tiles, per_block = tiles_ref.shape[:2]
    shares, copies = payload_ref.shape[0], out_ref.shape[0]
    per_share = row_tiles // shares
    total = row_tiles * per_block
    squares = tree_sum([read_squares(payload_ref.at[c]) for c in range(shares)])
    cols = cols_ref[...]
    for r in range(copies):
        out_ref[r, total] = squares
        out_ref[r, total + 1] = cols
    for c in range(shares):
        rays = payload_ref[c, :, : 2 * LANES]
        for q in range(per_share):
            for k in range(per_block):
                wide = jnp.dot(rays, tiles_ref[c * per_share + q, k], preferred_element_type=jnp.float32)
                at = 8 * (q // 2)
                block = wide_to_block(wide[at : at + 8], q % 2 == 1)
                for r in range(copies):
                    out_ref[r, (c * per_share + q) * per_block + k] = block


def voxel_kernel(first, own_cols_ref, tiles_ref, term_ref, *refs):
    if not first:
        right_ref, alpha_ref = refs[:2]
        refs = refs[2:]
    out_ref, beta_ref, raw_ref, cols_ref, sem = refs
    row_tiles, per_block = tiles_ref.shape[:2]
    shares, rows = out_ref.shape[0], term_ref.shape[0]
    per_share = row_tiles // shares
    per_row = row_tiles * per_block
    copy = pltpu.make_async_copy(term_ref.at[:, per_row + 1], cols_ref, sem)
    copy.start()
    col_tiles = raw_ref.shape[0]
    chunk = 16
    zeros = jnp.zeros((chunk, 8, LANES), jnp.float32)

    @pl.loop(0, col_tiles // chunk)
    def _(step):
        raw_ref[pl.ds(step * chunk, chunk)] = zeros

    beta = norm_of(tree_sum([term_ref[s, per_row] for s in range(rows)]))
    beta_ref[...] = beta
    unroll = 8
    copy.wait()
    for s in range(rows):

        @pl.loop(0, per_row // unroll)
        def _(step):
            for u in range(unroll):
                t = step * unroll + u
                col = cols_ref[s, 0, t].astype(jnp.int32)
                raw_ref[col] = raw_ref[col] + term_ref[s, t]

    beta_inv = 1.0 / beta
    if not first:
        right_scale = beta / alpha_ref[...]

    def scale(step, acc):
        at = pl.ds(step * chunk, chunk)
        raw = raw_ref[at] * beta_inv
        if not first:
            raw = raw - right_ref[at] * right_scale
        raw_ref[at] = raw
        return acc + jnp.sum(raw * raw, axis=0)

    acc = lax.fori_loop(0, col_tiles // chunk, scale, jnp.zeros((8, LANES), jnp.float32))
    for c in range(shares):
        for q in range(per_share):
            i = c * per_share + q
            wide = None
            for k in range(per_block):
                block = raw_ref[own_cols_ref[i * per_block + k]]
                lhs = jnp.concatenate([block, pltpu.roll(block, 4, 0)], axis=1).astype(jnp.bfloat16)
                part = lax.dot_general(
                    lhs, tiles_ref[i, k], (((1,), (1,)), ((), ())), preferred_element_type=jnp.float32
                )
                wide = part if wide is None else wide + part
            out_ref[c, q] = wide_to_block(wide, False)
        out_ref[c, per_share] = acc


def ray_kernel(part_ref, left_ref, beta_ref, raw_ref, alpha_ref, payload_ref, acc_ref):
    shares, per_share = part_ref.shape[0], raw_ref.shape[0]
    alpha = norm_of(tree_sum([part_ref[c, per_share] for c in range(shares)]))
    alpha_ref[...] = alpha
    alpha_inv = 1.0 / alpha
    left_scale = alpha / beta_ref[...]
    blocks = []
    for q in range(per_share):
        total = tree_sum([part_ref[c, q] for c in range(shares)])
        blocks.append(total * alpha_inv - left_ref[q] * left_scale)
        raw_ref[q] = blocks[-1]
    acc = tree_sum([b * b for b in blocks])
    for c in range(shares):
        acc_ref[c] = acc
        write_payload(payload_ref.at[c], blocks, acc)


def final_kernel(iters, pos_ref, last_ref, *refs):
    refs = list(refs)
    betas = [refs.pop(0) for _ in range(iters)]
    alphas = [refs.pop(0) for _ in range(iters)]
    raws = [refs.pop(0) for _ in range(iters)]
    out_ref, ratio_ref, held, sems = refs
    share = held.shape[1]
    start = pos_ref[0] * share
    copies = []
    for i in range(iters):
        copies.append(pltpu.make_async_copy(raws[i].at[pl.ds(start, share)], held.at[i], sems.at[i]))
        copies[-1].start()
    beta = [b[...] for b in betas] + [norm_of(tree_sum([last_ref[r] for r in range(last_ref.shape[0])]))]
    alpha = [a[...] for a in alphas]
    phibar, rhobar = beta[0], alpha[0]
    direction = [1.0 / alpha[0]] + [jnp.zeros_like(phibar)] * (iters - 1)
    weights = [jnp.zeros_like(phibar)] * iters
    for i in range(iters):
        rho = jnp.sqrt(rhobar * rhobar + beta[i + 1] * beta[i + 1])
        cosine, sine = rhobar / rho, beta[i + 1] / rho
        phi = cosine * phibar
        phibar = sine * phibar
        weights = [w + (phi / rho) * d for w, d in zip(weights, direction)]
        if i + 1 < iters:
            theta = sine * alpha[i + 1]
            rhobar = -cosine * alpha[i + 1]
            direction = [-(theta / rho) * d for d in direction]
            direction[i + 1] = direction[i + 1] + 1.0 / alpha[i + 1]
    ratio_ref[...] = phibar / beta[0]
    for copy in copies:
        copy.wait()
    unroll = 4

    @pl.loop(0, share // unroll)
    def _(step):
        for u in range(unroll):
            c = step * unroll + u
            block = held[0, c] * weights[0]
            for i in range(1, iters):
                block = block + held[i, c] * weights[i]
            at = pl.multiple_of(c * 2 * LANES, 2 * LANES)
            out_ref[:, pl.ds(at, LANES)] = block[:4]
            out_ref[:, pl.ds(at + LANES, LANES)] = block[4:]


def f32(*shape):
    return jax.ShapeDtypeStruct(shape, jnp.float32)


def swap(values, axis):
    return lax.all_to_all(values, axis, 0, 0)


def local(observed, tile_values, tile_cols):
    row_tiles, per_block, tile_size = tile_values.shape[:3]
    rows, shares = lax.axis_size("row"), lax.axis_size("col")
    col_tiles = N // (tile_size * shares)
    per_share = row_tiles // shares
    terms = row_tiles * per_block
    payload = jax.ShapeDtypeStruct((shares, max(16, 4 * per_share), 3 * LANES), jnp.bfloat16)
    pos = lax.axis_index("row").astype(jnp.int32).reshape(1)
    own_cols = tile_cols.reshape(-1)
    float_cols = jnp.zeros((8, LANES), jnp.float32).at[0, :terms].set(own_cols.astype(jnp.float32))

    def adjoint(payloads):
        return pl.pallas_call(
            adjoint_kernel,
            out_shape=f32(rows, terms + 2, 8, LANES),
            in_specs=[VMEM] * 3,
            out_specs=VMEM,
            compiler_params=PARAMS,
            name="adjoint",
        )(float_cols, tile_values, payloads)

    def voxel(term_array, previous):
        first = previous is None
        extra = [] if first else list(previous)
        return pl.pallas_call(
            functools.partial(voxel_kernel, first),
            out_shape=[f32(shares, per_share + 1, 8, LANES), f32(8, LANES), f32(col_tiles, 8, LANES)],
            in_specs=[SMEM] + [VMEM] * (2 + len(extra)),
            out_specs=[VMEM] * 3,
            scratch_shapes=[pltpu.SMEM((rows, 8, LANES), jnp.float32), pltpu.SemaphoreType.DMA],
            compiler_params=PARAMS,
            name="voxel",
        )(own_cols, tile_values, term_array, *extra)

    def ray(parts, left_raw, beta):
        return pl.pallas_call(
            ray_kernel,
            out_shape=[f32(per_share, 8, LANES), f32(8, LANES), payload, f32(shares, 8, LANES)],
            in_specs=[VMEM] * 3,
            out_specs=[VMEM] * 4,
            compiler_params=PARAMS,
            name="ray",
        )(parts, left_raw, beta)

    left_raw, message = pl.pallas_call(
        prepare_kernel,
        out_shape=[f32(per_share, 8, LANES), payload],
        in_specs=[VMEM],
        out_specs=[VMEM, VMEM],
        compiler_params=PARAMS,
        name="prepare",
    )(observed)
    betas, alphas, raws = [], [], []
    previous = None
    for iteration in range(ITERS + 1):
        parts, beta, right_raw = voxel(swap(adjoint(swap(message, "col")), "row"), previous)
        if iteration == ITERS:
            break
        left_raw, alpha, message, squares = ray(swap(parts, "col"), left_raw, beta)
        betas.append(beta)
        alphas.append(alpha)
        raws.append(right_raw)
        previous = (right_raw, alpha)
    shared = swap(squares, "col")
    shared = tree_sum([shared[c] for c in range(shares)])
    last = swap(jnp.broadcast_to(shared[None], (rows, 8, LANES)), "row")
    share = col_tiles // rows
    result, ratio = pl.pallas_call(
        functools.partial(final_kernel, ITERS),
        out_shape=[f32(4, share * tile_size), f32(8, LANES)],
        in_specs=[SMEM] + [VMEM] * (1 + 2 * ITERS) + [ANY] * ITERS,
        out_specs=[VMEM, VMEM],
        scratch_shapes=[pltpu.VMEM((ITERS, share, 8, LANES), jnp.float32), pltpu.SemaphoreType.DMA((ITERS,))],
        compiler_params=PARAMS,
        name="final",
    )(pos, last, *betas, *alphas, *raws)
    return result, ratio[:4, 0]


def solution(mesh):
    in_specs = (P(None, ("row", "col")), P("row", "col", None, None), P("row", "col"))
    out_specs = (P(None, ("col", "row")), P())
    return jax.shard_map(local, mesh=mesh, in_specs=in_specs, out_specs=out_specs, check_vma=False)
```

```python
import functools

import jax
import jax.numpy as jnp
from jax import lax
from jax.experimental import pallas as pl
from jax.experimental.pallas import tpu as pltpu
from jax.sharding import PartitionSpec as P

ITERS = 2
N = 1048576
epsilon_sq = 1e-06
LANES = 128
VMEM = pl.BlockSpec(memory_space=pltpu.VMEM)
SMEM = pl.BlockSpec(memory_space=pltpu.SMEM)
HBM = pl.BlockSpec(memory_space=pltpu.HBM)
PARAMS = pltpu.CompilerParams(vmem_limit_bytes=32 * 1024 * 1024)


def tree_sum(parts):
    while len(parts) > 1:
        parts = [parts[i] + parts[i + 1] for i in range(0, len(parts), 2)]
    return parts[0]


def lane_total(acc):
    rows = jnp.broadcast_to(jnp.sum(acc, axis=1, keepdims=True), acc.shape)
    return rows + pltpu.roll(rows, 4, 0)


def norm_of(acc):
    return jnp.sqrt(lane_total(acc) + epsilon_sq)


def low_half():
    return lax.broadcasted_iota(jnp.int32, (8, LANES), 0) < 4


def wide_to_block(wide, upper):
    first, second = wide[:, :LANES], wide[:, LANES:]
    if upper:
        return jnp.where(low_half(), pltpu.roll(first, 4, 0), second)
    return jnp.where(low_half(), first, pltpu.roll(second, 4, 0))


def write_payload(out_ref, blocks, acc):
    rows = out_ref.shape[0]
    first, second = [], []
    low = low_half()
    for q in range(0, len(blocks), 2):
        first.append(jnp.where(low, blocks[q], pltpu.roll(blocks[q + 1], 4, 0)))
        second.append(jnp.where(low, pltpu.roll(blocks[q], 4, 0), blocks[q + 1]))
    while len(first) * 8 < rows:
        first.append(jnp.zeros((8, LANES), jnp.float32))
        second.append(jnp.zeros((8, LANES), jnp.float32))
    out_ref[:, :LANES] = jnp.concatenate(first, axis=0).astype(jnp.bfloat16)
    out_ref[:, LANES : 2 * LANES] = jnp.concatenate(second, axis=0).astype(jnp.bfloat16)
    upper = acc.astype(jnp.bfloat16).astype(jnp.float32)
    pieces = [upper, acc - upper] + [jnp.zeros((8, LANES), jnp.float32)] * (rows // 8 - 2)
    out_ref[:, 2 * LANES :] = jnp.concatenate(pieces, axis=0).astype(jnp.bfloat16)


def read_squares(ref):
    both = ref[:, 2 * LANES :].astype(jnp.float32)
    return both[:8] + both[8:16]


def prepare_kernel(obs_ref, blocks_ref, payload_ref):
    obs = obs_ref[...]
    blocks = []
    for q in range(obs.shape[1] // (2 * LANES)):
        at = q * 2 * LANES
        blocks.append(jnp.concatenate([obs[:, at : at + LANES], obs[:, at + LANES : at + 2 * LANES]], axis=0))
    for q, block in enumerate(blocks):
        blocks_ref[q] = block
    squares = tree_sum([b * b for b in blocks])
    for c in range(payload_ref.shape[0]):
        write_payload(payload_ref.at[c], blocks, squares)


def split_store(value, upper_ref, lower_ref, i):
    upper = value.astype(jnp.bfloat16)
    upper_ref[i] = upper
    lower_ref[i] = (value - upper.astype(jnp.float32)).astype(jnp.bfloat16)


def adjoint_kernel(load, cols_ref, tiles_ref, payload_ref, upper_ref, lower_ref, *refs):
    row_tiles, per_block = tiles_ref.shape[:2]
    shares = payload_ref.shape[0]
    per_share = row_tiles // shares
    copies = []
    held_ref = tiles_ref
    if load:
        held_ref, sems = refs
        for c in range(shares):
            part = pl.ds(c * per_share, per_share)
            copies.append(pltpu.make_async_copy(tiles_ref.at[part], held_ref.at[part], sems.at[c]))
            copies[-1].start()
    squares = tree_sum([read_squares(payload_ref.at[c]) for c in range(shares)])
    rounded = squares.astype(jnp.bfloat16).astype(jnp.float32)
    upper_ref[row_tiles] = jnp.concatenate([rounded, squares - rounded], axis=0).astype(jnp.bfloat16)
    upper_ref[row_tiles + 1] = cols_ref[...].astype(jnp.bfloat16)
    for c in range(shares):
        if load:
            copies[c].wait()
        rays = payload_ref[c, :, : 2 * LANES]
        for q in range(per_share):
            i = c * per_share + q
            at = 8 * (q // 2)
            blocks = []
            for k in range(per_block):
                wide = jnp.dot(rays, held_ref[i, k], preferred_element_type=jnp.float32)
                blocks.append(wide_to_block(wide[at : at + 8], q % 2 == 1))
            split_store(jnp.concatenate(blocks, axis=0), upper_ref, lower_ref, i)


def voxel_kernel(first, rows, pos_ref, own_cols_ref, tiles_ref, *refs):
    terms, refs = refs[:rows], refs[rows:]
    if not first:
        right_ref, alpha_ref = refs[:2]
        refs = refs[2:]
    out_ref, beta_ref, raw_ref, share_ref, cols_ref, term_buf, cols_buf, cols_scalar, sem = refs
    row_tiles, per_block = tiles_ref.shape[:2]
    shares = out_ref.shape[0]
    per_share = row_tiles // shares
    for d in range(rows):
        slot = jnp.bitwise_xor(pos_ref[0], d)
        pieces = terms[d][row_tiles + 1].astype(jnp.float32)
        cols_buf[slot] = (pieces[:8] * 16.0 + pieces[8:]).astype(jnp.int32)
    copy = pltpu.make_async_copy(cols_buf, cols_scalar, sem)
    copy.start()
    cols_ref[...] = cols_buf[...]
    for d in range(rows):
        slot = jnp.bitwise_xor(pos_ref[0], d)
        term_buf[slot] = terms[d][:row_tiles]
    col_tiles = raw_ref.shape[0]
    chunk = 16
    zeros = jnp.zeros((chunk, 8, LANES), jnp.float32)

    @pl.loop(0, col_tiles // chunk)
    def _(step):
        raw_ref[pl.ds(step * chunk, chunk)] = zeros

    squares = []
    for d in range(rows):
        pieces = terms[d][row_tiles].astype(jnp.float32)
        squares.append(pieces[:8] + pieces[8:])
    beta = norm_of(tree_sum(squares))
    beta_ref[...] = beta
    unroll = 4
    copy.wait()
    for s in range(rows):

        @pl.loop(0, row_tiles // unroll)
        def _(step):
            for u in range(unroll):
                i = step * unroll + u
                pair = term_buf[s, i].astype(jnp.float32)
                for k in range(per_block):
                    col = cols_scalar[s, 0, i * per_block + k]
                    raw_ref[col] = raw_ref[col] + pair[8 * k : 8 * k + 8]

    beta_inv = 1.0 / beta
    if not first:
        right_scale = beta / alpha_ref[...]

    def scale(step, acc):
        at = pl.ds(step * chunk, chunk)
        raw = raw_ref[at] * beta_inv
        if not first:
            raw = raw - right_ref[at] * right_scale
        raw_ref[at] = raw
        return acc + jnp.sum(raw * raw, axis=0)

    acc = lax.fori_loop(0, col_tiles // chunk, scale, jnp.zeros((8, LANES), jnp.float32))
    for c in range(shares):
        for q in range(per_share):
            i = c * per_share + q
            wide = None
            for k in range(per_block):
                block = raw_ref[own_cols_ref[i * per_block + k]]
                lhs = jnp.concatenate([block, pltpu.roll(block, 4, 0)], axis=1).astype(jnp.bfloat16)
                part = lax.dot_general(
                    lhs, tiles_ref[i, k], (((1,), (1,)), ((), ())), preferred_element_type=jnp.float32
                )
                wide = part if wide is None else wide + part
            out_ref[c, q] = wide_to_block(wide, False)
        out_ref[c, per_share] = acc
    share = share_ref.shape[0]
    share_ref[...] = raw_ref[pl.ds(pos_ref[0] * share, share)]


def lower_kernel(pos_ref, cols_ref, *refs):
    terms, out_ref = refs[:-1], refs[-1]
    row_tiles = terms[0].shape[0]
    per_block = terms[0].shape[1] // 8
    share = out_ref.shape[0] - 1
    start = pos_ref[0] * share
    out_ref[...] = jnp.zeros(out_ref.shape, jnp.float32)
    unroll = 4
    for d, term in enumerate(terms):
        source = jnp.bitwise_xor(pos_ref[0], d)

        @pl.loop(0, row_tiles // unroll)
        def _(step):
            for u in range(unroll):
                i = step * unroll + u
                pair = term[i].astype(jnp.float32)
                for k in range(per_block):
                    col = cols_ref[source, 0, i * per_block + k] - start
                    col = jnp.where((col >= 0) & (col < share), col, share)
                    out_ref[col] = out_ref[col] + pair[8 * k : 8 * k + 8]


def ray_kernel(part_ref, left_ref, beta_ref, raw_ref, alpha_ref, payload_ref, acc_ref):
    shares, per_share = part_ref.shape[0], raw_ref.shape[0]
    alpha = norm_of(tree_sum([part_ref[c, per_share] for c in range(shares)]))
    alpha_ref[...] = alpha
    alpha_inv = 1.0 / alpha
    left_scale = alpha / beta_ref[...]
    blocks = []
    for q in range(per_share):
        total = tree_sum([part_ref[c, q] for c in range(shares)])
        blocks.append(total * alpha_inv - left_ref[q] * left_scale)
        raw_ref[q] = blocks[-1]
    acc = tree_sum([b * b for b in blocks])
    for c in range(acc_ref.shape[0]):
        acc_ref[c] = acc
    for c in range(shares):
        write_payload(payload_ref.at[c], blocks, acc)


def final_kernel(iters, last_ref, *refs):
    refs = list(refs)
    betas = [refs.pop(0) for _ in range(iters)]
    alphas = [refs.pop(0) for _ in range(iters)]
    raws = [refs.pop(0) for _ in range(iters)]
    lowers = [refs.pop(0) for _ in range(iters)]
    out_ref, ratio_ref = refs
    beta = [b[...] for b in betas] + [norm_of(tree_sum([last_ref[r] for r in range(last_ref.shape[0])]))]
    alpha = [a[...] for a in alphas]
    phibar, rhobar = beta[0], alpha[0]
    direction = [1.0 / alpha[0]] + [jnp.zeros_like(phibar)] * (iters - 1)
    weights = [jnp.zeros_like(phibar)] * iters
    for i in range(iters):
        rho = jnp.sqrt(rhobar * rhobar + beta[i + 1] * beta[i + 1])
        cosine, sine = rhobar / rho, beta[i + 1] / rho
        phi = cosine * phibar
        phibar = sine * phibar
        weights = [w + (phi / rho) * d for w, d in zip(weights, direction)]
        if i + 1 < iters:
            theta = sine * alpha[i + 1]
            rhobar = -cosine * alpha[i + 1]
            direction = [-(theta / rho) * d for d in direction]
            direction[i + 1] = direction[i + 1] + 1.0 / alpha[i + 1]
    ratio = phibar / beta[0]
    for n in range(4):
        ratio_ref[n] = jnp.max(ratio[n : n + 1])
    lower_weights = []
    carried = jnp.zeros_like(phibar)
    for i in reversed(range(iters)):
        carried = weights[i] - carried
        lower_weights.insert(0, carried / beta[i])
        if i > 0:
            carried = carried * (beta[i] / alpha[i - 1])
    unroll = 4

    @pl.loop(0, raws[0].shape[0] // unroll)
    def _(step):
        for u in range(unroll):
            c = step * unroll + u
            parts = [r[c] * w for r, w in zip(raws, weights)]
            parts += [r[c] * w for r, w in zip(lowers, lower_weights)]
            block = tree_sum(parts) if len(parts) % 2 == 0 else sum(parts)
            at = pl.multiple_of(c * 2 * LANES, 2 * LANES)
            out_ref[:, pl.ds(at, LANES)] = block[:4]
            out_ref[:, pl.ds(at + LANES, LANES)] = block[4:]


def f32(*shape):
    return jax.ShapeDtypeStruct(shape, jnp.float32)


def exchange(value, axis):
    size = lax.axis_size(axis)
    got = [value]
    for d in range(1, size):
        got.append(lax.ppermute(value, axis, [(i, i ^ d) for i in range(size)]))
    return got


def swap(values, axis):
    return lax.all_to_all(values, axis, 0, 0)


def local(observed, tile_values, tile_cols):
    row_tiles, per_block, tile_size = tile_values.shape[:3]
    rows, shares = lax.axis_size("row"), lax.axis_size("col")
    col_tiles = N // (tile_size * shares)
    per_share = row_tiles // shares
    terms = row_tiles * per_block
    payload = jax.ShapeDtypeStruct((shares, max(16, 4 * per_share), 3 * LANES), jnp.bfloat16)
    pos = lax.axis_index("row").astype(jnp.int32).reshape(1)
    share = col_tiles // rows
    own_cols = tile_cols.reshape(-1)
    float_cols = jnp.zeros((16, LANES), jnp.float32)
    float_cols = float_cols.at[0, :terms].set((own_cols // 16).astype(jnp.float32))
    float_cols = float_cols.at[8, :terms].set((own_cols % 16).astype(jnp.float32))
    upper_shape = jax.ShapeDtypeStruct((row_tiles + 2, 16, LANES), jnp.bfloat16)
    lower_shape = jax.ShapeDtypeStruct((row_tiles, 16, LANES), jnp.bfloat16)

    def adjoint(tiles, payloads, load):
        held = jax.ShapeDtypeStruct(tile_values.shape, tile_values.dtype)
        return pl.pallas_call(
            functools.partial(adjoint_kernel, load),
            out_shape=[upper_shape, lower_shape] + [held] * load,
            in_specs=[VMEM, HBM if load else VMEM, VMEM],
            out_specs=[VMEM] * (2 + load),
            scratch_shapes=[pltpu.SemaphoreType.DMA((shares,))] * load,
            compiler_params=PARAMS,
            name="adjoint",
        )(float_cols, tiles, payloads)

    def voxel(tiles, term_list, previous):
        first = previous is None
        extra = [] if first else list(previous)
        return pl.pallas_call(
            functools.partial(voxel_kernel, first, rows),
            out_shape=[
                f32(shares, per_share + 1, 8, LANES),
                f32(8, LANES),
                f32(col_tiles, 8, LANES),
                f32(share, 8, LANES),
                jax.ShapeDtypeStruct((rows, 8, LANES), jnp.int32),
            ],
            in_specs=[SMEM, SMEM] + [VMEM] * (1 + rows + len(extra)),
            out_specs=[VMEM] * 5,
            scratch_shapes=[
                pltpu.VMEM((rows, row_tiles, 16, LANES), jnp.bfloat16),
                pltpu.VMEM((rows, 8, LANES), jnp.int32),
                pltpu.SMEM((rows, 8, LANES), jnp.int32),
                pltpu.SemaphoreType.DMA,
            ],
            compiler_params=PARAMS,
            name="voxel",
        )(pos, own_cols, tiles, *term_list, *extra)

    def lower(cols, term_list):
        return pl.pallas_call(
            lower_kernel,
            out_shape=f32(share + 1, 8, LANES),
            in_specs=[SMEM, SMEM] + [VMEM] * rows,
            out_specs=VMEM,
            compiler_params=PARAMS,
            name="lower",
        )(pos, cols, *term_list)

    def ray(parts, left_raw, beta):
        return pl.pallas_call(
            ray_kernel,
            out_shape=[f32(per_share, 8, LANES), f32(8, LANES), payload, f32(rows * shares, 8, LANES)],
            in_specs=[VMEM] * 3,
            out_specs=[VMEM] * 4,
            compiler_params=PARAMS,
            name="ray",
        )(parts, left_raw, beta)

    left_raw, message = pl.pallas_call(
        prepare_kernel,
        out_shape=[f32(per_share, 8, LANES), payload],
        in_specs=[VMEM],
        out_specs=[VMEM, VMEM],
        compiler_params=PARAMS,
        name="prepare",
    )(observed)
    upper_terms, lower_terms, tiles = adjoint(pltpu.with_memory_space_constraint(tile_values, pltpu.HBM), swap(message, "col"), True)
    betas, alphas, raws, lowers = [], [], [], []
    previous = None
    for iteration in range(ITERS + 1):
        if iteration > 0:
            upper_terms, lower_terms = adjoint(tiles, swap(message, "col"), False)
        parts, beta, right_raw, right_share, cols = voxel(tiles, exchange(upper_terms, "row"), previous)
        if iteration == ITERS:
            break
        lowers.append(lower(cols, exchange(lower_terms, "row")))
        left_raw, alpha, message, squares = ray(swap(parts, "col"), left_raw, beta)
        betas.append(beta)
        alphas.append(alpha)
        raws.append(right_share)
        previous = (right_raw, alpha)
    result, ratio = pl.pallas_call(
        functools.partial(final_kernel, ITERS),
        out_shape=[f32(4, share * tile_size), f32(4)],
        in_specs=[VMEM] * (1 + 4 * ITERS),
        out_specs=[VMEM, SMEM],
        compiler_params=PARAMS,
        name="final",
    )(swap(squares, ("row", "col")), *betas, *alphas, *raws, *lowers)
    return result, ratio


def solution(mesh):
    in_specs = (P(None, ("row", "col")), P("row", "col", None, None), P("row", "col"))
    out_specs = (P(None, ("col", "row")), P())
    return jax.shard_map(local, mesh=mesh, in_specs=in_specs, out_specs=out_specs, check_vma=False)
```

```python
import functools

import jax
import jax.numpy as jnp
from jax import lax
from jax.experimental import pallas as pl
from jax.experimental.pallas import tpu as pltpu
from jax.sharding import PartitionSpec as P

ITERS = 2
N = 1048576
epsilon_sq = 1e-06
LANES = 128
RHS = 4
VMEM = pl.BlockSpec(memory_space=pltpu.VMEM)
SMEM = pl.BlockSpec(memory_space=pltpu.SMEM)
HBM = pl.BlockSpec(memory_space=pltpu.HBM)
ANY = pl.BlockSpec(memory_space=pl.ANY)
PARAMS = pltpu.CompilerParams(vmem_limit_bytes=32 * 1024 * 1024)


def tree_sum(parts):
    while len(parts) > 1:
        paired = [parts[i] + parts[i + 1] for i in range(0, len(parts) - 1, 2)]
        parts = paired + parts[2 * len(paired) :]
    return parts[0]


def norm_of(acc):
    rows = jnp.broadcast_to(jnp.sum(acc, axis=1, keepdims=True), acc.shape)
    return jnp.sqrt(rows + pltpu.roll(rows, 4, 0) + epsilon_sq)


def low_half(width):
    return lax.broadcasted_iota(jnp.int32, (8, width), 0) < 4


def in_two(acc):
    upper = acc.astype(jnp.bfloat16).astype(jnp.float32)
    return upper, acc - upper


def write_payload(out_ref, blocks, acc):
    rows = out_ref.shape[0]
    blank = [jnp.zeros((8, LANES), jnp.float32)] * (rows // 8)
    for h in range(2):
        half = (blocks[h::2] + blank)[: rows // 8]
        out_ref[:, h * LANES : (h + 1) * LANES] = jnp.concatenate(half, axis=0).astype(jnp.bfloat16)
    pieces = (list(in_two(acc)) + blank)[: rows // 8]
    out_ref[:, 2 * LANES :] = jnp.concatenate(pieces, axis=0).astype(jnp.bfloat16)


def read_squares(ref):
    both = ref[:, 2 * LANES :].astype(jnp.float32)
    return both[:8] + both[8:16]


def prepare_kernel(obs_ref, blocks_ref, payload_ref):
    obs = obs_ref[...]
    blocks = []
    for b in range(blocks_ref.shape[0]):
        at = (b // 2) * 4 * LANES + (b % 2) * LANES
        blocks.append(jnp.concatenate([obs[:, at : at + LANES], obs[:, at + 2 * LANES : at + 3 * LANES]], axis=0))
    for b, block in enumerate(blocks):
        blocks_ref[b] = block
    squares = tree_sum([b * b for b in blocks])
    for c in range(payload_ref.shape[0]):
        write_payload(payload_ref.at[c], blocks, squares)


def match_kernel(pos_ref, *refs):
    keys_list, (equal_ref, weight_ref, pick_ref, held) = refs[:-4], refs[-4:]
    rows = len(keys_list)
    per_row = keys_list[0].shape[1]
    for d, keys in enumerate(keys_list):
        held[jnp.bitwise_xor(pos_ref[0], d)] = jnp.broadcast_to(keys[...], (8, per_row))

    @pl.loop(0, rows)
    def _(s):
        down = jnp.broadcast_to(held[s][:1], (LANES, per_row)).T
        at = pl.ds(pl.multiple_of(s * per_row, per_row), per_row)
        count = jnp.zeros((per_row, LANES), jnp.float32)
        for other in range(rows):
            for h in range(per_row // LANES):
                across = held[other, :1, h * LANES : (h + 1) * LANES]
                same = jnp.where(down == across, 1.0, 0.0)
                count = count + same
                lane = other * per_row + h * LANES
                equal_ref[at, lane : lane + LANES] = same.astype(jnp.bfloat16)
        weight_ref[at, :] = jnp.broadcast_to(1.0 / jnp.sum(count, axis=1, keepdims=True), (per_row, LANES))

    wanted = pick_ref.shape[0]
    step_rows = 128
    start = pos_ref[0] * wanted

    @pl.loop(0, wanted // step_rows)
    def _(step):
        down = lax.broadcasted_iota(jnp.int32, (step_rows, LANES), 0) + (start + step * step_rows)
        down = down.astype(jnp.float32)
        at = pl.ds(pl.multiple_of(step * step_rows, step_rows), step_rows)
        for other in range(rows):
            for h in range(per_row // LANES):
                across = held[other, :1, h * LANES : (h + 1) * LANES]
                lane = other * per_row + h * LANES
                pick_ref[at, lane : lane + LANES] = jnp.where(down == across, 1.0, 0.0).astype(jnp.bfloat16)


def fetch(tiles_ref, held_ref, sems, shares):
    per_share = tiles_ref.shape[0] // shares
    copies = []
    for c in range(shares):
        part = pl.ds(c * per_share, per_share)
        copies.append(pltpu.make_async_copy(tiles_ref.at[part], held_ref.at[part], sems.at[c]))
        copies[-1].start()
    return copies


def adjoint_kernel(load, unread, tiles_ref, payload_ref, *refs):
    refs = refs[unread:]
    row_tiles, per_block = tiles_ref.shape[:2]
    shares = payload_ref.shape[0]
    per_share = row_tiles // shares
    copies = None
    if load:
        upper_ref, lower_ref, tiles_held, sems = refs
        copies = fetch(tiles_ref, tiles_held, sems, shares)
        tiles_ref = tiles_held
    else:
        (upper_ref,) = refs
    squares = tree_sum([read_squares(payload_ref.at[c]) for c in range(shares)])
    pieces = jnp.concatenate(in_two(squares), axis=1)
    terms = row_tiles * per_block * RHS
    upper_ref[terms:] = jnp.concatenate([pieces, jnp.zeros_like(pieces)], axis=0).astype(jnp.bfloat16)
    low = low_half(2 * LANES)
    for c in range(shares):
        if load:
            copies[c].wait()
        rays = payload_ref[c, :, : 2 * LANES]
        for g in range(per_share // 2):
            i = c * per_share + 2 * g
            wide = [
                jnp.dot(rays, tiles_ref[i + e, k], preferred_element_type=jnp.float32)[8 * g : 8 * g + 8]
                for e in range(2)
                for k in range(2)
            ]
            value = jnp.concatenate(
                [
                    jnp.where(low, wide[0], pltpu.roll(wide[1], 4, 0)),
                    jnp.where(low, pltpu.roll(wide[2], 4, 0), wide[3]),
                ],
                axis=0,
            )
            upper = value.astype(jnp.bfloat16)
            upper_ref[8 * i : 8 * i + 16] = upper
            if load:
                lower_ref[8 * i : 8 * i + 16] = (value - upper.astype(jnp.float32)).astype(jnp.bfloat16)


def voxel_kernel(first, rows, pos_ref, tiles_ref, equal_ref, weight_ref, *refs):
    terms, refs = refs[:rows], refs[rows:]
    if not first:
        right_ref, alpha_ref = refs[:2]
        refs = refs[2:]
    out_ref, beta_ref, raw_ref, all_ref = refs[:4]
    row_tiles, per_block = tiles_ref.shape[:2]
    shares = out_ref.shape[0]
    per_share = row_tiles // shares
    copies = None
    if first:
        tiles_held, sems = refs[4:]
        copies = fetch(tiles_ref, tiles_held, sems, shares)
        tiles_ref = tiles_held
    per_row = row_tiles * per_block * RHS
    squares = []
    for d in range(rows):
        slot = jnp.bitwise_xor(pos_ref[0], d)
        all_ref[pl.ds(pl.multiple_of(slot * per_row, per_row), per_row), :] = terms[d][:per_row]
        pieces = terms[d][per_row:].astype(jnp.float32)[:8]
        squares.append(pieces[:, :LANES] + pieces[:, LANES:])
    beta = norm_of(tree_sum(squares))
    beta_ref[...] = beta
    wide_scale = jnp.concatenate([1.0 / beta] * 2, axis=1)
    if not first:
        wide_right = jnp.concatenate([beta / alpha_ref[...]] * 2, axis=1)
    acc = jnp.zeros((8, LANES), jnp.float32)
    for s in range(rows):
        summed = jnp.dot(
            equal_ref[s * per_row : (s + 1) * per_row, :], all_ref[...], preferred_element_type=jnp.float32
        )
        for m in range(per_row // 8):
            at = s * per_row + 8 * m
            raw = summed[8 * m : 8 * m + 8] * wide_scale
            if not first:
                raw = raw - right_ref[at : at + 8] * wide_right
            raw_ref[at : at + 8] = raw
            square = raw * raw
            acc = acc + (square[:, :LANES] + square[:, LANES:]) * weight_ref[at : at + 8]
    low = low_half(2 * LANES)
    own = pos_ref[0] * per_row
    for c in range(shares):
        if first:
            copies[c].wait()
        for g in range(per_share // 2):
            i = c * per_share + 2 * g
            lhs = raw_ref[pl.ds(pl.multiple_of(own + 8 * i, 16), 16), :].astype(jnp.bfloat16)
            wide = [
                lax.dot_general(
                    lhs, tiles_ref[i + e, k], (((1,), (1,)), ((), ())), preferred_element_type=jnp.float32
                )[8 * e : 8 * e + 8]
                for e in range(2)
                for k in range(2)
            ]
            value = jnp.where(low, wide[0], wide[3]) + pltpu.roll(jnp.where(low, wide[2], wide[1]), 4, 0)
            out_ref[c, 2 * g] = value[:, :LANES]
            out_ref[c, 2 * g + 1] = value[:, LANES:]
        out_ref[c, per_share] = acc


def share_kernel(pos_ref, pick_ref, all_ref, *refs):
    lower_terms, out_ref = refs[:-1], refs[-1]
    if lower_terms:
        lower_terms, out_ref, held = lower_terms[:-1], refs[-2], refs[-1]
        per_row = lower_terms[0].shape[0]
        for d, term in enumerate(lower_terms):
            slot = jnp.bitwise_xor(pos_ref[0], d)
            held[pl.ds(pl.multiple_of(slot * per_row, per_row), per_row), :] = term[...]
    step = 128
    for at in range(0, out_ref.shape[0], step):
        pick = pick_ref[at : at + step, :]
        total = jnp.dot(pick, all_ref[...], preferred_element_type=jnp.float32)
        if lower_terms:
            total = total + jnp.dot(pick, held[...], preferred_element_type=jnp.float32)
        out_ref[at : at + step, :] = total


def ray_kernel(part_ref, left_ref, beta_ref, raw_ref, alpha_ref, payload_ref, acc_ref):
    shares, count = part_ref.shape[0], raw_ref.shape[0]
    alpha = norm_of(tree_sum([part_ref[c, count] for c in range(shares)]))
    alpha_ref[...] = alpha
    alpha_inv = 1.0 / alpha
    left_scale = alpha / beta_ref[...]
    blocks = []
    for b in range(count):
        total = tree_sum([part_ref[c, b] for c in range(shares)])
        blocks.append(total * alpha_inv - left_ref[b] * left_scale)
        raw_ref[b] = blocks[-1]
    acc = tree_sum([b * b for b in blocks])
    for c in range(acc_ref.shape[0]):
        acc_ref[c] = acc
    for c in range(shares):
        write_payload(payload_ref.at[c], blocks, acc)


def final_kernel(iters, last_ref, *refs):
    refs = list(refs)
    betas = [refs.pop(0) for _ in range(iters)]
    alphas = [refs.pop(0) for _ in range(iters)]
    products = [refs.pop(0) for _ in range(iters)]
    out_ref, ratio_ref = refs
    beta = [b[...] for b in betas] + [norm_of(tree_sum([last_ref[r] for r in range(last_ref.shape[0])]))]
    alpha = [a[...] for a in alphas]
    phibar, rhobar = beta[0], alpha[0]
    direction = [1.0 / alpha[0]] + [jnp.zeros_like(phibar)] * (iters - 1)
    weights = [jnp.zeros_like(phibar)] * iters
    for i in range(iters):
        rho = jnp.sqrt(rhobar * rhobar + beta[i + 1] * beta[i + 1])
        cosine, sine = rhobar / rho, beta[i + 1] / rho
        phi = cosine * phibar
        phibar = sine * phibar
        weights = [w + (phi / rho) * d for w, d in zip(weights, direction)]
        if i + 1 < iters:
            theta = sine * alpha[i + 1]
            rhobar = -cosine * alpha[i + 1]
            direction = [-(theta / rho) * d for d in direction]
            direction[i + 1] = direction[i + 1] + 1.0 / alpha[i + 1]
    ratio = phibar / beta[0]
    for n in range(RHS):
        ratio_ref[n] = jnp.max(ratio[n : n + 1])
    scales = []
    carried = jnp.zeros_like(phibar)
    for i in reversed(range(iters)):
        carried = weights[i] - carried
        scales.insert(0, jnp.concatenate([carried / beta[i]] * 2, axis=1))
        if i > 0:
            carried = carried * (beta[i] / alpha[i - 1])
    unroll = 4

    @pl.loop(0, products[0].shape[0] // (8 * unroll))
    def _(step):
        for u in range(unroll):
            m = step * unroll + u
            at = pl.ds(pl.multiple_of(m * 8, 8), 8)
            both = tree_sum([p[at, :] * s for p, s in zip(products, scales)])
            lane = pl.multiple_of(m * 4 * LANES, 4 * LANES)
            out_ref[:, pl.ds(lane, 2 * LANES)] = both[:4]
            out_ref[:, pl.ds(lane + 2 * LANES, 2 * LANES)] = both[4:]


def f32(*shape):
    return jax.ShapeDtypeStruct(shape, jnp.float32)


def bf16(*shape):
    return jax.ShapeDtypeStruct(shape, jnp.bfloat16)


def exchange(value, axis):
    size = lax.axis_size(axis)
    got = [value]
    for d in range(1, size):
        got.append(lax.ppermute(value, axis, [(i, i ^ d) for i in range(size)]))
    return got


def swap(values, axis):
    return lax.all_to_all(values, axis, 0, 0)


def local(observed, tile_values, tile_cols):
    row_tiles, per_block, tile_size = tile_values.shape[:3]
    rows, shares = lax.axis_size("row"), lax.axis_size("col")
    col_tiles = N // (tile_size * shares)
    per_share = row_tiles // shares
    per_row = row_tiles * per_block * RHS
    share_rows = col_tiles // rows * RHS
    payload = bf16(shares, max(16, 4 * per_share), 3 * LANES)
    pos = lax.axis_index("row").astype(jnp.int32).reshape(1)
    tiles_far = pltpu.with_memory_space_constraint(tile_values, pltpu.HBM)
    held = pltpu.VMEM(tile_values.shape, tile_values.dtype)
    tile_sems = pltpu.SemaphoreType.DMA((shares,))
    keys = tile_cols.reshape(-1, 1) * RHS + jnp.arange(RHS, dtype=jnp.int32)[None]
    keys = keys.astype(jnp.float32).reshape(1, per_row)
    all_keys = exchange(keys, "row")
    equal, weight, pick = pl.pallas_call(
        match_kernel,
        out_shape=[bf16(rows * per_row, rows * per_row), f32(rows * per_row, LANES), bf16(share_rows, rows * per_row)],
        in_specs=[SMEM] + [VMEM] * rows,
        out_specs=[VMEM] * 3,
        scratch_shapes=[pltpu.VMEM((rows, 8, per_row), jnp.float32)],
        compiler_params=PARAMS,
        name="match",
    )(pos, *all_keys)

    def adjoint(payloads, load, after):
        upper, lower = bf16(per_row + 16, tile_size), bf16(per_row, tile_size)
        return pl.pallas_call(
            functools.partial(adjoint_kernel, load, len(after)),
            out_shape=[upper] + [lower] * load,
            in_specs=[HBM if load else VMEM, VMEM] + [ANY] * len(after),
            out_specs=[VMEM] * (1 + load),
            scratch_shapes=[held, tile_sems] * load,
            compiler_params=PARAMS,
            name="adjoint",
        )(tiles_far if load else tile_values, payloads, *after)

    def voxel(term_list, previous):
        first = previous is None
        extra = [] if first else list(previous)
        return pl.pallas_call(
            functools.partial(voxel_kernel, first, rows),
            out_shape=[
                f32(shares, per_share + 1, 8, LANES),
                f32(8, LANES),
                f32(rows * per_row, tile_size),
                bf16(rows * per_row, tile_size),
            ],
            in_specs=[SMEM, HBM if first else VMEM] + [VMEM] * (2 + rows + len(extra)),
            out_specs=[VMEM] * 4,
            scratch_shapes=[held, tile_sems] * first,
            compiler_params=PARAMS,
            name="voxel",
        )(pos, tiles_far if first else tile_values, equal, weight, *term_list, *extra)

    def share(all_terms, lower_terms):
        return pl.pallas_call(
            share_kernel,
            out_shape=f32(share_rows, tile_size),
            in_specs=[SMEM] + [VMEM] * (2 + len(lower_terms)),
            out_specs=VMEM,
            scratch_shapes=[pltpu.VMEM((rows * per_row, tile_size), jnp.bfloat16)] * (len(lower_terms) > 0),
            compiler_params=PARAMS,
            name="share",
        )(pos, pick, all_terms, *lower_terms)

    def ray(parts, left_raw, beta):
        return pl.pallas_call(
            ray_kernel,
            out_shape=[f32(per_share, 8, LANES), f32(8, LANES), payload, f32(rows * shares, 8, LANES)],
            in_specs=[VMEM] * 3,
            out_specs=[VMEM] * 4,
            compiler_params=PARAMS,
            name="ray",
        )(parts, left_raw, beta)

    left_raw, message = pl.pallas_call(
        prepare_kernel,
        out_shape=[f32(per_share, 8, LANES), payload],
        in_specs=[VMEM],
        out_specs=[VMEM, VMEM],
        compiler_params=PARAMS,
        name="prepare",
    )(observed)
    betas, alphas, products = [], [], []
    previous = None
    for iteration in range(ITERS + 1):
        gathered = swap(message, "col")
        upper_terms, *lower_terms = adjoint(gathered, iteration == 0, products[-1:] or all_keys[1:])
        parts, beta, right_raw, all_terms = voxel(exchange(upper_terms, "row"), previous)
        if iteration == ITERS:
            break
        products.append(share(all_terms, exchange(lower_terms[0], "row") if lower_terms else []))
        left_raw, alpha, message, squares = ray(swap(parts, "col"), left_raw, beta)
        betas.append(beta)
        alphas.append(alpha)
        previous = (right_raw, alpha)
    result, ratio = pl.pallas_call(
        functools.partial(final_kernel, ITERS),
        out_shape=[f32(RHS, col_tiles // rows * tile_size), f32(RHS)],
        in_specs=[VMEM] * (1 + 3 * ITERS),
        out_specs=[VMEM, SMEM],
        compiler_params=PARAMS,
        name="final",
    )(swap(squares, ("row", "col")), *betas, *alphas, *products)
    return result, ratio


def solution(mesh):
    in_specs = (P(None, ("row", "col")), P("row", "col", None, None), P("row", "col"))
    out_specs = (P(None, ("col", "row")), P())
    return jax.shard_map(local, mesh=mesh, in_specs=in_specs, out_specs=out_specs, check_vma=False)
```

```python
import functools

import jax
import jax.numpy as jnp
from jax import lax
from jax.experimental import pallas as pl
from jax.experimental.pallas import tpu as pltpu
from jax.sharding import PartitionSpec as P

ITERS = 2
N = 1048576
epsilon_sq = 1e-06
LANES = 128
RHS = 4
VMEM = pl.BlockSpec(memory_space=pltpu.VMEM)
SMEM = pl.BlockSpec(memory_space=pltpu.SMEM)
HBM = pl.BlockSpec(memory_space=pltpu.HBM)
ANY = pl.BlockSpec(memory_space=pl.ANY)
PARAMS = pltpu.CompilerParams(vmem_limit_bytes=32 * 1024 * 1024)


def tree_sum(parts):
    while len(parts) > 1:
        paired = [parts[i] + parts[i + 1] for i in range(0, len(parts) - 1, 2)]
        parts = paired + parts[2 * len(paired) :]
    return parts[0]


def norm_of(acc):
    rows = jnp.broadcast_to(jnp.sum(acc, axis=1, keepdims=True), acc.shape)
    return jnp.sqrt(rows + pltpu.roll(rows, 4, 0) + epsilon_sq)


def low_half(width):
    return lax.broadcasted_iota(jnp.int32, (8, width), 0) < 4


def in_two(acc):
    upper = acc.astype(jnp.bfloat16).astype(jnp.float32)
    return upper, acc - upper


def write_payload(out_ref, blocks, acc):
    rows = out_ref.shape[0]
    blank = [jnp.zeros((8, LANES), jnp.float32)] * (rows // 8)
    for h in range(2):
        half = (blocks[h::2] + blank)[: rows // 8]
        out_ref[:, h * LANES : (h + 1) * LANES] = jnp.concatenate(half, axis=0).astype(jnp.bfloat16)
    pieces = (list(in_two(acc)) + blank)[: rows // 8]
    out_ref[:, 2 * LANES :] = jnp.concatenate(pieces, axis=0).astype(jnp.bfloat16)


def read_squares(ref):
    both = ref[:, 2 * LANES :].astype(jnp.float32)
    return both[:8] + both[8:16]


def ray_blocks(obs_ref, count):
    obs = obs_ref[...]
    blocks = []
    for b in range(count):
        at = (b // 2) * 4 * LANES + (b % 2) * LANES
        blocks.append(jnp.concatenate([obs[:, at : at + LANES], obs[:, at + 2 * LANES : at + 3 * LANES]], axis=0))
    return blocks


def prepare_kernel(obs_ref, payload_ref):
    blocks = ray_blocks(obs_ref, obs_ref.shape[1] // (2 * LANES))
    squares = tree_sum([b * b for b in blocks])
    for c in range(payload_ref.shape[0]):
        write_payload(payload_ref.at[c], blocks, squares)


def key_row(cols_ref):
    per_block, row_tiles = cols_ref.shape
    width = per_block * row_tiles * RHS
    lane = lax.broadcasted_iota(jnp.int32, (8, width), 1)
    keys = jnp.zeros((8, width), jnp.int32)
    for i in range(row_tiles):
        for k in range(per_block):
            keys = jnp.where(lane // RHS == i * per_block + k, cols_ref[k, i], keys)
    return (keys * RHS + lane % RHS).astype(jnp.float32)


def fill_equal(keys_ref, equal_ref, weight_ref):
    rows, _, per_row = keys_ref.shape

    @pl.loop(0, rows)
    def _(s):
        down = jnp.broadcast_to(keys_ref[s][:1], (LANES, per_row)).T
        at = pl.ds(pl.multiple_of(s * per_row, per_row), per_row)
        count = jnp.zeros((per_row, LANES), jnp.float32)
        for other in range(rows):
            for h in range(per_row // LANES):
                across = keys_ref[other, :1, h * LANES : (h + 1) * LANES]
                same = jnp.where(down == across, 1.0, 0.0)
                count = count + same
                lane = other * per_row + h * LANES
                equal_ref[at, lane : lane + LANES] = same.astype(jnp.bfloat16)
        weight_ref[at, :] = jnp.broadcast_to(1.0 / jnp.sum(count, axis=1, keepdims=True), (per_row, LANES))


def fill_pick(keys_ref, pick_ref):
    rows, _, per_row = keys_ref.shape
    wanted = pick_ref.shape[0]
    step_rows = 128
    start = lax.axis_index("row") * wanted

    @pl.loop(0, wanted // step_rows)
    def _(step):
        down = lax.broadcasted_iota(jnp.int32, (step_rows, LANES), 0) + (start + step * step_rows)
        down = down.astype(jnp.float32)
        at = pl.ds(pl.multiple_of(step * step_rows, step_rows), step_rows)
        for other in range(rows):
            for h in range(per_row // LANES):
                across = keys_ref[other, :1, h * LANES : (h + 1) * LANES]
                lane = other * per_row + h * LANES
                pick_ref[at, lane : lane + LANES] = jnp.where(down == across, 1.0, 0.0).astype(jnp.bfloat16)


def adjoint_kernel(first, *refs):
    if first:
        cols_ref, tiles_ref, payload_ref, term_ref = refs
    else:
        tiles_ref, payload_ref, term_ref = refs
    row_tiles, per_block = tiles_ref.shape[:2]
    shares = payload_ref.shape[0]
    per_share = row_tiles // shares
    terms = row_tiles * per_block * RHS
    squares = tree_sum([read_squares(payload_ref.at[c]) for c in range(shares)])
    if first:
        term_ref[terms : terms + 8] = jnp.concatenate([squares, jnp.zeros_like(squares)], axis=1)
        term_ref[terms + 8 :] = key_row(cols_ref)
    else:
        pieces = jnp.concatenate(in_two(squares), axis=1)
        term_ref[terms:] = jnp.concatenate([pieces, jnp.zeros_like(pieces)], axis=0).astype(jnp.bfloat16)
    low = low_half(2 * LANES)
    for c in range(shares):
        rays = payload_ref[c, :, : 2 * LANES]
        for g in range(per_share // 2):
            i = c * per_share + 2 * g
            wide = [
                jnp.dot(rays, tiles_ref[i + e, k], preferred_element_type=jnp.float32)[8 * g : 8 * g + 8]
                for e in range(2)
                for k in range(2)
            ]
            value = jnp.concatenate(
                [
                    jnp.where(low, wide[0], pltpu.roll(wide[1], 4, 0)),
                    jnp.where(low, pltpu.roll(wide[2], 4, 0), wide[3]),
                ],
                axis=0,
            )
            term_ref[8 * i : 8 * i + 16] = value.astype(term_ref.dtype)


def voxel_kernel(first, rows, tiles_ref, *refs):
    terms, refs = refs[:rows], list(refs[rows:])
    if first:
        out_ref, beta_ref, raw_ref, all_ref, low_ref, equal_ref, weight_ref, keys_ref = refs
    else:
        equal_ref, weight_ref, right_ref, alpha_ref = refs[:4]
        out_ref, beta_ref, raw_ref, all_ref = refs[-4:]
    my_row = lax.axis_index("row")
    row_tiles, per_block = tiles_ref.shape[:2]
    shares = out_ref.shape[0]
    per_share = row_tiles // shares
    per_row = row_tiles * per_block * RHS
    squares = []
    for d in range(rows):
        slot = jnp.bitwise_xor(my_row, d)
        at = pl.ds(pl.multiple_of(slot * per_row, per_row), per_row)
        if first:
            value = terms[d][:per_row]
            upper = value.astype(jnp.bfloat16)
            all_ref[at, :] = upper
            low_ref[at, :] = (value - upper.astype(jnp.float32)).astype(jnp.bfloat16)
            squares.append(terms[d][per_row : per_row + 8, :LANES])
            keys_ref[slot] = terms[d][per_row + 8 :]
        else:
            all_ref[at, :] = terms[d][:per_row]
            pieces = terms[d][per_row:].astype(jnp.float32)[:8]
            squares.append(pieces[:, :LANES] + pieces[:, LANES:])
    if first:
        fill_equal(keys_ref, equal_ref, weight_ref)
    beta = norm_of(tree_sum(squares))
    beta_ref[...] = beta
    wide_scale = jnp.concatenate([1.0 / beta] * 2, axis=1)
    if not first:
        wide_right = jnp.concatenate([beta / alpha_ref[...]] * 2, axis=1)
    acc = jnp.zeros((8, LANES), jnp.float32)
    for s in range(rows):
        same = equal_ref[s * per_row : (s + 1) * per_row, :]
        summed = jnp.dot(same, all_ref[...], preferred_element_type=jnp.float32)
        if first:
            summed = summed + jnp.dot(same, low_ref[...], preferred_element_type=jnp.float32)
        for m in range(per_row // 8):
            at = s * per_row + 8 * m
            raw = summed[8 * m : 8 * m + 8] * wide_scale
            if not first:
                raw = raw - right_ref[at : at + 8] * wide_right
            raw_ref[at : at + 8] = raw
            square = raw * raw
            acc = acc + (square[:, :LANES] + square[:, LANES:]) * weight_ref[at : at + 8]
    low = low_half(2 * LANES)
    own = my_row * per_row
    for c in range(shares):
        for g in range(per_share // 2):
            i = c * per_share + 2 * g
            lhs = raw_ref[pl.ds(pl.multiple_of(own + 8 * i, 16), 16), :].astype(jnp.bfloat16)
            wide = [
                lax.dot_general(
                    lhs, tiles_ref[i + e, k], (((1,), (1,)), ((), ())), preferred_element_type=jnp.float32
                )[8 * e : 8 * e + 8]
                for e in range(2)
                for k in range(2)
            ]
            value = jnp.where(low, wide[0], wide[3]) + pltpu.roll(jnp.where(low, wide[2], wide[1]), 4, 0)
            out_ref[c, 2 * g] = value[:, :LANES]
            out_ref[c, 2 * g + 1] = value[:, LANES:]
        out_ref[c, per_share] = acc


def share_kernel(pieces, first, unread, *refs):
    refs = refs[unread:]
    if first:
        keys_ref, values, out_ref, pick_ref = refs[0], refs[1 : 1 + pieces], refs[-2], refs[-1]
        fill_pick(keys_ref, pick_ref)
    else:
        pick_ref, values, out_ref = refs[0], refs[1 : 1 + pieces], refs[-1]
    step = 128
    for at in range(0, out_ref.shape[0], step):
        pick = pick_ref[at : at + step, :]
        out_ref[at : at + step, :] = tree_sum(
            [jnp.dot(pick, v[...], preferred_element_type=jnp.float32) for v in values]
        )


def ray_kernel(first, part_ref, left_ref, beta_ref, raw_ref, alpha_ref, payload_ref, acc_ref):
    shares, count = part_ref.shape[0], raw_ref.shape[0]
    alpha = norm_of(tree_sum([part_ref[c, count] for c in range(shares)]))
    alpha_ref[...] = alpha
    alpha_inv = 1.0 / alpha
    left_scale = alpha / beta_ref[...]
    left = ray_blocks(left_ref, count) if first else [left_ref[b] for b in range(count)]
    blocks = []
    for b in range(count):
        total = tree_sum([part_ref[c, b] for c in range(shares)])
        blocks.append(total * alpha_inv - left[b] * left_scale)
        raw_ref[b] = blocks[-1]
    acc = tree_sum([b * b for b in blocks])
    for c in range(acc_ref.shape[0]):
        acc_ref[c] = acc
    for c in range(shares):
        write_payload(payload_ref.at[c], blocks, acc)


def final_kernel(iters, last_ref, *refs):
    refs = list(refs)
    betas = [refs.pop(0) for _ in range(iters)]
    alphas = [refs.pop(0) for _ in range(iters)]
    products = [refs.pop(0) for _ in range(iters)]
    out_ref, ratio_ref = refs
    beta = [b[...] for b in betas] + [norm_of(tree_sum([last_ref[r] for r in range(last_ref.shape[0])]))]
    alpha = [a[...] for a in alphas]
    phibar, rhobar = beta[0], alpha[0]
    direction = [1.0 / alpha[0]] + [jnp.zeros_like(phibar)] * (iters - 1)
    weights = [jnp.zeros_like(phibar)] * iters
    for i in range(iters):
        rho = jnp.sqrt(rhobar * rhobar + beta[i + 1] * beta[i + 1])
        cosine, sine = rhobar / rho, beta[i + 1] / rho
        phi = cosine * phibar
        phibar = sine * phibar
        weights = [w + (phi / rho) * d for w, d in zip(weights, direction)]
        if i + 1 < iters:
            theta = sine * alpha[i + 1]
            rhobar = -cosine * alpha[i + 1]
            direction = [-(theta / rho) * d for d in direction]
            direction[i + 1] = direction[i + 1] + 1.0 / alpha[i + 1]
    ratio = phibar / beta[0]
    for n in range(RHS):
        ratio_ref[n] = jnp.max(ratio[n : n + 1])
    scales = []
    carried = jnp.zeros_like(phibar)
    for i in reversed(range(iters)):
        carried = weights[i] - carried
        scales.insert(0, jnp.concatenate([carried / beta[i]] * 2, axis=1))
        if i > 0:
            carried = carried * (beta[i] / alpha[i - 1])
    unroll = 4

    @pl.loop(0, products[0].shape[0] // (8 * unroll))
    def _(step):
        for u in range(unroll):
            m = step * unroll + u
            at = pl.ds(pl.multiple_of(m * 8, 8), 8)
            both = tree_sum([p[at, :] * s for p, s in zip(products, scales)])
            lane = pl.multiple_of(m * 4 * LANES, 4 * LANES)
            out_ref[:, pl.ds(lane, 2 * LANES)] = both[:4]
            out_ref[:, pl.ds(lane + 2 * LANES, 2 * LANES)] = both[4:]


def f32(*shape):
    return jax.ShapeDtypeStruct(shape, jnp.float32)


def bf16(*shape):
    return jax.ShapeDtypeStruct(shape, jnp.bfloat16)


def exchange(value, axis):
    size = lax.axis_size(axis)
    got = [value]
    for d in range(1, size):
        got.append(lax.ppermute(value, axis, [(i, i ^ d) for i in range(size)]))
    return got


def swap(values, axis):
    return lax.all_to_all(values, axis, 0, 0)


def local(observed, tile_values, tile_cols):
    row_tiles, per_block, tile_size = tile_values.shape[:3]
    rows, shares = lax.axis_size("row"), lax.axis_size("col")
    col_tiles = N // (tile_size * shares)
    per_share = row_tiles // shares
    per_row = row_tiles * per_block * RHS
    share_rows = col_tiles // rows * RHS
    payload = bf16(shares, max(16, 4 * per_share), 3 * LANES)

    def call(kernel, name, out_shape, args, in_specs=None):
        return pl.pallas_call(
            kernel,
            out_shape=out_shape,
            in_specs=in_specs or [VMEM] * len(args),
            out_specs=jax.tree.map(lambda _: VMEM, out_shape),
            compiler_params=PARAMS,
            name=name,
        )(*args)

    def adjoint(payloads, first):
        terms = (f32 if first else bf16)(per_row + 16, tile_size)
        args = [tile_cols.T] * first + [tile_values, payloads]
        return call(
            functools.partial(adjoint_kernel, first), "adjoint", terms, args, [SMEM] * first + [VMEM] * 2
        )

    def voxel(term_list, previous):
        first = not previous
        out_shape = [
            f32(shares, per_share + 1, 8, LANES),
            f32(8, LANES),
            f32(rows * per_row, tile_size),
            bf16(rows * per_row, tile_size),
        ]
        if first:
            out_shape += [
                bf16(rows * per_row, tile_size),
                bf16(rows * per_row, rows * per_row),
                f32(rows * per_row, LANES),
                f32(rows, 8, per_row),
            ]
        args = [tile_values, *term_list, *previous]
        specs = [VMEM] * len(args)
        return call(functools.partial(voxel_kernel, first, rows), "voxel", out_shape, args, specs)

    def share(selector, values, after, first):
        out_shape = [f32(share_rows, tile_size)] + [bf16(share_rows, rows * per_row)] * first
        return call(
            functools.partial(share_kernel, len(values), first, len(after)),
            "share",
            out_shape,
            [*after, selector, *values],
            [ANY] * len(after) + [VMEM] * (1 + len(values)),
        )

    def ray(parts, left_raw, beta, first):
        out_shape = [f32(per_share, 8, LANES), f32(8, LANES), payload, f32(rows * shares, 8, LANES)]
        return call(functools.partial(ray_kernel, first), "ray", out_shape, [parts, left_raw, beta])

    message = call(prepare_kernel, "prepare", payload, [observed])
    left_raw = observed
    betas, alphas, products = [], [], []
    previous = []
    waiting = None
    for iteration in range(ITERS + 1):
        first = iteration == 0
        terms = adjoint(swap(message, "col"), first)
        if waiting:
            product, *pick = share(*waiting, [squares if iteration == ITERS else terms], not products)
            selector = pick[0] if pick else selector
            products.append(product)
        parts, beta, right_raw, upper_terms, *fixed = voxel(exchange(terms, "row"), previous)
        if first:
            lower_terms, equal, weight, selector = fixed
        if iteration == ITERS:
            break
        waiting = (selector, [upper_terms, lower_terms] if first else [upper_terms])
        left_raw, alpha, message, squares = ray(swap(parts, "col"), left_raw, beta, first)
        betas.append(beta)
        alphas.append(alpha)
        previous = [equal, weight, right_raw, alpha]
    result, ratio = pl.pallas_call(
        functools.partial(final_kernel, ITERS),
        out_shape=[f32(RHS, col_tiles // rows * tile_size), f32(RHS)],
        in_specs=[VMEM] * (1 + 3 * ITERS),
        out_specs=[VMEM, SMEM],
        compiler_params=PARAMS,
        name="final",
    )(swap(squares, ("row", "col")), *betas, *alphas, *products)
    return result, ratio


def solution(mesh):
    in_specs = (P(None, ("row", "col")), P("row", "col", None, None), P("row", "col"))
    out_specs = (P(None, ("col", "row")), P())
    return jax.shard_map(local, mesh=mesh, in_specs=in_specs, out_specs=out_specs, check_vma=False)
```

```python
import functools

import jax
import jax.numpy as jnp
from jax import lax
from jax.experimental import pallas as pl
from jax.experimental.pallas import tpu as pltpu
from jax.sharding import PartitionSpec as P

ITERS = 2
N = 1048576
epsilon_sq = 1e-06
LANES = 128
RHS = 4
VMEM = pl.BlockSpec(memory_space=pltpu.VMEM)
SMEM = pl.BlockSpec(memory_space=pltpu.SMEM)
HBM = pl.BlockSpec(memory_space=pltpu.HBM)
ANY = pl.BlockSpec(memory_space=pl.ANY)
PARAMS = pltpu.CompilerParams(vmem_limit_bytes=32 * 1024 * 1024)


def tree_sum(parts):
    while len(parts) > 1:
        paired = [parts[i] + parts[i + 1] for i in range(0, len(parts) - 1, 2)]
        parts = paired + parts[2 * len(paired) :]
    return parts[0]


def norm_of(acc):
    rows = jnp.broadcast_to(jnp.sum(acc, axis=1, keepdims=True), acc.shape)
    return jnp.sqrt(rows + pltpu.roll(rows, 4, 0) + epsilon_sq)


def low_half(width):
    return lax.broadcasted_iota(jnp.int32, (8, width), 0) < 4


def in_two(acc):
    upper = acc.astype(jnp.bfloat16).astype(jnp.float32)
    return upper, acc - upper


def write_payload(out_ref, blocks, acc):
    rows = out_ref.shape[0]
    blank = [jnp.zeros((8, LANES), jnp.float32)] * (rows // 8)
    for h in range(2):
        half = (blocks[h::2] + blank)[: rows // 8]
        out_ref[:, h * LANES : (h + 1) * LANES] = jnp.concatenate(half, axis=0).astype(jnp.bfloat16)
    pieces = (list(in_two(acc)) + blank)[: rows // 8]
    out_ref[:, 2 * LANES :] = jnp.concatenate(pieces, axis=0).astype(jnp.bfloat16)


def read_squares(ref):
    both = ref[:, 2 * LANES :].astype(jnp.float32)
    return both[:8] + both[8:16]


def ray_blocks(obs_ref, count):
    obs = obs_ref[...]
    blocks = []
    for b in range(count):
        at = (b // 2) * 4 * LANES + (b % 2) * LANES
        blocks.append(jnp.concatenate([obs[:, at : at + LANES], obs[:, at + 2 * LANES : at + 3 * LANES]], axis=0))
    return blocks


def prepare_kernel(obs_ref, payload_ref):
    blocks = ray_blocks(obs_ref, obs_ref.shape[1] // (2 * LANES))
    write_payload(payload_ref, blocks, tree_sum([b * b for b in blocks]))


def load_kernel(unread_ref, cols_ref, tiles_ref, held_ref, keys_ref, sem):
    copy = pltpu.make_async_copy(tiles_ref, held_ref, sem)
    copy.start()
    keys_ref[...] = key_row(cols_ref)
    copy.wait()


def key_row(cols_ref):
    per_block, row_tiles = cols_ref.shape
    width = per_block * row_tiles * RHS
    lane = lax.broadcasted_iota(jnp.int32, (8, width), 1)
    keys = jnp.zeros((8, width), jnp.int32)
    for i in range(row_tiles):
        for k in range(per_block):
            keys = jnp.where(lane // RHS == i * per_block + k, cols_ref[k, i], keys)
    return (keys * RHS + lane % RHS).astype(jnp.float32)


def fill_equal(keys_ref, equal_ref, weight_ref):
    rows, _, per_row = keys_ref.shape

    @pl.loop(0, rows)
    def _(s):
        down = jnp.broadcast_to(keys_ref[s][:1], (LANES, per_row)).T
        at = pl.ds(pl.multiple_of(s * per_row, per_row), per_row)
        count = jnp.zeros((per_row, LANES), jnp.float32)
        for other in range(rows):
            for h in range(per_row // LANES):
                across = keys_ref[other, :1, h * LANES : (h + 1) * LANES]
                same = jnp.where(down == across, 1.0, 0.0)
                count = count + same
                lane = other * per_row + h * LANES
                equal_ref[at, lane : lane + LANES] = same.astype(jnp.bfloat16)
        weight_ref[at, :] = jnp.broadcast_to(1.0 / jnp.sum(count, axis=1, keepdims=True), (per_row, LANES))


def fill_pick(keys_ref, pick_ref):
    rows, _, per_row = keys_ref.shape
    wanted = pick_ref.shape[0]
    step_rows = 128
    start = lax.axis_index("row") * wanted

    @pl.loop(0, wanted // step_rows)
    def _(step):
        down = lax.broadcasted_iota(jnp.int32, (step_rows, LANES), 0) + (start + step * step_rows)
        down = down.astype(jnp.float32)
        at = pl.ds(pl.multiple_of(step * step_rows, step_rows), step_rows)
        for other in range(rows):
            for h in range(per_row // LANES):
                across = keys_ref[other, :1, h * LANES : (h + 1) * LANES]
                lane = other * per_row + h * LANES
                pick_ref[at, lane : lane + LANES] = jnp.where(down == across, 1.0, 0.0).astype(jnp.bfloat16)


def adjoint_kernel(first, *refs):
    if first:
        keys_ref, tiles_ref = refs[:2]
        payloads, term_ref = refs[2:-1], refs[-1]
        shares = len(payloads)
    else:
        tiles_ref, payload_ref, term_ref = refs
        shares = payload_ref.shape[0]
        payloads = [payload_ref.at[c] for c in range(shares)]
    row_tiles, per_block = tiles_ref.shape[:2]
    per_share = row_tiles // shares
    terms = row_tiles * per_block * RHS
    squares = tree_sum([read_squares(p) for p in payloads])
    if first:
        term_ref[terms : terms + 8] = jnp.concatenate([squares, jnp.zeros_like(squares)], axis=1)
        term_ref[terms + 8 :] = keys_ref[...]
    else:
        pieces = jnp.concatenate(in_two(squares), axis=1)
        term_ref[terms:] = jnp.concatenate([pieces, jnp.zeros_like(pieces)], axis=0).astype(jnp.bfloat16)
    low = low_half(2 * LANES)
    for c in range(shares):
        rays = payloads[c][:, : 2 * LANES]
        owner = jnp.bitwise_xor(lax.axis_index("col"), c) if first else c
        for g in range(per_share // 2):
            i = owner * per_share + 2 * g
            wide = [
                jnp.dot(rays, tiles_ref[i + e, k], preferred_element_type=jnp.float32)[8 * g : 8 * g + 8]
                for e in range(2)
                for k in range(2)
            ]
            value = jnp.concatenate(
                [
                    jnp.where(low, wide[0], pltpu.roll(wide[1], 4, 0)),
                    jnp.where(low, pltpu.roll(wide[2], 4, 0), wide[3]),
                ],
                axis=0,
            )
            at = pl.multiple_of(8 * i, 16) if first else 8 * i
            term_ref[pl.ds(at, 16), :] = value.astype(term_ref.dtype)


def voxel_kernel(first, rows, tiles_ref, *refs):
    terms, refs = refs[:rows], list(refs[rows:])
    if first:
        out_ref, beta_ref, raw_ref, all_ref, low_ref, equal_ref, weight_ref, keys_ref = refs
    else:
        equal_ref, weight_ref, right_ref, alpha_ref = refs[:4]
        out_ref, beta_ref, raw_ref, all_ref = refs[-4:]
    my_row = lax.axis_index("row")
    row_tiles, per_block = tiles_ref.shape[:2]
    shares = out_ref.shape[0]
    per_share = row_tiles // shares
    per_row = row_tiles * per_block * RHS
    squares = []
    for d in range(rows):
        slot = jnp.bitwise_xor(my_row, d)
        at = pl.ds(pl.multiple_of(slot * per_row, per_row), per_row)
        if first:
            value = terms[d][:per_row]
            upper = value.astype(jnp.bfloat16)
            all_ref[at, :] = upper
            low_ref[at, :] = (value - upper.astype(jnp.float32)).astype(jnp.bfloat16)
            squares.append(terms[d][per_row : per_row + 8, :LANES])
            keys_ref[slot] = terms[d][per_row + 8 :]
        else:
            all_ref[at, :] = terms[d][:per_row]
            pieces = terms[d][per_row:].astype(jnp.float32)[:8]
            squares.append(pieces[:, :LANES] + pieces[:, LANES:])
    if first:
        fill_equal(keys_ref, equal_ref, weight_ref)
    beta = norm_of(tree_sum(squares))
    beta_ref[...] = beta
    wide_scale = jnp.concatenate([1.0 / beta] * 2, axis=1)
    if not first:
        wide_right = jnp.concatenate([beta / alpha_ref[...]] * 2, axis=1)
    acc = jnp.zeros((8, LANES), jnp.float32)
    for s in range(rows):
        same = equal_ref[s * per_row : (s + 1) * per_row, :]
        summed = jnp.dot(same, all_ref[...], preferred_element_type=jnp.float32)
        if first:
            summed = summed + jnp.dot(same, low_ref[...], preferred_element_type=jnp.float32)
        for m in range(per_row // 8):
            at = s * per_row + 8 * m
            raw = summed[8 * m : 8 * m + 8] * wide_scale
            if not first:
                raw = raw - right_ref[at : at + 8] * wide_right
            raw_ref[at : at + 8] = raw
            square = raw * raw
            acc = acc + (square[:, :LANES] + square[:, LANES:]) * weight_ref[at : at + 8]
    low = low_half(2 * LANES)
    own = my_row * per_row
    for c in range(shares):
        for g in range(per_share // 2):
            i = c * per_share + 2 * g
            lhs = raw_ref[pl.ds(pl.multiple_of(own + 8 * i, 16), 16), :].astype(jnp.bfloat16)
            wide = [
                lax.dot_general(
                    lhs, tiles_ref[i + e, k], (((1,), (1,)), ((), ())), preferred_element_type=jnp.float32
                )[8 * e : 8 * e + 8]
                for e in range(2)
                for k in range(2)
            ]
            value = jnp.where(low, wide[0], wide[3]) + pltpu.roll(jnp.where(low, wide[2], wide[1]), 4, 0)
            out_ref[c, 2 * g] = value[:, :LANES]
            out_ref[c, 2 * g + 1] = value[:, LANES:]
        out_ref[c, per_share] = acc


def share_kernel(pieces, first, unread, *refs):
    refs = refs[unread:]
    if first:
        keys_ref, values, out_ref, pick_ref = refs[0], refs[1 : 1 + pieces], refs[-2], refs[-1]
        fill_pick(keys_ref, pick_ref)
    else:
        pick_ref, values, out_ref = refs[0], refs[1 : 1 + pieces], refs[-1]
    step = 128
    for at in range(0, out_ref.shape[0], step):
        pick = pick_ref[at : at + step, :]
        out_ref[at : at + step, :] = tree_sum(
            [jnp.dot(pick, v[...], preferred_element_type=jnp.float32) for v in values]
        )


def ray_kernel(first, part_ref, left_ref, beta_ref, raw_ref, alpha_ref, payload_ref, acc_ref):
    shares, count = part_ref.shape[0], raw_ref.shape[0]
    alpha = norm_of(tree_sum([part_ref[c, count] for c in range(shares)]))
    alpha_ref[...] = alpha
    alpha_inv = 1.0 / alpha
    left_scale = alpha / beta_ref[...]
    left = ray_blocks(left_ref, count) if first else [left_ref[b] for b in range(count)]
    blocks = []
    for b in range(count):
        total = tree_sum([part_ref[c, b] for c in range(shares)])
        blocks.append(total * alpha_inv - left[b] * left_scale)
        raw_ref[b] = blocks[-1]
    acc = tree_sum([b * b for b in blocks])
    for c in range(acc_ref.shape[0]):
        acc_ref[c] = acc
    for c in range(shares):
        write_payload(payload_ref.at[c], blocks, acc)


def final_kernel(iters, last_ref, *refs):
    refs = list(refs)
    betas = [refs.pop(0) for _ in range(iters)]
    alphas = [refs.pop(0) for _ in range(iters)]
    products = [refs.pop(0) for _ in range(iters)]
    out_ref, ratio_ref = refs
    beta = [b[...] for b in betas] + [norm_of(tree_sum([last_ref[r] for r in range(last_ref.shape[0])]))]
    alpha = [a[...] for a in alphas]
    phibar, rhobar = beta[0], alpha[0]
    direction = [1.0 / alpha[0]] + [jnp.zeros_like(phibar)] * (iters - 1)
    weights = [jnp.zeros_like(phibar)] * iters
    for i in range(iters):
        rho = jnp.sqrt(rhobar * rhobar + beta[i + 1] * beta[i + 1])
        cosine, sine = rhobar / rho, beta[i + 1] / rho
        phi = cosine * phibar
        phibar = sine * phibar
        weights = [w + (phi / rho) * d for w, d in zip(weights, direction)]
        if i + 1 < iters:
            theta = sine * alpha[i + 1]
            rhobar = -cosine * alpha[i + 1]
            direction = [-(theta / rho) * d for d in direction]
            direction[i + 1] = direction[i + 1] + 1.0 / alpha[i + 1]
    ratio = phibar / beta[0]
    for n in range(RHS):
        ratio_ref[n] = jnp.max(ratio[n : n + 1])
    scales = []
    carried = jnp.zeros_like(phibar)
    for i in reversed(range(iters)):
        carried = weights[i] - carried
        scales.insert(0, jnp.concatenate([carried / beta[i]] * 2, axis=1))
        if i > 0:
            carried = carried * (beta[i] / alpha[i - 1])
    unroll = 4

    @pl.loop(0, products[0].shape[0] // (8 * unroll))
    def _(step):
        for u in range(unroll):
            m = step * unroll + u
            at = pl.ds(pl.multiple_of(m * 8, 8), 8)
            both = tree_sum([p[at, :] * s for p, s in zip(products, scales)])
            lane = pl.multiple_of(m * 4 * LANES, 4 * LANES)
            out_ref[:, pl.ds(lane, 2 * LANES)] = both[:4]
            out_ref[:, pl.ds(lane + 2 * LANES, 2 * LANES)] = both[4:]


def f32(*shape):
    return jax.ShapeDtypeStruct(shape, jnp.float32)


def bf16(*shape):
    return jax.ShapeDtypeStruct(shape, jnp.bfloat16)


def exchange(value, axis):
    size = lax.axis_size(axis)
    got = [value]
    for d in range(1, size):
        got.append(lax.ppermute(value, axis, [(i, i ^ d) for i in range(size)]))
    return got


def swap(values, axis):
    return lax.all_to_all(values, axis, 0, 0)


def local(observed, tile_values, tile_cols):
    row_tiles, per_block, tile_size = tile_values.shape[:3]
    rows, shares = lax.axis_size("row"), lax.axis_size("col")
    col_tiles = N // (tile_size * shares)
    per_share = row_tiles // shares
    per_row = row_tiles * per_block * RHS
    share_rows = col_tiles // rows * RHS
    payload = bf16(max(16, 4 * per_share), 3 * LANES)
    payloads = bf16(shares, *payload.shape)

    def call(kernel, name, out_shape, args, in_specs=None):
        return pl.pallas_call(
            kernel,
            out_shape=out_shape,
            in_specs=in_specs or [VMEM] * len(args),
            out_specs=jax.tree.map(lambda _: VMEM, out_shape),
            compiler_params=PARAMS,
            name=name,
        )(*args)

    def adjoint(payloads, first):
        terms = (f32 if first else bf16)(per_row + 16, tile_size)
        args = [keys, tiles, *payloads] if first else [tiles, payloads]
        return call(functools.partial(adjoint_kernel, first), "adjoint", terms, args)

    def voxel(term_list, previous):
        first = not previous
        out_shape = [
            f32(shares, per_share + 1, 8, LANES),
            f32(8, LANES),
            f32(rows * per_row, tile_size),
            bf16(rows * per_row, tile_size),
        ]
        if first:
            out_shape += [
                bf16(rows * per_row, tile_size),
                bf16(rows * per_row, rows * per_row),
                f32(rows * per_row, LANES),
                f32(rows, 8, per_row),
            ]
        args = [tiles, *term_list, *previous]
        return call(functools.partial(voxel_kernel, first, rows), "voxel", out_shape, args)

    def share(selector, values, after, first):
        out_shape = [f32(share_rows, tile_size)] + [bf16(share_rows, rows * per_row)] * first
        return call(
            functools.partial(share_kernel, len(values), first, len(after)),
            "share",
            out_shape,
            [*after, selector, *values],
            [ANY] * len(after) + [VMEM] * (1 + len(values)),
        )

    def ray(parts, left_raw, beta, first):
        out_shape = [f32(per_share, 8, LANES), f32(8, LANES), payloads, f32(rows * shares, 8, LANES)]
        return call(functools.partial(ray_kernel, first), "ray", out_shape, [parts, left_raw, beta])

    message = call(prepare_kernel, "prepare", payload, [observed])
    tiles, keys = pl.pallas_call(
        load_kernel,
        out_shape=[jax.ShapeDtypeStruct(tile_values.shape, tile_values.dtype), f32(8, per_row)],
        in_specs=[ANY, SMEM, HBM],
        out_specs=[VMEM, VMEM],
        scratch_shapes=[pltpu.SemaphoreType.DMA],
        compiler_params=PARAMS,
        name="load",
    )(message, tile_cols.T, pltpu.with_memory_space_constraint(tile_values, pltpu.HBM))
    left_raw = observed
    betas, alphas, products = [], [], []
    previous = []
    waiting = None
    for iteration in range(ITERS + 1):
        first = iteration == 0
        terms = adjoint(exchange(message, "col") if first else swap(message, "col"), first)
        if waiting:
            product, *pick = share(*waiting, [squares if iteration == ITERS else terms], not products)
            selector = pick[0] if pick else selector
            products.append(product)
        parts, beta, right_raw, upper_terms, *fixed = voxel(exchange(terms, "row"), previous)
        if first:
            lower_terms, equal, weight, selector = fixed
        if iteration == ITERS:
            break
        waiting = (selector, [upper_terms, lower_terms] if first else [upper_terms])
        left_raw, alpha, message, squares = ray(swap(parts, "col"), left_raw, beta, first)
        betas.append(beta)
        alphas.append(alpha)
        previous = [equal, weight, right_raw, alpha]
    result, ratio = pl.pallas_call(
        functools.partial(final_kernel, ITERS),
        out_shape=[f32(RHS, col_tiles // rows * tile_size), f32(RHS)],
        in_specs=[VMEM] * (1 + 3 * ITERS),
        out_specs=[VMEM, SMEM],
        compiler_params=PARAMS,
        name="final",
    )(swap(squares, ("row", "col")), *betas, *alphas, *products)
    return result, ratio


def solution(mesh):
    in_specs = (P(None, ("row", "col")), P("row", "col", None, None), P("row", "col"))
    out_specs = (P(None, ("col", "row")), P())
    return jax.shard_map(local, mesh=mesh, in_specs=in_specs, out_specs=out_specs, check_vma=False)
```

```python
import functools

import jax
import jax.numpy as jnp
from jax import lax
from jax.experimental import pallas as pl
from jax.experimental.pallas import tpu as pltpu
from jax.sharding import PartitionSpec as P

ITERS = 2
N = 1048576
epsilon_sq = 1e-06
LANES = 128
RHS = 4
VMEM = pl.BlockSpec(memory_space=pltpu.VMEM)
SMEM = pl.BlockSpec(memory_space=pltpu.SMEM)
HBM = pl.BlockSpec(memory_space=pltpu.HBM)
ANY = pl.BlockSpec(memory_space=pl.ANY)
PARAMS = pltpu.CompilerParams(vmem_limit_bytes=32 * 1024 * 1024)


def tree_sum(parts):
    while len(parts) > 1:
        paired = [parts[i] + parts[i + 1] for i in range(0, len(parts) - 1, 2)]
        parts = paired + parts[2 * len(paired) :]
    return parts[0]


def norm_of(acc):
    rows = jnp.broadcast_to(jnp.sum(acc, axis=1, keepdims=True), acc.shape)
    return jnp.sqrt(rows + pltpu.roll(rows, 4, 0) + epsilon_sq)


def low_half(width):
    return lax.broadcasted_iota(jnp.int32, (8, width), 0) < 4


def in_two(acc):
    upper = acc.astype(jnp.bfloat16).astype(jnp.float32)
    return upper, acc - upper


def write_payload(out_ref, blocks, acc):
    rows = out_ref.shape[0]
    blank = [jnp.zeros((8, LANES), jnp.float32)] * (rows // 8)
    for h in range(2):
        half = (blocks[h::2] + blank)[: rows // 8]
        out_ref[:, h * LANES : (h + 1) * LANES] = jnp.concatenate(half, axis=0).astype(jnp.bfloat16)
    pieces = (list(in_two(acc)) + blank)[: rows // 8]
    out_ref[:, 2 * LANES :] = jnp.concatenate(pieces, axis=0).astype(jnp.bfloat16)


def read_squares(ref):
    both = ref[:, 2 * LANES :].astype(jnp.float32)
    return both[:8] + both[8:16]


def ray_blocks(obs_ref, count):
    obs = obs_ref[...]
    blocks = []
    for b in range(count):
        at = (b // 2) * 4 * LANES + (b % 2) * LANES
        blocks.append(jnp.concatenate([obs[:, at : at + LANES], obs[:, at + 2 * LANES : at + 3 * LANES]], axis=0))
    return blocks


def prepare_kernel(obs_ref, unread_ref, payload_ref):
    blocks = ray_blocks(obs_ref, obs_ref.shape[1] // (2 * LANES))
    write_payload(payload_ref, blocks, tree_sum([b * b for b in blocks]))


def keys_kernel(unread_ref, cols_ref, keys_ref):
    keys_ref[...] = key_row(cols_ref)


def key_row(cols_ref):
    per_block, row_tiles = cols_ref.shape
    width = per_block * row_tiles * RHS
    lane = lax.broadcasted_iota(jnp.int32, (8, width), 1)
    keys = jnp.zeros((8, width), jnp.int32)
    for i in range(row_tiles):
        for k in range(per_block):
            keys = jnp.where(lane // RHS == i * per_block + k, cols_ref[k, i], keys)
    return (keys * RHS + lane % RHS).astype(jnp.float32)


def fill_equal(keys_ref, equal_ref, weight_ref):
    rows, _, per_row = keys_ref.shape

    @pl.loop(0, rows)
    def _(s):
        down = jnp.broadcast_to(keys_ref[s][:1], (LANES, per_row)).T
        at = pl.ds(pl.multiple_of(s * per_row, per_row), per_row)
        count = jnp.zeros((per_row, LANES), jnp.float32)
        for other in range(rows):
            for h in range(per_row // LANES):
                across = keys_ref[other, :1, h * LANES : (h + 1) * LANES]
                same = jnp.where(down == across, 1.0, 0.0)
                count = count + same
                lane = other * per_row + h * LANES
                equal_ref[at, lane : lane + LANES] = same.astype(jnp.bfloat16)
        weight_ref[at, :] = jnp.broadcast_to(1.0 / jnp.sum(count, axis=1, keepdims=True), (per_row, LANES))


def fill_pick(keys_ref, pick_ref):
    rows, _, per_row = keys_ref.shape
    wanted = pick_ref.shape[0]
    step_rows = 128
    start = lax.axis_index("row") * wanted

    @pl.loop(0, wanted // step_rows)
    def _(step):
        down = lax.broadcasted_iota(jnp.int32, (step_rows, LANES), 0) + (start + step * step_rows)
        down = down.astype(jnp.float32)
        at = pl.ds(pl.multiple_of(step * step_rows, step_rows), step_rows)
        for other in range(rows):
            for h in range(per_row // LANES):
                across = keys_ref[other, :1, h * LANES : (h + 1) * LANES]
                lane = other * per_row + h * LANES
                pick_ref[at, lane : lane + LANES] = jnp.where(down == across, 1.0, 0.0).astype(jnp.bfloat16)


def adjoint_kernel(first, *refs):
    if first:
        keys_ref, tiles_ref = refs[:2]
        payloads, (term_ref, lower_ref) = refs[2:-2], refs[-2:]
        shares = len(payloads)
    else:
        tiles_ref, payload_ref, term_ref = refs
        shares = payload_ref.shape[0]
        payloads = [payload_ref.at[c] for c in range(shares)]
    row_tiles, per_block = tiles_ref.shape[:2]
    per_share = row_tiles // shares
    terms = row_tiles * per_block * RHS
    squares = tree_sum([read_squares(p) for p in payloads])
    low = low_half(2 * LANES)
    pieces = jnp.concatenate(in_two(squares), axis=1)
    extra = jnp.zeros_like(pieces)
    if first:
        keys = keys_ref[...]
        coarse = jnp.floor(keys * (1.0 / 64))
        extra = jnp.where(low, coarse, keys - 64 * coarse)
    term_ref[terms:] = jnp.concatenate([pieces, extra], axis=0).astype(jnp.bfloat16)
    for c in range(shares):
        rays = payloads[c][:, : 2 * LANES]
        owner = jnp.bitwise_xor(lax.axis_index("col"), c) if first else c
        for g in range(per_share // 2):
            i = owner * per_share + 2 * g
            wide = [
                jnp.dot(rays, tiles_ref[i + e, k], preferred_element_type=jnp.float32)[8 * g : 8 * g + 8]
                for e in range(2)
                for k in range(2)
            ]
            value = jnp.concatenate(
                [
                    jnp.where(low, wide[0], pltpu.roll(wide[1], 4, 0)),
                    jnp.where(low, pltpu.roll(wide[2], 4, 0), wide[3]),
                ],
                axis=0,
            )
            at = pl.multiple_of(8 * i, 16) if first else 8 * i
            upper = value.astype(jnp.bfloat16)
            term_ref[pl.ds(at, 16), :] = upper
            if first:
                lower_ref[pl.ds(at, 16), :] = (value - upper.astype(jnp.float32)).astype(jnp.bfloat16)


def voxel_kernel(first, rows, tiles_ref, *refs):
    terms, refs = refs[:rows], list(refs[rows:])
    if first:
        out_ref, beta_ref, raw_ref, all_ref, equal_ref, weight_ref, keys_ref = refs
    else:
        equal_ref, weight_ref, right_ref, alpha_ref = refs[:4]
        out_ref, beta_ref, raw_ref, all_ref = refs[-4:]
    my_row = lax.axis_index("row")
    row_tiles, per_block = tiles_ref.shape[:2]
    shares = out_ref.shape[0]
    per_share = row_tiles // shares
    per_row = row_tiles * per_block * RHS
    low = low_half(2 * LANES)
    squares = []
    for d in range(rows):
        slot = jnp.bitwise_xor(my_row, d)
        at = pl.ds(pl.multiple_of(slot * per_row, per_row), per_row)
        all_ref[at, :] = terms[d][:per_row]
        extra = terms[d][per_row:].astype(jnp.float32)
        squares.append(extra[:8, :LANES] + extra[:8, LANES:])
        if first:
            pieces = jnp.where(low, extra[8:] * 64, extra[8:])
            keys_ref[slot] = pieces + pltpu.roll(pieces, 4, 0)
    if first:
        fill_equal(keys_ref, equal_ref, weight_ref)
    beta = norm_of(tree_sum(squares))
    beta_ref[...] = beta
    wide_scale = jnp.concatenate([1.0 / beta] * 2, axis=1)
    if not first:
        wide_right = jnp.concatenate([beta / alpha_ref[...]] * 2, axis=1)
    acc = jnp.zeros((8, LANES), jnp.float32)
    for s in range(rows):
        same = equal_ref[s * per_row : (s + 1) * per_row, :]
        summed = jnp.dot(same, all_ref[...], preferred_element_type=jnp.float32)
        for m in range(per_row // 8):
            at = s * per_row + 8 * m
            raw = summed[8 * m : 8 * m + 8] * wide_scale
            if not first:
                raw = raw - right_ref[at : at + 8] * wide_right
            raw_ref[at : at + 8] = raw
            square = raw * raw
            acc = acc + (square[:, :LANES] + square[:, LANES:]) * weight_ref[at : at + 8]
    own = my_row * per_row
    for c in range(shares):
        for g in range(per_share // 2):
            i = c * per_share + 2 * g
            lhs = raw_ref[pl.ds(pl.multiple_of(own + 8 * i, 16), 16), :].astype(jnp.bfloat16)
            wide = [
                lax.dot_general(
                    lhs, tiles_ref[i + e, k], (((1,), (1,)), ((), ())), preferred_element_type=jnp.float32
                )[8 * e : 8 * e + 8]
                for e in range(2)
                for k in range(2)
            ]
            value = jnp.where(low, wide[0], wide[3]) + pltpu.roll(jnp.where(low, wide[2], wide[1]), 4, 0)
            out_ref[c, 2 * g] = value[:, :LANES]
            out_ref[c, 2 * g + 1] = value[:, LANES:]
        out_ref[c, per_share] = acc


def share_kernel(remainders, *refs):
    pick_ref, all_ref = refs[1:3]
    lower_terms, out_ref = refs[3 : 3 + remainders], refs[3 + remainders]
    values = [all_ref]
    if remainders:
        held = refs[-1]
        per_row = lower_terms[0].shape[0]
        for d, term in enumerate(lower_terms):
            slot = jnp.bitwise_xor(lax.axis_index("row"), d)
            held[pl.ds(pl.multiple_of(slot * per_row, per_row), per_row), :] = term[...]
        values.append(held)
    step = 128
    for at in range(0, out_ref.shape[0], step):
        pick = pick_ref[at : at + step, :]
        out_ref[at : at + step, :] = tree_sum(
            [jnp.dot(pick, v[...], preferred_element_type=jnp.float32) for v in values]
        )


def pick_kernel(unread_ref, keys_ref, pick_ref):
    fill_pick(keys_ref, pick_ref)


def ray_kernel(first, part_ref, left_ref, beta_ref, *refs):
    if not first:
        refs[-1][...] = refs[0][...]
        refs = refs[1:-1]
    raw_ref, alpha_ref, payload_ref, acc_ref = refs
    shares, count = part_ref.shape[0], raw_ref.shape[0]
    alpha = norm_of(tree_sum([part_ref[c, count] for c in range(shares)]))
    alpha_ref[...] = alpha
    alpha_inv = 1.0 / alpha
    left_scale = alpha / beta_ref[...]
    left = ray_blocks(left_ref, count) if first else [left_ref[b] for b in range(count)]
    blocks = []
    for b in range(count):
        total = tree_sum([part_ref[c, b] for c in range(shares)])
        blocks.append(total * alpha_inv - left[b] * left_scale)
        raw_ref[b] = blocks[-1]
    acc = tree_sum([b * b for b in blocks])
    for c in range(acc_ref.shape[0]):
        acc_ref[c] = acc
    for c in range(shares):
        write_payload(payload_ref.at[c], blocks, acc)


def final_kernel(iters, last_ref, *refs):
    refs = list(refs)
    betas = [refs.pop(0) for _ in range(iters)]
    alphas = [refs.pop(0) for _ in range(iters)]
    products = [refs.pop(0) for _ in range(iters)]
    out_ref, ratio_ref = refs
    beta = [b[...] for b in betas] + [norm_of(tree_sum([last_ref[r] for r in range(last_ref.shape[0])]))]
    alpha = [a[...] for a in alphas]
    phibar, rhobar = beta[0], alpha[0]
    direction = [1.0 / alpha[0]] + [jnp.zeros_like(phibar)] * (iters - 1)
    weights = [jnp.zeros_like(phibar)] * iters
    for i in range(iters):
        rho = jnp.sqrt(rhobar * rhobar + beta[i + 1] * beta[i + 1])
        cosine, sine = rhobar / rho, beta[i + 1] / rho
        phi = cosine * phibar
        phibar = sine * phibar
        weights = [w + (phi / rho) * d for w, d in zip(weights, direction)]
        if i + 1 < iters:
            theta = sine * alpha[i + 1]
            rhobar = -cosine * alpha[i + 1]
            direction = [-(theta / rho) * d for d in direction]
            direction[i + 1] = direction[i + 1] + 1.0 / alpha[i + 1]
    ratio = phibar / beta[0]
    for n in range(RHS):
        ratio_ref[n] = jnp.max(ratio[n : n + 1])
    scales = []
    carried = jnp.zeros_like(phibar)
    for i in reversed(range(iters)):
        carried = weights[i] - carried
        scales.insert(0, jnp.concatenate([carried / beta[i]] * 2, axis=1))
        if i > 0:
            carried = carried * (beta[i] / alpha[i - 1])
    unroll = 4

    @pl.loop(0, products[0].shape[0] // (8 * unroll))
    def _(step):
        for u in range(unroll):
            m = step * unroll + u
            at = pl.ds(pl.multiple_of(m * 8, 8), 8)
            both = tree_sum([p[at, :] * s for p, s in zip(products, scales)])
            lane = pl.multiple_of(m * 4 * LANES, 4 * LANES)
            out_ref[:, pl.ds(lane, 2 * LANES)] = both[:4]
            out_ref[:, pl.ds(lane + 2 * LANES, 2 * LANES)] = both[4:]


def f32(*shape):
    return jax.ShapeDtypeStruct(shape, jnp.float32)


def bf16(*shape):
    return jax.ShapeDtypeStruct(shape, jnp.bfloat16)


def exchange(value, axis):
    size = lax.axis_size(axis)
    got = [value]
    for d in range(1, size):
        got.append(lax.ppermute(value, axis, [(i, i ^ d) for i in range(size)]))
    return got


def swap(values, axis):
    return lax.all_to_all(values, axis, 0, 0)


def local(observed, tile_values, tile_cols):
    row_tiles, per_block, tile_size = tile_values.shape[:3]
    rows, shares = lax.axis_size("row"), lax.axis_size("col")
    col_tiles = N // (tile_size * shares)
    per_share = row_tiles // shares
    per_row = row_tiles * per_block * RHS
    share_rows = col_tiles // rows * RHS
    payload = bf16(max(16, 4 * per_share), 3 * LANES)
    payloads = bf16(shares, *payload.shape)

    def call(kernel, name, out_shape, args, in_specs=None, scratch=()):
        return pl.pallas_call(
            kernel,
            out_shape=out_shape,
            in_specs=in_specs or [VMEM] * len(args),
            out_specs=jax.tree.map(lambda _: VMEM, out_shape),
            scratch_shapes=list(scratch),
            compiler_params=PARAMS,
            name=name,
        )(*args)

    def adjoint(payloads, first):
        out_shape = [bf16(per_row + 16, tile_size)] + [bf16(per_row, tile_size)] * first
        args = [keys, tile_values, *payloads] if first else [tile_values, payloads]
        return call(functools.partial(adjoint_kernel, first), "adjoint", out_shape, args)

    def voxel(term_list, previous):
        first = not previous
        out_shape = [
            f32(shares, per_share + 1, 8, LANES),
            f32(8, LANES),
            f32(rows * per_row, tile_size),
            bf16(rows * per_row, tile_size),
        ]
        if first:
            out_shape += [
                bf16(rows * per_row, rows * per_row),
                f32(rows * per_row, LANES),
                f32(rows, 8, per_row),
            ]
        args = [tile_values, *term_list, *previous]
        return call(functools.partial(voxel_kernel, first, rows), "voxel", out_shape, args)

    def share(selector, all_terms, lower_terms):
        scratch = [pltpu.VMEM((rows * per_row, tile_size), jnp.bfloat16)] * (len(lower_terms) > 0)
        kernel = functools.partial(share_kernel, len(lower_terms))
        args = [squares, selector, all_terms, *lower_terms]
        specs = [ANY] + [VMEM] * (len(args) - 1)
        return call(kernel, "share", f32(share_rows, tile_size), args, specs, scratch)

    def ray(parts, left_raw, beta, passed):
        out_shape = [f32(per_share, 8, LANES), f32(8, LANES), payloads, f32(rows * shares, 8, LANES)]
        out_shape += [bf16(per_row, tile_size) for _ in passed]
        return call(functools.partial(ray_kernel, not passed), "ray", out_shape, [parts, left_raw, beta, *passed])

    far = pltpu.with_memory_space_constraint(tile_values, pltpu.HBM)
    message = call(prepare_kernel, "prepare", payload, [observed, far], [VMEM, HBM])
    keys = call(keys_kernel, "keys", f32(8, per_row), [message, tile_cols.T], [ANY, SMEM])
    left_raw = observed
    betas, alphas, combined = [], [], []
    previous = []
    for iteration in range(ITERS + 1):
        first = iteration == 0
        terms, *lower = adjoint(exchange(message, "col") if first else swap(message, "col"), first)
        if iteration == 1:
            selector = call(pick_kernel, "pick", bf16(share_rows, rows * per_row), [terms, all_keys], [ANY, VMEM])
        parts, beta, right_raw, upper_terms, *fixed = voxel(exchange(terms, "row"), previous)
        if iteration == ITERS:
            break
        if first:
            equal, weight, all_keys = fixed
            remainder = lower[0]
        combined.append(upper_terms)
        left_raw, alpha, message, squares, *passed = ray(
            swap(parts, "col"), left_raw, beta, [] if first else [remainder]
        )
        if passed:
            remainder = passed[0]
        betas.append(beta)
        alphas.append(alpha)
        previous = [equal, weight, right_raw, alpha]
    remainders = exchange(remainder, "row")
    products = [share(selector, c, [] if i else remainders) for i, c in enumerate(combined)]
    result, ratio = pl.pallas_call(
        functools.partial(final_kernel, ITERS),
        out_shape=[f32(RHS, col_tiles // rows * tile_size), f32(RHS)],
        in_specs=[VMEM] * (1 + 3 * ITERS),
        out_specs=[VMEM, SMEM],
        compiler_params=PARAMS,
        name="final",
    )(swap(squares, ("row", "col")), *betas, *alphas, *products)
    return result, ratio


def solution(mesh):
    in_specs = (P(None, ("row", "col")), P("row", "col", None, None), P("row", "col"))
    out_specs = (P(None, ("col", "row")), P())
    return jax.shard_map(local, mesh=mesh, in_specs=in_specs, out_specs=out_specs, check_vma=False)
```

```python
import functools

import jax
import jax.numpy as jnp
from jax import lax
from jax.experimental import pallas as pl
from jax.experimental.pallas import tpu as pltpu
from jax.sharding import PartitionSpec as P

ITERS = 2
N = 1048576
epsilon_sq = 1e-06
LANES = 128
RHS = 4
VMEM = pl.BlockSpec(memory_space=pltpu.VMEM)
SMEM = pl.BlockSpec(memory_space=pltpu.SMEM)
HBM = pl.BlockSpec(memory_space=pltpu.HBM)
ANY = pl.BlockSpec(memory_space=pl.ANY)
PARAMS = pltpu.CompilerParams(vmem_limit_bytes=32 * 1024 * 1024)


def tree_sum(parts):
    while len(parts) > 1:
        paired = [parts[i] + parts[i + 1] for i in range(0, len(parts) - 1, 2)]
        parts = paired + parts[2 * len(paired) :]
    return parts[0]


def norm_of(acc):
    rows = jnp.broadcast_to(jnp.sum(acc, axis=1, keepdims=True), acc.shape)
    return jnp.sqrt(rows + pltpu.roll(rows, 4, 0) + epsilon_sq)


def low_half(width):
    return lax.broadcasted_iota(jnp.int32, (8, width), 0) < 4


def in_two(acc):
    upper = acc.astype(jnp.bfloat16).astype(jnp.float32)
    return upper, acc - upper


def packed(blocks, rows):
    blank = [jnp.zeros((8, LANES), jnp.float32)] * (rows // 8)
    halves = [jnp.concatenate((blocks[h::2] + blank)[: rows // 8], axis=0) for h in range(2)]
    return jnp.concatenate(halves, axis=1).astype(jnp.bfloat16)


def packed_squares(acc):
    return jnp.concatenate(in_two(acc), axis=0).astype(jnp.bfloat16)


def read_squares(both):
    both = both.astype(jnp.float32)
    return both[:8] + both[8:16]


def ray_blocks(obs_ref, count):
    obs = obs_ref[...]
    blocks = []
    for b in range(count):
        at = (b // 2) * 4 * LANES + (b % 2) * LANES
        blocks.append(jnp.concatenate([obs[:, at : at + LANES], obs[:, at + 2 * LANES : at + 3 * LANES]], axis=0))
    return blocks


def pack_kernel(flat, left_ref, unread_ref, payload_ref, blocks_ref):
    count = blocks_ref.shape[0] - 1
    blocks = ray_blocks(left_ref, count) if flat else [left_ref[b] for b in range(count)]
    rows = payload_ref.shape[0]
    payload_ref[:, : 2 * LANES] = packed(blocks, rows)
    payload_ref[:, 2 * LANES :] = jnp.zeros((rows, LANES), jnp.bfloat16)
    squares = packed_squares(tree_sum([b * b for b in blocks]))
    payload_ref[:16, 2 * LANES :] = squares
    for b, block in enumerate(blocks):
        blocks_ref[b] = block
    blocks_ref[count] = read_squares(squares)


def keys_kernel(unread_ref, cols_ref, keys_ref):
    keys_ref[...] = key_row(cols_ref)


def key_row(cols_ref):
    per_block, row_tiles = cols_ref.shape
    width = per_block * row_tiles * RHS
    lane = lax.broadcasted_iota(jnp.int32, (8, width), 1)
    keys = jnp.zeros((8, width), jnp.int32)
    for i in range(row_tiles):
        for k in range(per_block):
            keys = jnp.where(lane // RHS == i * per_block + k, cols_ref[k, i], keys)
    return (keys * RHS + lane % RHS).astype(jnp.float32)


def fill_equal(keys_ref, equal_ref, weight_ref):
    rows, _, per_row = keys_ref.shape

    @pl.loop(0, rows)
    def _(s):
        down = jnp.broadcast_to(keys_ref[s][:1], (LANES, per_row)).T
        at = pl.ds(pl.multiple_of(s * per_row, per_row), per_row)
        count = jnp.zeros((per_row, LANES), jnp.float32)
        for other in range(rows):
            for h in range(per_row // LANES):
                across = keys_ref[other, :1, h * LANES : (h + 1) * LANES]
                same = jnp.where(down == across, 1.0, 0.0)
                count = count + same
                lane = other * per_row + h * LANES
                equal_ref[at, lane : lane + LANES] = same.astype(jnp.bfloat16)
        weight_ref[at, :] = jnp.broadcast_to(1.0 / jnp.sum(count, axis=1, keepdims=True), (per_row, LANES))


def fill_pick(keys_ref, pick_ref):
    rows, _, per_row = keys_ref.shape
    wanted = pick_ref.shape[0]
    step_rows = 128
    start = lax.axis_index("row") * wanted

    @pl.loop(0, wanted // step_rows)
    def _(step):
        down = lax.broadcasted_iota(jnp.int32, (step_rows, LANES), 0) + (start + step * step_rows)
        down = down.astype(jnp.float32)
        at = pl.ds(pl.multiple_of(step * step_rows, step_rows), step_rows)
        for other in range(rows):
            for h in range(per_row // LANES):
                across = keys_ref[other, :1, h * LANES : (h + 1) * LANES]
                lane = other * per_row + h * LANES
                pick_ref[at, lane : lane + LANES] = jnp.where(down == across, 1.0, 0.0).astype(jnp.bfloat16)


def adjoint_kernel(first, keys_ref, tiles_ref, *refs):
    row_tiles, per_block = tiles_ref.shape[:2]
    shares = lax.axis_size("col")
    me = lax.axis_index("col")
    per_share = row_tiles // shares
    terms = row_tiles * per_block * RHS
    if first:
        payloads, (term_ref, lower_ref) = refs[:shares], refs[shares:]
        rows = payloads[1].shape[0]
        squares, sources = [], []
        for d in range(shares):
            owner = jnp.bitwise_xor(me, d)
            if d % 2:
                squares.append(read_squares(payloads[d][:16, 2 * LANES :]))
                sources.append((owner, payloads[d][:, : 2 * LANES]))
            else:
                squares.append(payloads[d][per_share])
                sources.append((owner, packed([payloads[d][b] for b in range(per_share)], rows)))
    else:
        halves, (term_ref,) = refs[:2], refs[2:]
        rows = (halves[0].shape[0] - 16) // (shares // 2)
        squares = [read_squares(half[-16:, :LANES]) for half in halves]
        sources = [
            (2 * slot + jnp.bitwise_xor(me % 2, h), half[slot * rows : (slot + 1) * rows])
            for h, half in enumerate(halves)
            for slot in range(shares // 2)
        ]
    squares = tree_sum(squares)
    low = low_half(2 * LANES)
    pieces = jnp.concatenate(in_two(squares), axis=1)
    extra = jnp.zeros_like(pieces)
    if first:
        keys = keys_ref[...]
        coarse = jnp.floor(keys * (1.0 / 64))
        extra = jnp.where(low, coarse, keys - 64 * coarse)
    term_ref[terms:] = jnp.concatenate([pieces, extra], axis=0).astype(jnp.bfloat16)
    for owner, rays in sources:
        for g in range(per_share // 2):
            i = owner * per_share + 2 * g
            wide = [
                jnp.dot(rays, tiles_ref[i + e, k], preferred_element_type=jnp.float32)[8 * g : 8 * g + 8]
                for e in range(2)
                for k in range(2)
            ]
            value = jnp.concatenate(
                [
                    jnp.where(low, wide[0], pltpu.roll(wide[1], 4, 0)),
                    jnp.where(low, pltpu.roll(wide[2], 4, 0), wide[3]),
                ],
                axis=0,
            )
            at = pl.multiple_of(8 * i, 16)
            upper = value.astype(jnp.bfloat16)
            term_ref[pl.ds(at, 16), :] = upper
            if first:
                lower_ref[pl.ds(at, 16), :] = (value - upper.astype(jnp.float32)).astype(jnp.bfloat16)


def voxel_kernel(first, rows, tiles_ref, *refs):
    terms, refs = refs[:rows], list(refs[rows:])
    if first:
        own_ref, other_ref, beta_ref, raw_ref, all_ref, equal_ref, weight_ref, keys_ref = refs
    else:
        equal_ref, weight_ref, right_ref, alpha_ref = refs[:4]
        out_ref, beta_ref, raw_ref, all_ref = refs[-4:]
    my_row = lax.axis_index("row")
    row_tiles, per_block = tiles_ref.shape[:2]
    shares = lax.axis_size("col")
    per_share = row_tiles // shares
    per_row = row_tiles * per_block * RHS
    low = low_half(2 * LANES)
    squares = []
    for d in range(rows):
        slot = jnp.bitwise_xor(my_row, d)
        at = pl.ds(pl.multiple_of(slot * per_row, per_row), per_row)
        all_ref[at, :] = terms[d][:per_row]
        extra = terms[d][per_row:].astype(jnp.float32)
        squares.append(extra[:8, :LANES] + extra[:8, LANES:])
        if first:
            pieces = jnp.where(low, extra[8:] * 64, extra[8:])
            keys_ref[slot] = pieces + pltpu.roll(pieces, 4, 0)
    if first:
        fill_equal(keys_ref, equal_ref, weight_ref)
    beta = norm_of(tree_sum(squares))
    beta_ref[...] = beta
    wide_scale = jnp.concatenate([1.0 / beta] * 2, axis=1)
    if not first:
        wide_right = jnp.concatenate([beta / alpha_ref[...]] * 2, axis=1)
    acc = jnp.zeros((8, LANES), jnp.float32)
    for s in range(rows):
        same = equal_ref[s * per_row : (s + 1) * per_row, :]
        summed = jnp.dot(same, all_ref[...], preferred_element_type=jnp.float32)
        for m in range(per_row // 8):
            at = s * per_row + 8 * m
            raw = summed[8 * m : 8 * m + 8] * wide_scale
            if not first:
                raw = raw - right_ref[at : at + 8] * wide_right
            raw_ref[at : at + 8] = raw
            square = raw * raw
            acc = acc + (square[:, :LANES] + square[:, LANES:]) * weight_ref[at : at + 8]
    own = my_row * per_row
    core = lax.axis_index("col") % 2
    for e in range(shares):
        if first:
            half, slot = divmod(e, shares // 2)
            c = 2 * slot + jnp.bitwise_xor(core, half)
            ref, at = (own_ref, other_ref)[half], slot * per_share
        else:
            c, ref, at = e, out_ref.at[e], 0
        for g in range(per_share // 2):
            i = c * per_share + 2 * g
            lhs = raw_ref[pl.ds(pl.multiple_of(own + 8 * i, 16), 16), :].astype(jnp.bfloat16)
            wide = [
                lax.dot_general(
                    lhs, tiles_ref[i + e, k], (((1,), (1,)), ((), ())), preferred_element_type=jnp.float32
                )[8 * e : 8 * e + 8]
                for e in range(2)
                for k in range(2)
            ]
            value = jnp.where(low, wide[0], wide[3]) + pltpu.roll(jnp.where(low, wide[2], wide[1]), 4, 0)
            ref[at + 2 * g] = value[:, :LANES]
            ref[at + 2 * g + 1] = value[:, LANES:]
        if not first:
            ref[per_share] = acc
    if first:
        own_ref[own_ref.shape[0] - 1] = acc
        other_ref[own_ref.shape[0] - 1] = acc


def pair_kernel(own_ref, other_ref, out_ref):
    out_ref[...] = own_ref[...] + other_ref[...]


def half_ray_kernel(peers, *refs):
    parts, lefts = refs[:peers], refs[peers : 2 * peers]
    beta_ref, raw_ref, alpha_ref, half_ref = refs[2 * peers :]
    per_share = raw_ref.shape[0]
    rows = (half_ref.shape[0] - 16) // peers
    alpha = norm_of(tree_sum([p[p.shape[0] - 1] for p in parts]))
    alpha_ref[...] = alpha
    alpha_inv = 1.0 / alpha
    left_scale = alpha / beta_ref[...]
    squares = []
    for e in range(peers):
        slot = jnp.bitwise_xor(lax.axis_index("col") // 2, e)
        blocks = []
        for b in range(per_share):
            total = tree_sum([p[slot * per_share + b] for p in parts])
            blocks.append(total * alpha_inv - lefts[e][b] * left_scale)
            if e == 0:
                raw_ref[b] = blocks[-1]
        half_ref[pl.ds(pl.multiple_of(slot * rows, 16), rows), :] = packed(blocks, rows)
        squares.append(tree_sum([b * b for b in blocks]))
    pieces = packed_squares(tree_sum(squares))
    half_ref[peers * rows :, :LANES] = pieces
    half_ref[peers * rows :, LANES:] = jnp.zeros_like(pieces)


def share_kernel(remainders, *refs):
    pick_ref, all_ref = refs[1:3]
    lower_terms, out_ref = refs[3 : 3 + remainders], refs[3 + remainders]
    values = [all_ref]
    if remainders:
        held = refs[-1]
        per_row = lower_terms[0].shape[0]
        for d, term in enumerate(lower_terms):
            slot = jnp.bitwise_xor(lax.axis_index("row"), d)
            held[pl.ds(pl.multiple_of(slot * per_row, per_row), per_row), :] = term[...]
        values.append(held)
    step = 128
    for at in range(0, out_ref.shape[0], step):
        pick = pick_ref[at : at + step, :]
        out_ref[at : at + step, :] = tree_sum(
            [jnp.dot(pick, v[...], preferred_element_type=jnp.float32) for v in values]
        )


def pick_kernel(unread_ref, keys_ref, pick_ref):
    fill_pick(keys_ref, pick_ref)


def ray_kernel(part_ref, left_ref, beta_ref, lower_ref, raw_ref, alpha_ref, acc_ref, passed_ref):
    passed_ref[...] = lower_ref[...]
    shares, count = part_ref.shape[0], raw_ref.shape[0]
    alpha = norm_of(tree_sum([part_ref[c, count] for c in range(shares)]))
    alpha_ref[...] = alpha
    alpha_inv = 1.0 / alpha
    left_scale = alpha / beta_ref[...]
    blocks = []
    for b in range(count):
        total = tree_sum([part_ref[c, b] for c in range(shares)])
        blocks.append(total * alpha_inv - left_ref[b] * left_scale)
        raw_ref[b] = blocks[-1]
    acc = tree_sum([b * b for b in blocks])
    for c in range(acc_ref.shape[0]):
        acc_ref[c] = acc


def final_kernel(iters, last_ref, *refs):
    refs = list(refs)
    betas = [refs.pop(0) for _ in range(iters)]
    alphas = [refs.pop(0) for _ in range(iters)]
    products = [refs.pop(0) for _ in range(iters)]
    out_ref, ratio_ref = refs
    beta = [b[...] for b in betas] + [norm_of(tree_sum([last_ref[r] for r in range(last_ref.shape[0])]))]
    alpha = [a[...] for a in alphas]
    phibar, rhobar = beta[0], alpha[0]
    direction = [1.0 / alpha[0]] + [jnp.zeros_like(phibar)] * (iters - 1)
    weights = [jnp.zeros_like(phibar)] * iters
    for i in range(iters):
        rho = jnp.sqrt(rhobar * rhobar + beta[i + 1] * beta[i + 1])
        cosine, sine = rhobar / rho, beta[i + 1] / rho
        phi = cosine * phibar
        phibar = sine * phibar
        weights = [w + (phi / rho) * d for w, d in zip(weights, direction)]
        if i + 1 < iters:
            theta = sine * alpha[i + 1]
            rhobar = -cosine * alpha[i + 1]
            direction = [-(theta / rho) * d for d in direction]
            direction[i + 1] = direction[i + 1] + 1.0 / alpha[i + 1]
    ratio = phibar / beta[0]
    for n in range(RHS):
        ratio_ref[n] = jnp.max(ratio[n : n + 1])
    scales = []
    carried = jnp.zeros_like(phibar)
    for i in reversed(range(iters)):
        carried = weights[i] - carried
        scales.insert(0, jnp.concatenate([carried / beta[i]] * 2, axis=1))
        if i > 0:
            carried = carried * (beta[i] / alpha[i - 1])
    unroll = 4

    @pl.loop(0, products[0].shape[0] // (8 * unroll))
    def _(step):
        for u in range(unroll):
            m = step * unroll + u
            at = pl.ds(pl.multiple_of(m * 8, 8), 8)
            both = tree_sum([p[at, :] * s for p, s in zip(products, scales)])
            lane = pl.multiple_of(m * 4 * LANES, 4 * LANES)
            out_ref[:, pl.ds(lane, 2 * LANES)] = both[:4]
            out_ref[:, pl.ds(lane + 2 * LANES, 2 * LANES)] = both[4:]


def f32(*shape):
    return jax.ShapeDtypeStruct(shape, jnp.float32)


def bf16(*shape):
    return jax.ShapeDtypeStruct(shape, jnp.bfloat16)


def from_peer(value, axis, d):
    return lax.ppermute(value, axis, [(i, i ^ d) for i in range(lax.axis_size(axis))])


def exchange(value, axis, step=1):
    return [value] + [from_peer(value, axis, d) for d in range(step, lax.axis_size(axis), step)]


def swap(values, axis):
    return lax.all_to_all(values, axis, 0, 0)


def local(observed, tile_values, tile_cols):
    row_tiles, per_block, tile_size = tile_values.shape[:3]
    rows, shares = lax.axis_size("row"), lax.axis_size("col")
    col_tiles = N // (tile_size * shares)
    per_share = row_tiles // shares
    per_row = row_tiles * per_block * RHS
    share_rows = col_tiles // rows * RHS
    payload = bf16(max(16, 4 * per_share), 3 * LANES)
    half_shares = shares // 2
    half_parts = f32(half_shares * per_share + 1, 8, LANES)
    def call(kernel, name, out_shape, args, in_specs=None, scratch=()):
        return pl.pallas_call(
            kernel,
            out_shape=out_shape,
            in_specs=in_specs or [VMEM] * len(args),
            out_specs=jax.tree.map(lambda _: VMEM, out_shape),
            scratch_shapes=list(scratch),
            compiler_params=PARAMS,
            name=name,
        )(*args)

    def pack(left, unread):
        flat = left.ndim == 2
        message, blocks = call(
            functools.partial(pack_kernel, flat),
            "pack",
            [payload, f32(per_share + 1, 8, LANES)],
            [left, unread],
            [VMEM, HBM],
        )
        gathered = [blocks]
        for d in range(1, shares):
            gathered.append(from_peer(message if d % 2 else blocks, "col", d))
        return message, gathered

    def adjoint(payloads, first):
        out_shape = [bf16(per_row + 16, tile_size)] + [bf16(per_row, tile_size)] * first
        args = [keys, tile_values, *payloads]
        return call(functools.partial(adjoint_kernel, first), "adjoint", out_shape, args)

    def voxel(term_list, previous):
        first = not previous
        out_shape = [half_parts] * 2 if first else [f32(shares, per_share + 1, 8, LANES)]
        out_shape += [f32(8, LANES), f32(rows * per_row, tile_size), bf16(rows * per_row, tile_size)]
        if first:
            out_shape += [
                bf16(rows * per_row, rows * per_row),
                f32(rows * per_row, LANES),
                f32(rows, 8, per_row),
            ]
        args = [tile_values, *term_list, *previous]
        return call(functools.partial(voxel_kernel, first, rows), "voxel", out_shape, args)

    def half_ray(parts, lefts, beta):
        out_shape = [f32(per_share, 8, LANES), f32(8, LANES), bf16(half_shares * payload.shape[0] + 16, 2 * LANES)]
        kernel = functools.partial(half_ray_kernel, half_shares)
        return call(kernel, "half_ray", out_shape, [*parts, *lefts, beta])

    def share(selector, all_terms, lower_terms):
        scratch = [pltpu.VMEM((rows * per_row, tile_size), jnp.bfloat16)] * (len(lower_terms) > 0)
        kernel = functools.partial(share_kernel, len(lower_terms))
        args = [squares, selector, all_terms, *lower_terms]
        specs = [ANY] + [VMEM] * (len(args) - 1)
        return call(kernel, "share", f32(share_rows, tile_size), args, specs, scratch)

    def ray(parts, left_raw, beta, passed):
        out_shape = [f32(per_share, 8, LANES), f32(8, LANES), f32(rows * shares, 8, LANES), bf16(per_row, tile_size)]
        return call(ray_kernel, "ray", out_shape, [parts, left_raw, beta, passed])

    far = pltpu.with_memory_space_constraint(tile_values, pltpu.HBM)
    message, gathered = pack(observed, far)
    keys = call(keys_kernel, "keys", f32(8, per_row), [message, tile_cols.T], [ANY, SMEM])
    terms, remainder = adjoint(gathered, True)
    own, other, beta0, right_raw0, combined0, equal, weight, all_keys = voxel(exchange(terms, "row"), [])
    pair = call(pair_kernel, "pair", half_parts, [own, from_peer(other, "col", 1)])
    left_raw, alpha0, half = half_ray(exchange(pair, "col", 2), gathered[::2], beta0)
    (terms,) = adjoint([half, from_peer(half, "col", 1)], False)
    selector = call(pick_kernel, "pick", bf16(share_rows, rows * per_row), [terms, all_keys], [ANY, VMEM])
    parts, beta1, right_raw1, combined1 = voxel(exchange(terms, "row"), [equal, weight, right_raw0, alpha0])
    left_raw, alpha1, squares, remainder = ray(swap(parts, "col"), left_raw, beta1, remainder)
    terms, _ = adjoint(pack(left_raw, far)[1], True)
    voxel(exchange(terms, "row"), [equal, weight, right_raw1, alpha1])
    products = [share(selector, combined0, exchange(remainder, "row")), share(selector, combined1, [])]
    betas, alphas = [beta0, beta1], [alpha0, alpha1]
    result, ratio = pl.pallas_call(
        functools.partial(final_kernel, ITERS),
        out_shape=[f32(RHS, col_tiles // rows * tile_size), f32(RHS)],
        in_specs=[VMEM] * (1 + 3 * ITERS),
        out_specs=[VMEM, SMEM],
        compiler_params=PARAMS,
        name="final",
    )(swap(squares, ("row", "col")), *betas, *alphas, *products)
    return result, ratio


def solution(mesh):
    in_specs = (P(None, ("row", "col")), P("row", "col", None, None), P("row", "col"))
    out_specs = (P(None, ("col", "row")), P())
    return jax.shard_map(local, mesh=mesh, in_specs=in_specs, out_specs=out_specs, check_vma=False)
```

```python
import functools

import jax
import jax.numpy as jnp
from jax import lax
from jax.experimental import pallas as pl
from jax.experimental.pallas import tpu as pltpu
from jax.sharding import PartitionSpec as P

ITERS = 2
N = 1048576
epsilon_sq = 1e-06
LANES = 128
RHS = 4
VMEM = pl.BlockSpec(memory_space=pltpu.VMEM)
SMEM = pl.BlockSpec(memory_space=pltpu.SMEM)
HBM = pl.BlockSpec(memory_space=pltpu.HBM)
ANY = pl.BlockSpec(memory_space=pl.ANY)
PARAMS = pltpu.CompilerParams(vmem_limit_bytes=32 * 1024 * 1024)


def tree_sum(parts):
    while len(parts) > 1:
        paired = [parts[i] + parts[i + 1] for i in range(0, len(parts) - 1, 2)]
        parts = paired + parts[2 * len(paired) :]
    return parts[0]


def norm_of(acc):
    rows = jnp.broadcast_to(jnp.sum(acc, axis=1, keepdims=True), acc.shape)
    return jnp.sqrt(rows + pltpu.roll(rows, 4, 0) + epsilon_sq)


def low_half(width):
    return lax.broadcasted_iota(jnp.int32, (8, width), 0) < 4


def in_two(acc):
    upper = acc.astype(jnp.bfloat16).astype(jnp.float32)
    return upper, acc - upper


def packed(blocks, rows):
    blank = [jnp.zeros((8, LANES), jnp.float32)] * (rows // 8)
    halves = [jnp.concatenate((blocks[h::2] + blank)[: rows // 8], axis=0) for h in range(2)]
    return jnp.concatenate(halves, axis=1).astype(jnp.bfloat16)


def packed_squares(acc):
    return jnp.concatenate(in_two(acc), axis=0).astype(jnp.bfloat16)


def read_squares(both):
    both = both.astype(jnp.float32)
    return both[:8] + both[8:16]


def ray_blocks(obs_ref, count):
    obs = obs_ref[...]
    blocks = []
    for b in range(count):
        at = (b // 2) * 4 * LANES + (b % 2) * LANES
        blocks.append(jnp.concatenate([obs[:, at : at + LANES], obs[:, at + 2 * LANES : at + 3 * LANES]], axis=0))
    return blocks


def pack_kernel(obs_ref, unread_ref, blocks_ref):
    count = blocks_ref.shape[0] - 1
    blocks = ray_blocks(obs_ref, count)
    for b, block in enumerate(blocks):
        blocks_ref[b] = block
    blocks_ref[count] = tree_sum([b * b for b in blocks])


def join_kernel(own_ref, other_ref, both_ref):
    count = own_ref.shape[0] - 1
    both_ref[:count] = own_ref[:count]
    both_ref[count : 2 * count] = other_ref[:count]
    both_ref[2 * count] = own_ref[count] + other_ref[count]


def keys_kernel(unread_ref, cols_ref, keys_ref):
    keys_ref[...] = key_row(cols_ref)


def key_row(cols_ref):
    per_block, row_tiles = cols_ref.shape
    width = per_block * row_tiles * RHS
    lane = lax.broadcasted_iota(jnp.int32, (8, width), 1)
    keys = jnp.zeros((8, width), jnp.int32)
    for i in range(row_tiles):
        for k in range(per_block):
            keys = jnp.where(lane // RHS == i * per_block + k, cols_ref[k, i], keys)
    return (keys * RHS + lane % RHS).astype(jnp.float32)


def fill_equal(keys_ref, equal_ref, weight_ref):
    rows, _, per_row = keys_ref.shape

    @pl.loop(0, rows)
    def _(s):
        down = jnp.broadcast_to(keys_ref[s][:1], (LANES, per_row)).T
        at = pl.ds(pl.multiple_of(s * per_row, per_row), per_row)
        count = jnp.zeros((per_row, LANES), jnp.float32)
        for other in range(rows):
            for h in range(per_row // LANES):
                across = keys_ref[other, :1, h * LANES : (h + 1) * LANES]
                same = jnp.where(down == across, 1.0, 0.0)
                count = count + same
                lane = other * per_row + h * LANES
                equal_ref[at, lane : lane + LANES] = same.astype(jnp.bfloat16)
        weight_ref[at, :] = jnp.broadcast_to(1.0 / jnp.sum(count, axis=1, keepdims=True), (per_row, LANES))


def fill_pick(keys_ref, pick_ref):
    rows, _, per_row = keys_ref.shape
    wanted = pick_ref.shape[0]
    step_rows = 128
    start = lax.axis_index("row") * wanted

    @pl.loop(0, wanted // step_rows)
    def _(step):
        down = lax.broadcasted_iota(jnp.int32, (step_rows, LANES), 0) + (start + step * step_rows)
        down = down.astype(jnp.float32)
        at = pl.ds(pl.multiple_of(step * step_rows, step_rows), step_rows)
        for other in range(rows):
            for h in range(per_row // LANES):
                across = keys_ref[other, :1, h * LANES : (h + 1) * LANES]
                lane = other * per_row + h * LANES
                pick_ref[at, lane : lane + LANES] = jnp.where(down == across, 1.0, 0.0).astype(jnp.bfloat16)


def adjoint_kernel(first, keys_ref, tiles_ref, *refs):
    row_tiles, per_block = tiles_ref.shape[:2]
    shares = lax.axis_size("col")
    me = lax.axis_index("col")
    per_share = row_tiles // shares
    terms = row_tiles * per_block * RHS
    if first:
        pairs, (term_ref, lower_ref) = refs[: shares // 2], refs[shares // 2 :]
        squares, sources = [], []
        for e, pair in enumerate(pairs):
            squares.append(pair[2 * per_share])
            for h in range(2):
                blocks = [pair[h * per_share + b] for b in range(per_share)]
                owner = jnp.bitwise_xor(me, 2 * e + h)
                sources.append((owner, packed(blocks, max(16, 4 * per_share))))
    else:
        halves, (term_ref,) = refs[:2], refs[2:]
        rows = (halves[0].shape[0] - 16) // (shares // 2)
        squares = [read_squares(half[-16:, :LANES]) for half in halves]
        sources = [
            (2 * slot + jnp.bitwise_xor(me % 2, h), half[slot * rows : (slot + 1) * rows])
            for h, half in enumerate(halves)
            for slot in range(shares // 2)
        ]
    squares = tree_sum(squares)
    low = low_half(2 * LANES)
    pieces = jnp.concatenate(in_two(squares), axis=1)
    extra = jnp.zeros_like(pieces)
    if first:
        keys = keys_ref[...]
        coarse = jnp.floor(keys * (1.0 / 64))
        extra = jnp.where(low, coarse, keys - 64 * coarse)
    term_ref[terms:] = jnp.concatenate([pieces, extra], axis=0).astype(jnp.bfloat16)
    for owner, rays in sources:
        for g in range(per_share // 2):
            i = owner * per_share + 2 * g
            wide = [
                jnp.dot(rays, tiles_ref[i + e, k], preferred_element_type=jnp.float32)[8 * g : 8 * g + 8]
                for e in range(2)
                for k in range(2)
            ]
            value = jnp.concatenate(
                [
                    jnp.where(low, wide[0], pltpu.roll(wide[1], 4, 0)),
                    jnp.where(low, pltpu.roll(wide[2], 4, 0), wide[3]),
                ],
                axis=0,
            )
            at = pl.multiple_of(8 * i, 16)
            upper = value.astype(jnp.bfloat16)
            term_ref[pl.ds(at, 16), :] = upper
            if first:
                lower_ref[pl.ds(at, 16), :] = (value - upper.astype(jnp.float32)).astype(jnp.bfloat16)


def voxel_kernel(first, rows, tiles_ref, *refs):
    terms, refs = refs[:rows], list(refs[rows:])
    if first:
        own_ref, other_ref, beta_ref, raw_ref, all_ref, equal_ref, weight_ref, keys_ref = refs
    else:
        equal_ref, weight_ref, right_ref, alpha_ref = refs[:4]
        own_ref, other_ref, beta_ref, raw_ref, all_ref = refs[-5:]
    my_row = lax.axis_index("row")
    row_tiles, per_block = tiles_ref.shape[:2]
    shares = lax.axis_size("col")
    per_share = row_tiles // shares
    per_row = row_tiles * per_block * RHS
    low = low_half(2 * LANES)
    squares = []
    for d in range(rows):
        slot = jnp.bitwise_xor(my_row, d)
        at = pl.ds(pl.multiple_of(slot * per_row, per_row), per_row)
        all_ref[at, :] = terms[d][:per_row]
        extra = terms[d][per_row:].astype(jnp.float32)
        squares.append(extra[:8, :LANES] + extra[:8, LANES:])
        if first:
            pieces = jnp.where(low, extra[8:] * 64, extra[8:])
            keys_ref[slot] = pieces + pltpu.roll(pieces, 4, 0)
    if first:
        fill_equal(keys_ref, equal_ref, weight_ref)
    beta = norm_of(tree_sum(squares))
    beta_ref[...] = beta
    wide_scale = jnp.concatenate([1.0 / beta] * 2, axis=1)
    if not first:
        wide_right = jnp.concatenate([beta / alpha_ref[...]] * 2, axis=1)
    acc = jnp.zeros((8, LANES), jnp.float32)
    for s in range(rows):
        same = equal_ref[s * per_row : (s + 1) * per_row, :]
        summed = jnp.dot(same, all_ref[...], preferred_element_type=jnp.float32)
        for m in range(per_row // 8):
            at = s * per_row + 8 * m
            raw = summed[8 * m : 8 * m + 8] * wide_scale
            if not first:
                raw = raw - right_ref[at : at + 8] * wide_right
            raw_ref[at : at + 8] = raw
            square = raw * raw
            acc = acc + (square[:, :LANES] + square[:, LANES:]) * weight_ref[at : at + 8]
    own = my_row * per_row
    core = lax.axis_index("col") % 2
    for half, slot in [(h, s) for h in range(2) for s in range(shares // 2)]:
        c = 2 * slot + jnp.bitwise_xor(core, half)
        ref, at = (own_ref, other_ref)[half], slot * per_share
        for g in range(per_share // 2):
            i = c * per_share + 2 * g
            lhs = raw_ref[pl.ds(pl.multiple_of(own + 8 * i, 16), 16), :].astype(jnp.bfloat16)
            wide = [
                lax.dot_general(
                    lhs, tiles_ref[i + e, k], (((1,), (1,)), ((), ())), preferred_element_type=jnp.float32
                )[8 * e : 8 * e + 8]
                for e in range(2)
                for k in range(2)
            ]
            value = jnp.where(low, wide[0], wide[3]) + pltpu.roll(jnp.where(low, wide[2], wide[1]), 4, 0)
            ref[at + 2 * g] = value[:, :LANES]
            ref[at + 2 * g + 1] = value[:, LANES:]
    own_ref[own_ref.shape[0] - 1] = acc
    other_ref[own_ref.shape[0] - 1] = acc


def pair_kernel(*refs):
    passed = (len(refs) - 3) // 2
    refs[2 + passed][...] = refs[0][...] + refs[1][...]
    for i in range(passed):
        refs[3 + passed + i][...] = refs[2 + i][...]


def half_ray_kernel(peers, first, unread, *refs):
    refs = refs[unread:]
    parts, refs = refs[:peers], refs[peers:]
    lefts, (beta_ref, raw_ref, alpha_ref, half_ref, acc_ref) = refs[:-5], refs[-5:]
    per_share = raw_ref.shape[0] // peers
    rows = (half_ref.shape[0] - 16) // peers
    alpha = norm_of(tree_sum([p[p.shape[0] - 1] for p in parts]))
    alpha_ref[...] = alpha
    alpha_inv = 1.0 / alpha
    left_scale = alpha / beta_ref[...]
    squares = []
    for e in range(peers):
        slot = jnp.bitwise_xor(lax.axis_index("col") // 2, e)
        blocks = []
        for b in range(per_share):
            at = slot * per_share + b
            left = lefts[e][b] if first else lefts[0][at]
            blocks.append(tree_sum([p[at] for p in parts]) * alpha_inv - left * left_scale)
            raw_ref[at] = blocks[-1]
        half_ref[pl.ds(pl.multiple_of(slot * rows, 16), rows), :] = packed(blocks, rows)
        squares.append(tree_sum([b * b for b in blocks]))
    acc = tree_sum(squares)
    acc_ref[...] = acc
    pieces = packed_squares(acc)
    half_ref[peers * rows :, :LANES] = pieces
    half_ref[peers * rows :, LANES:] = jnp.zeros_like(pieces)


def share_kernel(remainders, *refs):
    pick_ref, all_ref = refs[:2]
    lower_terms, out_ref = refs[2 : 2 + remainders], refs[2 + remainders]
    values = [all_ref]
    if remainders:
        held = refs[-1]
        per_row = lower_terms[0].shape[0]
        for d, term in enumerate(lower_terms):
            slot = jnp.bitwise_xor(lax.axis_index("row"), d)
            held[pl.ds(pl.multiple_of(slot * per_row, per_row), per_row), :] = term[...]
        values.append(held)
    step = 128
    for at in range(0, out_ref.shape[0], step):
        pick = pick_ref[at : at + step, :]
        out_ref[at : at + step, :] = tree_sum(
            [jnp.dot(pick, v[...], preferred_element_type=jnp.float32) for v in values]
        )


def pick_kernel(unread_ref, keys_ref, pick_ref):
    fill_pick(keys_ref, pick_ref)


def final_kernel(rows, iters, *refs):
    refs = list(refs)
    last = [refs.pop(0) for _ in range(rows)]
    betas = [refs.pop(0) for _ in range(iters)]
    alphas = [refs.pop(0) for _ in range(iters)]
    products = [refs.pop(0) for _ in range(iters)]
    out_ref, ratio_ref = refs
    beta = [b[...] for b in betas] + [norm_of(tree_sum([p[...] for p in last]))]
    alpha = [a[...] for a in alphas]
    phibar, rhobar = beta[0], alpha[0]
    direction = [1.0 / alpha[0]] + [jnp.zeros_like(phibar)] * (iters - 1)
    weights = [jnp.zeros_like(phibar)] * iters
    for i in range(iters):
        rho = jnp.sqrt(rhobar * rhobar + beta[i + 1] * beta[i + 1])
        cosine, sine = rhobar / rho, beta[i + 1] / rho
        phi = cosine * phibar
        phibar = sine * phibar
        weights = [w + (phi / rho) * d for w, d in zip(weights, direction)]
        if i + 1 < iters:
            theta = sine * alpha[i + 1]
            rhobar = -cosine * alpha[i + 1]
            direction = [-(theta / rho) * d for d in direction]
            direction[i + 1] = direction[i + 1] + 1.0 / alpha[i + 1]
    ratio = phibar / beta[0]
    for n in range(RHS):
        ratio_ref[n] = jnp.max(ratio[n : n + 1])
    scales = []
    carried = jnp.zeros_like(phibar)
    for i in reversed(range(iters)):
        carried = weights[i] - carried
        scales.insert(0, jnp.concatenate([carried / beta[i]] * 2, axis=1))
        if i > 0:
            carried = carried * (beta[i] / alpha[i - 1])
    unroll = 4

    @pl.loop(0, products[0].shape[0] // (8 * unroll))
    def _(step):
        for u in range(unroll):
            m = step * unroll + u
            at = pl.ds(pl.multiple_of(m * 8, 8), 8)
            both = tree_sum([p[at, :] * s for p, s in zip(products, scales)])
            lane = pl.multiple_of(m * 4 * LANES, 4 * LANES)
            out_ref[:, pl.ds(lane, 2 * LANES)] = both[:4]
            out_ref[:, pl.ds(lane + 2 * LANES, 2 * LANES)] = both[4:]


def f32(*shape):
    return jax.ShapeDtypeStruct(shape, jnp.float32)


def bf16(*shape):
    return jax.ShapeDtypeStruct(shape, jnp.bfloat16)


def from_peer(value, axis, d):
    return lax.ppermute(value, axis, [(i, i ^ d) for i in range(lax.axis_size(axis))])


def exchange(value, axis, step=1):
    return [value] + [from_peer(value, axis, d) for d in range(step, lax.axis_size(axis), step)]


def local(observed, tile_values, tile_cols):
    row_tiles, per_block, tile_size = tile_values.shape[:3]
    rows, shares = lax.axis_size("row"), lax.axis_size("col")
    col_tiles = N // (tile_size * shares)
    per_share = row_tiles // shares
    per_row = row_tiles * per_block * RHS
    share_rows = col_tiles // rows * RHS
    ray_rows = max(16, RHS * per_share)
    half_shares = shares // 2
    half_blocks = half_shares * per_share
    def call(kernel, name, out_shape, args, in_specs=None, scratch=()):
        return pl.pallas_call(
            kernel,
            out_shape=out_shape,
            in_specs=in_specs or [VMEM] * len(args),
            out_specs=jax.tree.map(lambda _: VMEM, out_shape),
            scratch_shapes=list(scratch),
            compiler_params=PARAMS,
            name=name,
        )(*args)

    def adjoint(payloads, first):
        out_shape = [bf16(per_row + 16, tile_size)] + [bf16(per_row, tile_size)] * first
        args = [keys, tile_values, *payloads]
        return call(functools.partial(adjoint_kernel, first), "adjoint", out_shape, args)

    def voxel(term_list, previous):
        first = not previous
        out_shape = [f32(half_blocks + 1, 8, LANES)] * 2
        out_shape += [f32(8, LANES), f32(rows * per_row, tile_size), bf16(rows * per_row, tile_size)]
        if first:
            out_shape += [
                bf16(rows * per_row, rows * per_row),
                f32(rows * per_row, LANES),
                f32(rows, 8, per_row),
            ]
        args = [tile_values, *term_list, *previous]
        return call(functools.partial(voxel_kernel, first, rows), "voxel", out_shape, args)

    def pair(own, other, passed):
        args = [own, from_peer(other, "col", 1), *passed]
        out_shape = [jax.ShapeDtypeStruct(x.shape, x.dtype) for x in [own, *passed]]
        return call(pair_kernel, "pair", out_shape, args)

    def half_ray(parts, lefts, beta, after):
        out_shape = [
            f32(half_blocks, 8, LANES),
            f32(8, LANES),
            bf16(half_shares * ray_rows + 16, 2 * LANES),
            f32(8, LANES),
        ]
        kernel = functools.partial(half_ray_kernel, half_shares, len(lefts) > 1, len(after))
        args = [*after, *parts, *lefts, beta]
        specs = [ANY] * len(after) + [VMEM] * (len(args) - len(after))
        return call(kernel, "half_ray", out_shape, args, specs)

    def share(selector, all_terms, lower_terms):
        scratch = [pltpu.VMEM((rows * per_row, tile_size), jnp.bfloat16)] * (len(lower_terms) > 0)
        kernel = functools.partial(share_kernel, len(lower_terms))
        args = [selector, all_terms, *lower_terms]
        return call(kernel, "share", f32(share_rows, tile_size), args, None, scratch)

    far = pltpu.with_memory_space_constraint(tile_values, pltpu.HBM)
    blocks = call(pack_kernel, "pack", f32(per_share + 1, 8, LANES), [observed, far], [VMEM, HBM])
    keys = call(keys_kernel, "keys", f32(8, per_row), [blocks, tile_cols.T], [ANY, SMEM])
    both = call(join_kernel, "join", f32(2 * per_share + 1, 8, LANES), [blocks, from_peer(blocks, "col", 1)])
    lefts = exchange(both, "col", 2)
    terms, remainder = adjoint(lefts, True)
    own, other, beta, right_raw, upper_terms, equal, weight, all_keys = voxel(exchange(terms, "row"), [])
    betas, alphas, combined = [], [], []
    for iteration in range(ITERS):
        last = iteration == ITERS - 1
        betas.append(beta)
        combined.append(upper_terms)
        summed, *passed = pair(own, other, [remainder] * last)
        remainders = exchange(passed[0], "row") if last else []
        left_raw, alpha, half, squares = half_ray(exchange(summed, "col", 2), lefts, beta, remainders)
        alphas.append(alpha)
        lefts = [left_raw]
        (terms,) = adjoint([half, from_peer(half, "col", 1)], False)
        if iteration == 0:
            selector = call(pick_kernel, "pick", bf16(share_rows, rows * per_row), [terms, all_keys], [ANY, VMEM])
        own, other, beta, right_raw, upper_terms = voxel(
            exchange(terms, "row"), [equal, weight, right_raw, alpha]
        )
    products = [share(selector, c, [] if i else remainders) for i, c in enumerate(combined)]
    (squares,) = call(pair_kernel, "pair", [f32(8, LANES)], [squares, from_peer(squares, "col", 1)])
    result, ratio = pl.pallas_call(
        functools.partial(final_kernel, rows, ITERS),
        out_shape=[f32(RHS, col_tiles // rows * tile_size), f32(RHS)],
        in_specs=[VMEM] * (rows + 3 * ITERS),
        out_specs=[VMEM, SMEM],
        compiler_params=PARAMS,
        name="final",
    )(*exchange(squares, "row"), *betas, *alphas, *products)
    return result, ratio


def solution(mesh):
    in_specs = (P(None, ("row", "col")), P("row", "col", None, None), P("row", "col"))
    out_specs = (P(None, ("col", "row")), P())
    return jax.shard_map(local, mesh=mesh, in_specs=in_specs, out_specs=out_specs, check_vma=False)
```

```python
import functools

import jax
import jax.numpy as jnp
from jax import lax
from jax.experimental import pallas as pl
from jax.experimental.pallas import tpu as pltpu
from jax.sharding import PartitionSpec as P

ITERS = 2
N = 1048576
epsilon_sq = 1e-06
LANES = 128
RHS = 4
VMEM = pl.BlockSpec(memory_space=pltpu.VMEM)
SMEM = pl.BlockSpec(memory_space=pltpu.SMEM)
HBM = pl.BlockSpec(memory_space=pltpu.HBM)
ANY = pl.BlockSpec(memory_space=pl.ANY)
PARAMS = pltpu.CompilerParams(vmem_limit_bytes=32 * 1024 * 1024)


def tree_sum(parts):
    while len(parts) > 1:
        paired = [parts[i] + parts[i + 1] for i in range(0, len(parts) - 1, 2)]
        parts = paired + parts[2 * len(paired) :]
    return parts[0]


def norm_of(acc):
    rows = jnp.broadcast_to(jnp.sum(acc, axis=1, keepdims=True), acc.shape)
    return jnp.sqrt(rows + pltpu.roll(rows, 4, 0) + epsilon_sq)


def low_half(width):
    return lax.broadcasted_iota(jnp.int32, (8, width), 0) < 4


def in_two(acc):
    upper = acc.astype(jnp.bfloat16).astype(jnp.float32)
    return upper, acc - upper


def packed(blocks, rows):
    blank = [jnp.zeros((8, LANES), jnp.float32)] * (rows // 8)
    halves = [jnp.concatenate((blocks[h::2] + blank)[: rows // 8], axis=0) for h in range(2)]
    return jnp.concatenate(halves, axis=1).astype(jnp.bfloat16)


def packed_squares(acc):
    return jnp.concatenate(in_two(acc), axis=0).astype(jnp.bfloat16)


def read_squares(both):
    both = both.astype(jnp.float32)
    return both[:8] + both[8:16]


def ray_blocks(obs_ref, count):
    obs = obs_ref[...]
    blocks = []
    for b in range(count):
        at = (b // 2) * 4 * LANES + (b % 2) * LANES
        blocks.append(jnp.concatenate([obs[:, at : at + LANES], obs[:, at + 2 * LANES : at + 3 * LANES]], axis=0))
    return blocks


def pack_kernel(obs_ref, unread_ref, blocks_ref):
    count = blocks_ref.shape[0] - 1
    blocks = ray_blocks(obs_ref, count)
    for b, block in enumerate(blocks):
        blocks_ref[b] = block
    blocks_ref[count] = tree_sum([b * b for b in blocks])


def join_kernel(own_ref, other_ref, both_ref):
    count = own_ref.shape[0] - 1
    both_ref[:count] = own_ref[:count]
    both_ref[count : 2 * count] = other_ref[:count]
    both_ref[2 * count] = own_ref[count] + other_ref[count]


def keys_kernel(unread_ref, cols_ref, keys_ref):
    keys_ref[...] = key_row(cols_ref)


def key_row(cols_ref):
    per_block, row_tiles = cols_ref.shape
    width = per_block * row_tiles * RHS
    lane = lax.broadcasted_iota(jnp.int32, (8, width), 1)
    keys = jnp.zeros((8, width), jnp.int32)
    for i in range(row_tiles):
        for k in range(per_block):
            keys = jnp.where(lane // RHS == i * per_block + k, cols_ref[k, i], keys)
    return (keys * RHS + lane % RHS).astype(jnp.float32)


def fill_equal(keys_ref, equal_ref, weight_ref):
    rows, _, per_row = keys_ref.shape

    @pl.loop(0, rows)
    def _(s):
        down = jnp.broadcast_to(keys_ref[s][:1], (LANES, per_row)).T
        at = pl.ds(pl.multiple_of(s * per_row, per_row), per_row)
        count = jnp.zeros((per_row, LANES), jnp.float32)
        for other in range(rows):
            for h in range(per_row // LANES):
                across = keys_ref[other, :1, h * LANES : (h + 1) * LANES]
                same = jnp.where(down == across, 1.0, 0.0)
                count = count + same
                lane = other * per_row + h * LANES
                equal_ref[at, lane : lane + LANES] = same.astype(jnp.bfloat16)
        weight_ref[at, :] = jnp.broadcast_to(1.0 / jnp.sum(count, axis=1, keepdims=True), (per_row, LANES))


def fill_pick(keys_ref, pick_ref):
    rows, _, per_row = keys_ref.shape
    wanted = pick_ref.shape[0]
    step_rows = 128
    start = lax.axis_index("row") * wanted

    @pl.loop(0, wanted // step_rows)
    def _(step):
        down = lax.broadcasted_iota(jnp.int32, (step_rows, LANES), 0) + (start + step * step_rows)
        down = down.astype(jnp.float32)
        at = pl.ds(pl.multiple_of(step * step_rows, step_rows), step_rows)
        for other in range(rows):
            for h in range(per_row // LANES):
                across = keys_ref[other, :1, h * LANES : (h + 1) * LANES]
                lane = other * per_row + h * LANES
                pick_ref[at, lane : lane + LANES] = jnp.where(down == across, 1.0, 0.0).astype(jnp.bfloat16)


def adjoint_kernel(first, keys_ref, tiles_ref, *refs):
    row_tiles, per_block = tiles_ref.shape[:2]
    shares = lax.axis_size("col")
    me = lax.axis_index("col")
    per_share = row_tiles // shares
    terms = row_tiles * per_block * RHS
    if first:
        pairs, (term_ref, lower_ref) = refs[: shares // 2], refs[shares // 2 :]
        squares, sources = [], []
        for e, pair in enumerate(pairs):
            squares.append(pair[2 * per_share])
            for h in range(2):
                blocks = [pair[h * per_share + b] for b in range(per_share)]
                owner = jnp.bitwise_xor(me, 2 * e + h)
                sources.append((owner, packed(blocks, max(16, 4 * per_share))))
    else:
        halves, (term_ref,) = refs[:2], refs[2:]
        rows = (halves[0].shape[0] - 16) // (shares // 2)
        squares = [read_squares(half[-16:, :LANES]) for half in halves]
        sources = [
            (2 * slot + jnp.bitwise_xor(me % 2, h), half[slot * rows : (slot + 1) * rows])
            for h, half in enumerate(halves)
            for slot in range(shares // 2)
        ]
    squares = tree_sum(squares)
    low = low_half(2 * LANES)
    pieces = jnp.concatenate(in_two(squares), axis=1)
    extra = jnp.zeros_like(pieces)
    if first:
        keys = keys_ref[...]
        coarse = jnp.floor(keys * (1.0 / 64))
        extra = jnp.where(low, coarse, keys - 64 * coarse)
    term_ref[terms:] = jnp.concatenate([pieces, extra], axis=0).astype(jnp.bfloat16)
    for owner, rays in sources:
        for g in range(per_share // 2):
            i = owner * per_share + 2 * g
            wide = [
                jnp.dot(rays, tiles_ref[i + e, k], preferred_element_type=jnp.float32)[8 * g : 8 * g + 8]
                for e in range(2)
                for k in range(2)
            ]
            value = jnp.concatenate(
                [
                    jnp.where(low, wide[0], pltpu.roll(wide[1], 4, 0)),
                    jnp.where(low, pltpu.roll(wide[2], 4, 0), wide[3]),
                ],
                axis=0,
            )
            at = pl.multiple_of(8 * i, 16)
            upper = value.astype(jnp.bfloat16)
            term_ref[pl.ds(at, 16), :] = upper
            if first:
                lower_ref[pl.ds(at, 16), :] = (value - upper.astype(jnp.float32)).astype(jnp.bfloat16)


def voxel_kernel(first, rows, tiles_ref, *refs):
    terms, refs = refs[:rows], list(refs[rows:])
    if first:
        own_ref, other_ref, beta_ref, all_ref, raw_ref, equal_ref, weight_ref, keys_ref = refs
    else:
        equal_ref, weight_ref, right_ref, alpha_ref = refs[:4]
        own_ref, other_ref, beta_ref, all_ref, raw_ref = refs[-5:]
    my_row = lax.axis_index("row")
    row_tiles, per_block = tiles_ref.shape[:2]
    shares = lax.axis_size("col")
    per_share = row_tiles // shares
    per_row = row_tiles * per_block * RHS
    low = low_half(2 * LANES)
    squares = []
    for d in range(rows):
        slot = jnp.bitwise_xor(my_row, d)
        at = pl.ds(pl.multiple_of(slot * per_row, per_row), per_row)
        all_ref[at, :] = terms[d][:per_row]
        extra = terms[d][per_row:].astype(jnp.float32)
        squares.append(extra[:8, :LANES] + extra[:8, LANES:])
        if first:
            pieces = jnp.where(low, extra[8:] * 64, extra[8:])
            keys_ref[slot] = pieces + pltpu.roll(pieces, 4, 0)
    if first:
        fill_equal(keys_ref, equal_ref, weight_ref)
    beta = norm_of(tree_sum(squares))
    beta_ref[...] = beta
    wide_scale = jnp.concatenate([1.0 / beta] * 2, axis=1)
    if not first:
        wide_right = jnp.concatenate([beta / alpha_ref[...]] * 2, axis=1)
    acc = jnp.zeros((8, LANES), jnp.float32)
    for s in range(rows):
        same = equal_ref[s * per_row : (s + 1) * per_row, :]
        summed = jnp.dot(same, all_ref[...], preferred_element_type=jnp.float32)
        for m in range(per_row // 8):
            at = s * per_row + 8 * m
            raw = summed[8 * m : 8 * m + 8] * wide_scale
            if not first:
                raw = raw - right_ref[at : at + 8] * wide_right
            raw_ref[at : at + 8] = raw
            square = raw * raw
            acc = acc + (square[:, :LANES] + square[:, LANES:]) * weight_ref[at : at + 8]
    own = my_row * per_row
    core = lax.axis_index("col") % 2
    for half, slot in [(h, s) for h in range(2) for s in range(shares // 2)]:
        c = 2 * slot + jnp.bitwise_xor(core, half)
        ref, at = (own_ref, other_ref)[half], slot * per_share
        for g in range(per_share // 2):
            i = c * per_share + 2 * g
            lhs = raw_ref[pl.ds(pl.multiple_of(own + 8 * i, 16), 16), :].astype(jnp.bfloat16)
            wide = [
                lax.dot_general(
                    lhs, tiles_ref[i + e, k], (((1,), (1,)), ((), ())), preferred_element_type=jnp.float32
                )[8 * e : 8 * e + 8]
                for e in range(2)
                for k in range(2)
            ]
            value = jnp.where(low, wide[0], wide[3]) + pltpu.roll(jnp.where(low, wide[2], wide[1]), 4, 0)
            ref[at + 2 * g] = value[:, :LANES]
            ref[at + 2 * g + 1] = value[:, LANES:]
    own_ref[own_ref.shape[0] - 1] = acc
    other_ref[own_ref.shape[0] - 1] = acc


def pair_kernel(narrow, own_ref, other_ref, *refs):
    passed = len(refs) // 2
    out_ref = refs[passed]
    for i in range(passed):
        refs[1 + passed + i][...] = refs[i][...]
    if not narrow:
        out_ref[...] = own_ref[...] + other_ref[...]
        return
    count = own_ref.shape[0] - 1
    for b in range(0, count, 2):
        two = [own_ref[b + i] + other_ref[b + i] for i in range(2)]
        out_ref[8 * b : 8 * b + 16, :] = jnp.concatenate(two, axis=0).astype(jnp.bfloat16)
    out_ref[8 * count :, :] = packed_squares(own_ref[count] + other_ref[count])


def half_ray_kernel(peers, first, narrow, update, unread, *refs):
    refs = refs[unread:]
    parts, refs = refs[:peers], refs[peers:]
    if update:
        lefts, (beta_ref, alpha_ref, raw_ref, half_ref) = refs[:-4], refs[-4:]
        rows = (half_ref.shape[0] - 16) // peers
    else:
        lefts, (beta_ref, alpha_ref, acc_ref) = refs[:-3], refs[-3:]
    if narrow:
        count = (parts[0].shape[0] - 16) // 8
        squares = [read_squares(p[8 * count :, :]) for p in parts]
    else:
        count = parts[0].shape[0] - 1
        squares = [p[count] for p in parts]
    per_share = count // peers
    alpha = norm_of(tree_sum(squares))
    alpha_ref[...] = alpha
    alpha_inv = 1.0 / alpha
    left_scale = alpha / beta_ref[...]
    squares = []
    for e in range(peers):
        slot = jnp.bitwise_xor(lax.axis_index("col") // 2, e)
        if narrow:
            at = pl.ds(pl.multiple_of(slot * per_share * 8, 16), per_share * 8)
            whole = tree_sum([p[at, :].astype(jnp.float32) for p in parts])
            totals = [whole[8 * b : 8 * b + 8] for b in range(per_share)]
        else:
            totals = [tree_sum([p[slot * per_share + b] for p in parts]) for b in range(per_share)]
        blocks = []
        for b in range(per_share):
            at = slot * per_share + b
            left = lefts[e][b] if first else lefts[0][at]
            blocks.append(totals[b] * alpha_inv - left * left_scale)
            if update:
                raw_ref[at] = blocks[-1]
        if update:
            half_ref[pl.ds(pl.multiple_of(slot * rows, 16), rows), :] = packed(blocks, rows)
        squares.append(tree_sum([b * b for b in blocks]))
    acc = tree_sum(squares)
    if update:
        pieces = packed_squares(acc)
        half_ref[peers * rows :, :LANES] = pieces
        half_ref[peers * rows :, LANES:] = jnp.zeros_like(pieces)
    else:
        acc_ref[...] = acc


def share_kernel(remainders, *refs):
    pick_ref, all_ref = refs[:2]
    lower_terms, out_ref = refs[2 : 2 + remainders], refs[2 + remainders]
    values = [all_ref]
    if remainders:
        held = refs[-1]
        per_row = lower_terms[0].shape[0]
        for d, term in enumerate(lower_terms):
            slot = jnp.bitwise_xor(lax.axis_index("row"), d)
            held[pl.ds(pl.multiple_of(slot * per_row, per_row), per_row), :] = term[...]
        values.append(held)
    step = 128
    for at in range(0, out_ref.shape[0], step):
        pick = pick_ref[at : at + step, :]
        out_ref[at : at + step, :] = tree_sum(
            [jnp.dot(pick, v[...], preferred_element_type=jnp.float32) for v in values]
        )


def pick_kernel(unread_ref, keys_ref, pick_ref):
    fill_pick(keys_ref, pick_ref)


def final_kernel(rows, iters, *refs):
    refs = list(refs)
    last = [refs.pop(0) for _ in range(rows)]
    betas = [refs.pop(0) for _ in range(iters)]
    alphas = [refs.pop(0) for _ in range(iters)]
    products = [refs.pop(0) for _ in range(iters)]
    out_ref, ratio_ref = refs
    beta = [b[...] for b in betas] + [norm_of(tree_sum([p[...] for p in last]))]
    alpha = [a[...] for a in alphas]
    phibar, rhobar = beta[0], alpha[0]
    direction = [1.0 / alpha[0]] + [jnp.zeros_like(phibar)] * (iters - 1)
    weights = [jnp.zeros_like(phibar)] * iters
    for i in range(iters):
        rho = jnp.sqrt(rhobar * rhobar + beta[i + 1] * beta[i + 1])
        cosine, sine = rhobar / rho, beta[i + 1] / rho
        phi = cosine * phibar
        phibar = sine * phibar
        weights = [w + (phi / rho) * d for w, d in zip(weights, direction)]
        if i + 1 < iters:
            theta = sine * alpha[i + 1]
            rhobar = -cosine * alpha[i + 1]
            direction = [-(theta / rho) * d for d in direction]
            direction[i + 1] = direction[i + 1] + 1.0 / alpha[i + 1]
    ratio = phibar / beta[0]
    for n in range(RHS):
        ratio_ref[n] = jnp.max(ratio[n : n + 1])
    scales = []
    carried = jnp.zeros_like(phibar)
    for i in reversed(range(iters)):
        carried = weights[i] - carried
        scales.insert(0, jnp.concatenate([carried / beta[i]] * 2, axis=1))
        if i > 0:
            carried = carried * (beta[i] / alpha[i - 1])
    unroll = 4

    @pl.loop(0, products[0].shape[0] // (8 * unroll))
    def _(step):
        for u in range(unroll):
            m = step * unroll + u
            at = pl.ds(pl.multiple_of(m * 8, 8), 8)
            both = tree_sum([p[at, :] * s for p, s in zip(products, scales)])
            lane = pl.multiple_of(m * 4 * LANES, 4 * LANES)
            out_ref[:, pl.ds(lane, 2 * LANES)] = both[:4]
            out_ref[:, pl.ds(lane + 2 * LANES, 2 * LANES)] = both[4:]


def f32(*shape):
    return jax.ShapeDtypeStruct(shape, jnp.float32)


def bf16(*shape):
    return jax.ShapeDtypeStruct(shape, jnp.bfloat16)


def from_peer(value, axis, d):
    return lax.ppermute(value, axis, [(i, i ^ d) for i in range(lax.axis_size(axis))])


def exchange(value, axis, step=1):
    return [value] + [from_peer(value, axis, d) for d in range(step, lax.axis_size(axis), step)]


def local(observed, tile_values, tile_cols):
    row_tiles, per_block, tile_size = tile_values.shape[:3]
    rows, shares = lax.axis_size("row"), lax.axis_size("col")
    col_tiles = N // (tile_size * shares)
    per_share = row_tiles // shares
    per_row = row_tiles * per_block * RHS
    share_rows = col_tiles // rows * RHS
    ray_rows = max(16, RHS * per_share)
    half_shares = shares // 2
    half_blocks = half_shares * per_share
    def call(kernel, name, out_shape, args, in_specs=None, scratch=()):
        return pl.pallas_call(
            kernel,
            out_shape=out_shape,
            in_specs=in_specs or [VMEM] * len(args),
            out_specs=jax.tree.map(lambda _: VMEM, out_shape),
            scratch_shapes=list(scratch),
            compiler_params=PARAMS,
            name=name,
        )(*args)

    def adjoint(payloads, first):
        out_shape = [bf16(per_row + 16, tile_size)] + [bf16(per_row, tile_size)] * first
        args = [keys, tile_values, *payloads]
        return call(functools.partial(adjoint_kernel, first), "adjoint", out_shape, args)

    def voxel(term_list, previous, keep):
        first = not previous
        out_shape = [f32(half_blocks + 1, 8, LANES)] * 2 + [f32(8, LANES), bf16(rows * per_row, tile_size)]
        raw_shape = (rows * per_row, tile_size)
        out_shape += [f32(*raw_shape)] * keep
        if first:
            out_shape += [
                bf16(rows * per_row, rows * per_row),
                f32(rows * per_row, LANES),
                f32(rows, 8, per_row),
            ]
        args = [tile_values, *term_list, *previous]
        scratch = [pltpu.VMEM(raw_shape, jnp.float32)] * (not keep)
        return call(functools.partial(voxel_kernel, first, rows), "voxel", out_shape, args, None, scratch)

    def pair(own, other, passed, narrow):
        args = [own, from_peer(other, "col", 1), *passed]
        out_shape = [jax.ShapeDtypeStruct(x.shape, x.dtype) for x in [own, *passed]]
        if narrow:
            out_shape[0] = bf16(8 * half_blocks + 16, LANES)
        return call(functools.partial(pair_kernel, narrow), "pair", out_shape, args)

    def half_ray(parts, lefts, beta, after, narrow, update):
        out_shape = [f32(8, LANES)]
        if update:
            out_shape += [f32(half_blocks, 8, LANES), bf16(half_shares * ray_rows + 16, 2 * LANES)]
        else:
            out_shape += [f32(8, LANES)]
        kernel = functools.partial(half_ray_kernel, half_shares, len(lefts) > 1, narrow, update, len(after))
        args = [*after, *parts, *lefts, beta]
        specs = [ANY] * len(after) + [VMEM] * (len(args) - len(after))
        return call(kernel, "half_ray", out_shape, args, specs)

    def share(selector, all_terms, lower_terms):
        scratch = [pltpu.VMEM((rows * per_row, tile_size), jnp.bfloat16)] * (len(lower_terms) > 0)
        kernel = functools.partial(share_kernel, len(lower_terms))
        args = [selector, all_terms, *lower_terms]
        return call(kernel, "share", f32(share_rows, tile_size), args, None, scratch)

    far = pltpu.with_memory_space_constraint(tile_values, pltpu.HBM)
    blocks = call(pack_kernel, "pack", f32(per_share + 1, 8, LANES), [observed, far], [VMEM, HBM])
    keys = call(keys_kernel, "keys", f32(8, per_row), [blocks, tile_cols.T], [ANY, SMEM])
    both = call(join_kernel, "join", f32(2 * per_share + 1, 8, LANES), [blocks, from_peer(blocks, "col", 1)])
    lefts = exchange(both, "col", 2)
    terms, remainder = adjoint(lefts, True)
    terms = exchange(terms, "row")
    own, other, beta, upper_terms, right_raw, equal, weight, all_keys = voxel(terms, [], True)
    betas, alphas, combined = [], [], []
    remainders = [None] * rows
    for iteration in range(ITERS):
        last = iteration == ITERS - 1
        betas.append(beta)
        combined.append(upper_terms)
        crossing = range(1, rows // 2 + 1) if iteration == 0 else range(rows // 2 + 1, rows) if last else []
        summed, *passed = pair(own, other, [remainder] * (len(crossing) > 0), last)
        for d in crossing:
            remainders[d] = from_peer(passed[0], "row", d)
        after = [remainders[d] for d in crossing]
        gathered = exchange(summed, "col", 2)
        if last:
            alpha, squares = half_ray(gathered, lefts, beta, after, True, False)
        alpha, left_raw, half = half_ray(gathered, lefts, beta, after, last, True) if not last else (
            alpha,
            *half_ray(gathered, lefts, beta, after, True, True)[1:],
        )
        alphas.append(alpha)
        lefts = [left_raw]
        (new_terms,) = adjoint([half, from_peer(half, "col", 1)], False)
        if iteration == 0:
            selector = call(pick_kernel, "pick", bf16(share_rows, rows * per_row), [new_terms, all_keys], [ANY, VMEM])
        new_terms = exchange(new_terms, "row")
        fixed = [equal, weight, right_raw, alpha]
        own, other, beta, upper_terms = voxel(new_terms, fixed, False)
        right_raw = voxel(new_terms, fixed, True)[4]
    remainders[0] = remainder
    products = [share(selector, c, [] if i else remainders) for i, c in enumerate(combined)]
    (squares,) = call(functools.partial(pair_kernel, False), "pair", [f32(8, LANES)], [squares, from_peer(squares, "col", 1)])
    result, ratio = pl.pallas_call(
        functools.partial(final_kernel, rows, ITERS),
        out_shape=[f32(RHS, col_tiles // rows * tile_size), f32(RHS)],
        in_specs=[VMEM] * (rows + 3 * ITERS),
        out_specs=[VMEM, SMEM],
        compiler_params=PARAMS,
        name="final",
    )(*exchange(squares, "row"), *betas, *alphas, *products)
    return result, ratio


def solution(mesh):
    in_specs = (P(None, ("row", "col")), P("row", "col", None, None), P("row", "col"))
    out_specs = (P(None, ("col", "row")), P())
    return jax.shard_map(local, mesh=mesh, in_specs=in_specs, out_specs=out_specs, check_vma=False)
```

```python
import functools

import jax
import jax.numpy as jnp
from jax import lax
from jax.experimental import pallas as pl
from jax.experimental.pallas import tpu as pltpu
from jax.sharding import PartitionSpec as P

ITERS = 2
N = 1048576
epsilon_sq = 1e-06
LANES = 128
RHS = 4
VMEM = pl.BlockSpec(memory_space=pltpu.VMEM)
SMEM = pl.BlockSpec(memory_space=pltpu.SMEM)
HBM = pl.BlockSpec(memory_space=pltpu.HBM)
ANY = pl.BlockSpec(memory_space=pl.ANY)
PARAMS = pltpu.CompilerParams(vmem_limit_bytes=32 * 1024 * 1024)


def tree_sum(parts):
    while len(parts) > 1:
        paired = [parts[i] + parts[i + 1] for i in range(0, len(parts) - 1, 2)]
        parts = paired + parts[2 * len(paired) :]
    return parts[0]


def norm_of(acc):
    rows = jnp.broadcast_to(jnp.sum(acc, axis=1, keepdims=True), acc.shape)
    return jnp.sqrt(rows + pltpu.roll(rows, 4, 0) + epsilon_sq)


def low_half(width):
    return lax.broadcasted_iota(jnp.int32, (8, width), 0) < 4


def in_two(acc):
    upper = acc.astype(jnp.bfloat16).astype(jnp.float32)
    return upper, acc - upper


def packed(blocks, rows):
    blank = [jnp.zeros((8, LANES), jnp.float32)] * (rows // 8)
    halves = [jnp.concatenate((blocks[h::2] + blank)[: rows // 8], axis=0) for h in range(2)]
    return jnp.concatenate(halves, axis=1).astype(jnp.bfloat16)


def packed_squares(acc):
    return jnp.concatenate(in_two(acc), axis=0).astype(jnp.bfloat16)


def read_squares(both):
    both = both.astype(jnp.float32)
    return both[:8] + both[8:16]


def ray_blocks(obs_ref, count):
    obs = obs_ref[...]
    blocks = []
    for b in range(count):
        at = (b // 2) * 4 * LANES + (b % 2) * LANES
        blocks.append(jnp.concatenate([obs[:, at : at + LANES], obs[:, at + 2 * LANES : at + 3 * LANES]], axis=0))
    return blocks


def pack_kernel(obs_ref, unread_ref, blocks_ref):
    count = blocks_ref.shape[0] - 1
    blocks = ray_blocks(obs_ref, count)
    for b, block in enumerate(blocks):
        blocks_ref[b] = block
    blocks_ref[count] = tree_sum([b * b for b in blocks])


def join_kernel(own_ref, other_ref, both_ref):
    count = own_ref.shape[0] - 1
    both_ref[:count] = own_ref[:count]
    both_ref[count : 2 * count] = other_ref[:count]
    both_ref[2 * count] = own_ref[count] + other_ref[count]


def keys_kernel(unread_ref, cols_ref, keys_ref):
    keys_ref[...] = key_row(cols_ref)


def key_row(cols_ref):
    per_block, row_tiles = cols_ref.shape
    width = per_block * row_tiles * RHS
    lane = lax.broadcasted_iota(jnp.int32, (8, width), 1)
    keys = jnp.zeros((8, width), jnp.int32)
    for i in range(row_tiles):
        for k in range(per_block):
            keys = jnp.where(lane // RHS == i * per_block + k, cols_ref[k, i], keys)
    return (keys * RHS + lane % RHS).astype(jnp.float32)


def fill_equal(keys_ref, equal_ref, weight_ref):
    rows, _, per_row = keys_ref.shape

    @pl.loop(0, rows)
    def _(s):
        down = jnp.broadcast_to(keys_ref[s][:1], (LANES, per_row)).T
        at = pl.ds(pl.multiple_of(s * per_row, per_row), per_row)
        count = jnp.zeros((per_row, LANES), jnp.float32)
        for other in range(rows):
            for h in range(per_row // LANES):
                across = keys_ref[other, :1, h * LANES : (h + 1) * LANES]
                same = jnp.where(down == across, 1.0, 0.0)
                count = count + same
                lane = other * per_row + h * LANES
                equal_ref[at, lane : lane + LANES] = same.astype(jnp.bfloat16)
        weight_ref[at, :] = jnp.broadcast_to(1.0 / jnp.sum(count, axis=1, keepdims=True), (per_row, LANES))


def fill_pick(keys_ref, pick_ref):
    rows, _, per_row = keys_ref.shape
    wanted = pick_ref.shape[0]
    step_rows = 128
    start = lax.axis_index("row") * wanted

    @pl.loop(0, wanted // step_rows)
    def _(step):
        down = lax.broadcasted_iota(jnp.int32, (step_rows, LANES), 0) + (start + step * step_rows)
        down = down.astype(jnp.float32)
        at = pl.ds(pl.multiple_of(step * step_rows, step_rows), step_rows)
        for other in range(rows):
            for h in range(per_row // LANES):
                across = keys_ref[other, :1, h * LANES : (h + 1) * LANES]
                lane = other * per_row + h * LANES
                pick_ref[at, lane : lane + LANES] = jnp.where(down == across, 1.0, 0.0).astype(jnp.bfloat16)


def adjoint_kernel(first, unread, keys_ref, tiles_ref, *refs):
    refs = refs[unread:]
    row_tiles, per_block = tiles_ref.shape[:2]
    shares = lax.axis_size("col")
    me = lax.axis_index("col")
    per_share = row_tiles // shares
    terms = row_tiles * per_block * RHS
    if first:
        pairs, (term_ref, lower_ref) = refs[: shares // 2], refs[shares // 2 :]
        squares, sources = [], []
        for e, pair in enumerate(pairs):
            squares.append(pair[2 * per_share])
            for h in range(2):
                blocks = [pair[h * per_share + b] for b in range(per_share)]
                owner = jnp.bitwise_xor(me, 2 * e + h)
                sources.append((owner, packed(blocks, max(16, 4 * per_share))))
    else:
        halves, (term_ref,) = refs[:2], refs[2:]
        rows = (halves[0].shape[0] - 16) // (shares // 2)
        squares = [read_squares(half[-16:, :LANES]) for half in halves]
        sources = [
            (2 * slot + jnp.bitwise_xor(me % 2, h), half[slot * rows : (slot + 1) * rows])
            for h, half in enumerate(halves)
            for slot in range(shares // 2)
        ]
    squares = tree_sum(squares)
    low = low_half(2 * LANES)
    pieces = jnp.concatenate(in_two(squares), axis=1)
    extra = jnp.zeros_like(pieces)
    if first:
        keys = keys_ref[...]
        coarse = jnp.floor(keys * (1.0 / 64))
        extra = jnp.where(low, coarse, keys - 64 * coarse)
    term_ref[terms:] = jnp.concatenate([pieces, extra], axis=0).astype(jnp.bfloat16)
    for owner, rays in sources:
        for g in range(per_share // 2):
            i = owner * per_share + 2 * g
            wide = [
                jnp.dot(rays, tiles_ref[i + e, k], preferred_element_type=jnp.float32)[8 * g : 8 * g + 8]
                for e in range(2)
                for k in range(2)
            ]
            value = jnp.concatenate(
                [
                    jnp.where(low, wide[0], pltpu.roll(wide[1], 4, 0)),
                    jnp.where(low, pltpu.roll(wide[2], 4, 0), wide[3]),
                ],
                axis=0,
            )
            at = pl.multiple_of(8 * i, 16)
            upper = value.astype(jnp.bfloat16)
            term_ref[pl.ds(at, 16), :] = upper
            if first:
                lower_ref[pl.ds(at, 16), :] = (value - upper.astype(jnp.float32)).astype(jnp.bfloat16)


def voxel_kernel(first, rows, tiles_ref, *refs):
    terms, refs = refs[:rows], list(refs[rows:])
    if first:
        lhs_ref, acc_ref, other_ref, beta_ref, all_ref, raw_ref, equal_ref, weight_ref, keys_ref = refs
    else:
        equal_ref, weight_ref, right_ref, alpha_ref = refs[:4]
        lhs_ref, acc_ref, other_ref, beta_ref, all_ref, raw_ref = refs[-6:]
    my_row = lax.axis_index("row")
    row_tiles, per_block = tiles_ref.shape[:2]
    per_row = row_tiles * per_block * RHS
    low = low_half(2 * LANES)
    squares = []
    for d in range(rows):
        slot = jnp.bitwise_xor(my_row, d)
        at = pl.ds(pl.multiple_of(slot * per_row, per_row), per_row)
        all_ref[at, :] = terms[d][:per_row]
        extra = terms[d][per_row:].astype(jnp.float32)
        squares.append(extra[:8, :LANES] + extra[:8, LANES:])
        if first:
            pieces = jnp.where(low, extra[8:] * 64, extra[8:])
            keys_ref[slot] = pieces + pltpu.roll(pieces, 4, 0)
    if first:
        fill_equal(keys_ref, equal_ref, weight_ref)
    beta = norm_of(tree_sum(squares))
    beta_ref[...] = beta
    wide_scale = jnp.concatenate([1.0 / beta] * 2, axis=1)
    if not first:
        wide_right = jnp.concatenate([beta / alpha_ref[...]] * 2, axis=1)
    acc = jnp.zeros((8, LANES), jnp.float32)
    for s in range(rows):
        same = equal_ref[s * per_row : (s + 1) * per_row, :]
        summed = jnp.dot(same, all_ref[...], preferred_element_type=jnp.float32)
        for m in range(per_row // 8):
            at = s * per_row + 8 * m
            raw = summed[8 * m : 8 * m + 8] * wide_scale
            if not first:
                raw = raw - right_ref[at : at + 8] * wide_right
            raw_ref[at : at + 8] = raw
            square = raw * raw
            acc = acc + (square[:, :LANES] + square[:, LANES:]) * weight_ref[at : at + 8]
    lhs_ref[...] = raw_ref[pl.ds(pl.multiple_of(my_row * per_row, 16), per_row), :].astype(jnp.bfloat16)
    forward_half(1, tiles_ref, lhs_ref, other_ref)
    other_ref[other_ref.shape[0] - 1] = acc
    acc_ref[...] = acc


def forward_half(half, tiles_ref, lhs_ref, out_ref):
    shares = lax.axis_size("col")
    per_share = tiles_ref.shape[0] // shares
    low = low_half(2 * LANES)
    core = lax.axis_index("col") % 2
    for slot in range(shares // 2):
        c = 2 * slot + jnp.bitwise_xor(core, half)
        for g in range(per_share // 2):
            i = c * per_share + 2 * g
            lhs = lhs_ref[pl.ds(pl.multiple_of(8 * i, 16), 16), :]
            wide = [
                lax.dot_general(
                    lhs, tiles_ref[i + e, k], (((1,), (1,)), ((), ())), preferred_element_type=jnp.float32
                )[8 * e : 8 * e + 8]
                for e in range(2)
                for k in range(2)
            ]
            value = jnp.where(low, wide[0], wide[3]) + pltpu.roll(jnp.where(low, wide[2], wide[1]), 4, 0)
            at = slot * per_share + 2 * g
            out_ref[at] = value[:, :LANES]
            out_ref[at + 1] = value[:, LANES:]


def forward_kernel(tiles_ref, lhs_ref, acc_ref, own_ref):
    forward_half(0, tiles_ref, lhs_ref, own_ref)
    own_ref[own_ref.shape[0] - 1] = acc_ref[...]


def pair_kernel(narrow, own_ref, other_ref, *refs):
    passed = len(refs) // 2
    out_ref = refs[passed]
    for i in range(passed):
        refs[1 + passed + i][...] = refs[i][...]
    if not narrow:
        out_ref[...] = own_ref[...] + other_ref[...]
        return
    count = own_ref.shape[0] - 1
    for b in range(0, count, 2):
        two = [own_ref[b + i] + other_ref[b + i] for i in range(2)]
        out_ref[8 * b : 8 * b + 16, :] = jnp.concatenate(two, axis=0).astype(jnp.bfloat16)
    out_ref[8 * count :, :] = packed_squares(own_ref[count] + other_ref[count])


def sum_kernel(*refs):
    refs[-1][...] = refs[-3][...] + refs[-2][...]


def half_ray_kernel(peers, first, narrow, update, unread, *refs):
    refs = refs[unread:]
    parts, refs = refs[:peers], refs[peers:]
    if update:
        lefts, (beta_ref, alpha_ref, raw_ref, half_ref) = refs[:-4], refs[-4:]
        rows = (half_ref.shape[0] - 16) // peers
    else:
        lefts, (beta_ref, alpha_ref, acc_ref) = refs[:-3], refs[-3:]
    if narrow:
        count = (parts[0].shape[0] - 16) // 8
        squares = [read_squares(p[8 * count :, :]) for p in parts]
    else:
        count = parts[0].shape[0] - 1
        squares = [p[count] for p in parts]
    per_share = count // peers
    alpha = norm_of(tree_sum(squares))
    alpha_ref[...] = alpha
    alpha_inv = 1.0 / alpha
    left_scale = alpha / beta_ref[...]
    squares = []
    for e in range(peers):
        slot = jnp.bitwise_xor(lax.axis_index("col") // 2, e)
        if narrow:
            at = pl.ds(pl.multiple_of(slot * per_share * 8, 16), per_share * 8)
            whole = tree_sum([p[at, :].astype(jnp.float32) for p in parts])
            totals = [whole[8 * b : 8 * b + 8] for b in range(per_share)]
        else:
            totals = [tree_sum([p[slot * per_share + b] for p in parts]) for b in range(per_share)]
        blocks = []
        for b in range(per_share):
            at = slot * per_share + b
            left = lefts[e][b] if first else lefts[0][at]
            blocks.append(totals[b] * alpha_inv - left * left_scale)
            if update:
                raw_ref[at] = blocks[-1]
        if update:
            half_ref[pl.ds(pl.multiple_of(slot * rows, 16), rows), :] = packed(blocks, rows)
        squares.append(tree_sum([b * b for b in blocks]))
    acc = tree_sum(squares)
    if update:
        pieces = packed_squares(acc)
        half_ref[peers * rows :, :LANES] = pieces
        half_ref[peers * rows :, LANES:] = jnp.zeros_like(pieces)
    else:
        acc_ref[...] = acc


def share_kernel(remainders, *refs):
    pick_ref, all_ref = refs[:2]
    lower_terms, out_ref = refs[2 : 2 + remainders], refs[2 + remainders]
    values = [all_ref]
    if remainders:
        held = refs[-1]
        per_row = lower_terms[0].shape[0]
        for d, term in enumerate(lower_terms):
            slot = jnp.bitwise_xor(lax.axis_index("row"), d)
            held[pl.ds(pl.multiple_of(slot * per_row, per_row), per_row), :] = term[...]
        values.append(held)
    step = 128
    for at in range(0, out_ref.shape[0], step):
        pick = pick_ref[at : at + step, :]
        out_ref[at : at + step, :] = tree_sum(
            [jnp.dot(pick, v[...], preferred_element_type=jnp.float32) for v in values]
        )


def pick_kernel(unread_ref, keys_ref, pick_ref):
    fill_pick(keys_ref, pick_ref)


def final_kernel(rows, iters, *refs):
    refs = list(refs)
    last = [refs.pop(0) for _ in range(rows)]
    betas = [refs.pop(0) for _ in range(iters)]
    alphas = [refs.pop(0) for _ in range(iters)]
    products = [refs.pop(0) for _ in range(iters)]
    out_ref, ratio_ref = refs
    beta = [b[...] for b in betas] + [norm_of(tree_sum([p[...] for p in last]))]
    alpha = [a[...] for a in alphas]
    phibar, rhobar = beta[0], alpha[0]
    direction = [1.0 / alpha[0]] + [jnp.zeros_like(phibar)] * (iters - 1)
    weights = [jnp.zeros_like(phibar)] * iters
    for i in range(iters):
        rho = jnp.sqrt(rhobar * rhobar + beta[i + 1] * beta[i + 1])
        cosine, sine = rhobar / rho, beta[i + 1] / rho
        phi = cosine * phibar
        phibar = sine * phibar
        weights = [w + (phi / rho) * d for w, d in zip(weights, direction)]
        if i + 1 < iters:
            theta = sine * alpha[i + 1]
            rhobar = -cosine * alpha[i + 1]
            direction = [-(theta / rho) * d for d in direction]
            direction[i + 1] = direction[i + 1] + 1.0 / alpha[i + 1]
    ratio = phibar / beta[0]
    for n in range(RHS):
        ratio_ref[n] = jnp.max(ratio[n : n + 1])
    scales = []
    carried = jnp.zeros_like(phibar)
    for i in reversed(range(iters)):
        carried = weights[i] - carried
        scales.insert(0, jnp.concatenate([carried / beta[i]] * 2, axis=1))
        if i > 0:
            carried = carried * (beta[i] / alpha[i - 1])
    unroll = 4

    @pl.loop(0, products[0].shape[0] // (8 * unroll))
    def _(step):
        for u in range(unroll):
            m = step * unroll + u
            at = pl.ds(pl.multiple_of(m * 8, 8), 8)
            both = tree_sum([p[at, :] * s for p, s in zip(products, scales)])
            lane = pl.multiple_of(m * 4 * LANES, 4 * LANES)
            out_ref[:, pl.ds(lane, 2 * LANES)] = both[:4]
            out_ref[:, pl.ds(lane + 2 * LANES, 2 * LANES)] = both[4:]


def f32(*shape):
    return jax.ShapeDtypeStruct(shape, jnp.float32)


def bf16(*shape):
    return jax.ShapeDtypeStruct(shape, jnp.bfloat16)


def from_peer(value, axis, d):
    return lax.ppermute(value, axis, [(i, i ^ d) for i in range(lax.axis_size(axis))])


def exchange(value, axis, step=1):
    return [value] + [from_peer(value, axis, d) for d in range(step, lax.axis_size(axis), step)]


def local(observed, tile_values, tile_cols):
    row_tiles, per_block, tile_size = tile_values.shape[:3]
    rows, shares = lax.axis_size("row"), lax.axis_size("col")
    col_tiles = N // (tile_size * shares)
    per_share = row_tiles // shares
    per_row = row_tiles * per_block * RHS
    share_rows = col_tiles // rows * RHS
    ray_rows = max(16, RHS * per_share)
    half_shares = shares // 2
    half_blocks = half_shares * per_share
    def call(kernel, name, out_shape, args, in_specs=None, scratch=(), flops=None):
        return pl.pallas_call(
            kernel,
            out_shape=out_shape,
            in_specs=in_specs or [VMEM] * len(args),
            out_specs=jax.tree.map(lambda _: VMEM, out_shape),
            scratch_shapes=list(scratch),
            compiler_params=PARAMS,
            cost_estimate=flops and pl.CostEstimate(flops=flops, bytes_accessed=0, transcendentals=0),
            name=name,
        )(*args)

    def adjoint(payloads, first, after):
        out_shape = [bf16(per_row + 16, tile_size)] + [bf16(per_row, tile_size)] * first
        args = [keys, tile_values, *after, *payloads]
        specs = [VMEM] * 2 + [ANY] * len(after) + [VMEM] * len(payloads)
        return call(functools.partial(adjoint_kernel, first, len(after)), "adjoint", out_shape, args, specs)

    def voxel(term_list, previous, keep):
        first = not previous
        out_shape = [bf16(per_row, tile_size), f32(8, LANES), f32(half_blocks + 1, 8, LANES)]
        out_shape += [f32(8, LANES), bf16(rows * per_row, tile_size)]
        raw_shape = (rows * per_row, tile_size)
        out_shape += [f32(*raw_shape)] * keep
        if first:
            out_shape += [
                bf16(rows * per_row, rows * per_row),
                f32(rows * per_row, LANES),
                f32(rows, 8, per_row),
            ]
        args = [tile_values, *term_list, *previous]
        scratch = [pltpu.VMEM(raw_shape, jnp.float32)] * (not keep)
        lhs, acc, other, *rest = call(
            functools.partial(voxel_kernel, first, rows), "voxel", out_shape, args, None, scratch
        )
        own = call(forward_kernel, "forward", f32(half_blocks + 1, 8, LANES), [tile_values, lhs, acc])
        return own, other, *rest

    def pair(own, other, passed, narrow):
        args = [own, from_peer(other, "col", 1), *passed]
        out_shape = [jax.ShapeDtypeStruct(x.shape, x.dtype) for x in [own, *passed]]
        if narrow:
            out_shape[0] = bf16(8 * half_blocks + 16, LANES)
        return call(functools.partial(pair_kernel, narrow), "pair", out_shape, args)

    def half_ray(parts, lefts, beta, after, narrow, update):
        out_shape = [f32(8, LANES)]
        if update:
            out_shape += [f32(half_blocks, 8, LANES), bf16(half_shares * ray_rows + 16, 2 * LANES)]
        else:
            out_shape += [f32(8, LANES)]
        kernel = functools.partial(half_ray_kernel, half_shares, len(lefts) > 1, narrow, update, len(after))
        args = [*after, *parts, *lefts, beta]
        specs = [ANY] * len(after) + [VMEM] * (len(args) - len(after))
        return call(kernel, "half_ray", out_shape, args, specs, (), 2 * 10**9)

    def share(selector, all_terms, lower_terms):
        scratch = [pltpu.VMEM((rows * per_row, tile_size), jnp.bfloat16)] * (len(lower_terms) > 0)
        kernel = functools.partial(share_kernel, len(lower_terms))
        args = [selector, all_terms, *lower_terms]
        return call(kernel, "share", f32(share_rows, tile_size), args, None, scratch)

    far = pltpu.with_memory_space_constraint(tile_values, pltpu.HBM)
    blocks = call(pack_kernel, "pack", f32(per_share + 1, 8, LANES), [observed, far], [VMEM, HBM])
    keys = call(keys_kernel, "keys", f32(8, per_row), [blocks, tile_cols.T], [ANY, SMEM])
    both = call(join_kernel, "join", f32(2 * per_share + 1, 8, LANES), [blocks, from_peer(blocks, "col", 1)])
    lefts = exchange(both, "col", 2)
    terms, remainder = adjoint(lefts, True, [])
    terms = exchange(terms, "row")
    own, other, beta, upper_terms, right_raw, equal, weight, all_keys = voxel(terms, [], True)
    betas, alphas, combined = [], [], []
    remainders = [None] * rows
    for iteration in range(ITERS):
        last = iteration == ITERS - 1
        betas.append(beta)
        combined.append(upper_terms)
        crossing = range(1, rows // 2 + 1) if iteration == 0 else range(rows // 2 + 1, rows) if last else []
        summed, *passed = pair(own, other, [remainder] * (len(crossing) > 0), last)
        gathered = exchange(summed, "col", 2)
        for d in crossing:
            remainders[d] = from_peer(passed[0], "row", d)
        after = [remainders[d] for d in crossing]
        if last:
            alpha, squares = half_ray(gathered, lefts, beta, [], True, False)
            _, left_raw, half = half_ray(gathered, lefts, beta, [], True, True)
        else:
            alpha, left_raw, half = half_ray(gathered, lefts, beta, [], False, True)
        alphas.append(alpha)
        lefts = [left_raw]
        (new_terms,) = adjoint([half, from_peer(half, "col", 1)], False, after)
        if iteration == 0:
            selector = call(pick_kernel, "pick", bf16(share_rows, rows * per_row), [new_terms, all_keys], [ANY, VMEM])
        new_terms = exchange(new_terms, "row")
        fixed = [equal, weight, right_raw, alpha]
        own, other, beta, upper_terms = voxel(new_terms, fixed, False)
        right_raw = voxel(new_terms, fixed, True)[4]
    remainders[0] = remainder
    products = [share(selector, c, [] if i else remainders) for i, c in enumerate(combined)]
    squares = call(
        sum_kernel, "sum", f32(8, LANES), [*after, squares, from_peer(squares, "col", 1)], [ANY] * len(after) + [VMEM] * 2
    )
    result, ratio = pl.pallas_call(
        functools.partial(final_kernel, rows, ITERS),
        out_shape=[f32(RHS, col_tiles // rows * tile_size), f32(RHS)],
        in_specs=[VMEM] * (rows + 3 * ITERS),
        out_specs=[VMEM, SMEM],
        compiler_params=PARAMS,
        name="final",
    )(*exchange(squares, "row"), *betas, *alphas, *products)
    return result, ratio


def solution(mesh):
    in_specs = (P(None, ("row", "col")), P("row", "col", None, None), P("row", "col"))
    out_specs = (P(None, ("col", "row")), P())
    return jax.shard_map(local, mesh=mesh, in_specs=in_specs, out_specs=out_specs, check_vma=False)
```

```python
import functools

import jax
import jax.numpy as jnp
from jax import lax
from jax.experimental import pallas as pl
from jax.experimental.pallas import tpu as pltpu
from jax.sharding import PartitionSpec as P

ITERS = 2
N = 1048576
epsilon_sq = 1e-06
LANES = 128
RHS = 4
VMEM = pl.BlockSpec(memory_space=pltpu.VMEM)
SMEM = pl.BlockSpec(memory_space=pltpu.SMEM)
HBM = pl.BlockSpec(memory_space=pltpu.HBM)
ANY = pl.BlockSpec(memory_space=pl.ANY)
PARAMS = pltpu.CompilerParams(vmem_limit_bytes=32 * 1024 * 1024)


def tree_sum(parts):
    while len(parts) > 1:
        paired = [parts[i] + parts[i + 1] for i in range(0, len(parts) - 1, 2)]
        parts = paired + parts[2 * len(paired) :]
    return parts[0]


def norm_of(acc):
    rows = jnp.broadcast_to(jnp.sum(acc, axis=1, keepdims=True), acc.shape)
    return jnp.sqrt(rows + pltpu.roll(rows, 4, 0) + epsilon_sq)


def low_half(width):
    return lax.broadcasted_iota(jnp.int32, (8, width), 0) < 4


def in_two(acc):
    upper = acc.astype(jnp.bfloat16).astype(jnp.float32)
    return upper, acc - upper


def packed(blocks, rows):
    blank = [jnp.zeros((8, LANES), jnp.float32)] * (rows // 8)
    halves = [jnp.concatenate((blocks[h::2] + blank)[: rows // 8], axis=0) for h in range(2)]
    return jnp.concatenate(halves, axis=1).astype(jnp.bfloat16)


def packed_squares(acc):
    return jnp.concatenate(in_two(acc), axis=0).astype(jnp.bfloat16)


def read_squares(both):
    both = both.astype(jnp.float32)
    return both[:8] + both[8:16]


def ray_blocks(obs_ref, count):
    obs = obs_ref[...]
    blocks = []
    for b in range(count):
        at = (b // 2) * 4 * LANES + (b % 2) * LANES
        blocks.append(jnp.concatenate([obs[:, at : at + LANES], obs[:, at + 2 * LANES : at + 3 * LANES]], axis=0))
    return blocks


def pack_kernel(obs_ref, unread_ref, blocks_ref):
    count = blocks_ref.shape[0] - 1
    blocks = ray_blocks(obs_ref, count)
    for b, block in enumerate(blocks):
        blocks_ref[b] = block
    blocks_ref[count] = tree_sum([b * b for b in blocks])


def join_kernel(own_ref, other_ref, both_ref):
    count = own_ref.shape[0] - 1
    both_ref[:count] = own_ref[:count]
    both_ref[count : 2 * count] = other_ref[:count]
    both_ref[2 * count] = own_ref[count] + other_ref[count]


def keys_kernel(unread_ref, cols_ref, keys_ref):
    keys_ref[...] = key_row(cols_ref)


def key_row(cols_ref):
    per_block, row_tiles = cols_ref.shape
    width = per_block * row_tiles * RHS
    lane = lax.broadcasted_iota(jnp.int32, (8, width), 1)
    keys = jnp.zeros((8, width), jnp.int32)
    for i in range(row_tiles):
        for k in range(per_block):
            keys = jnp.where(lane // RHS == i * per_block + k, cols_ref[k, i], keys)
    return (keys * RHS + lane % RHS).astype(jnp.float32)


def fill_equal(keys_ref, equal_ref, weight_ref):
    rows, _, per_row = keys_ref.shape

    @pl.loop(0, rows)
    def _(s):
        down = jnp.broadcast_to(keys_ref[s][:1], (LANES, per_row)).T
        at = pl.ds(pl.multiple_of(s * per_row, per_row), per_row)
        count = jnp.zeros((per_row, LANES), jnp.float32)
        for other in range(rows):
            for h in range(per_row // LANES):
                across = keys_ref[other, :1, h * LANES : (h + 1) * LANES]
                same = jnp.where(down == across, 1.0, 0.0)
                count = count + same
                lane = other * per_row + h * LANES
                equal_ref[at, lane : lane + LANES] = same.astype(jnp.bfloat16)
        weight_ref[at, :] = jnp.broadcast_to(1.0 / jnp.sum(count, axis=1, keepdims=True), (per_row, LANES))


def fill_pick(keys_ref, pick_ref):
    rows, _, per_row = keys_ref.shape
    wanted = pick_ref.shape[0]
    step_rows = 128
    start = lax.axis_index("row") * wanted

    @pl.loop(0, wanted // step_rows)
    def _(step):
        down = lax.broadcasted_iota(jnp.int32, (step_rows, LANES), 0) + (start + step * step_rows)
        down = down.astype(jnp.float32)
        at = pl.ds(pl.multiple_of(step * step_rows, step_rows), step_rows)
        for other in range(rows):
            for h in range(per_row // LANES):
                across = keys_ref[other, :1, h * LANES : (h + 1) * LANES]
                lane = other * per_row + h * LANES
                pick_ref[at, lane : lane + LANES] = jnp.where(down == across, 1.0, 0.0).astype(jnp.bfloat16)


def adjoint_rows(rays, tiles_ref, owner, per_share, g):
    low = low_half(2 * LANES)
    i = owner * per_share + 2 * g
    wide = [
        jnp.dot(rays, tiles_ref[i + e, k], preferred_element_type=jnp.float32)[8 * g : 8 * g + 8]
        for e in range(2)
        for k in range(2)
    ]
    value = jnp.concatenate(
        [
            jnp.where(low, wide[0], pltpu.roll(wide[1], 4, 0)),
            jnp.where(low, pltpu.roll(wide[2], 4, 0), wide[3]),
        ],
        axis=0,
    )
    return value, pl.multiple_of(8 * i, 16)


def half_sources(half_ref, half):
    peers = lax.axis_size("col") // 2
    rows = (half_ref.shape[0] - 16) // peers
    core = jnp.bitwise_xor(lax.axis_index("col") % 2, half)
    return [(2 * slot + core, half_ref[slot * rows : (slot + 1) * rows]) for slot in range(peers)]


def own_adjoint_kernel(tiles_ref, half_ref, out_ref):
    per_share = tiles_ref.shape[0] // lax.axis_size("col")
    at = 0
    for owner, rays in half_sources(half_ref, 0):
        for g in range(per_share // 2):
            value, _ = adjoint_rows(rays, tiles_ref, owner, per_share, g)
            out_ref[at : at + 16] = value.astype(jnp.bfloat16)
            at += 16


def adjoint_kernel(first, unread, keys_ref, tiles_ref, *refs):
    refs = refs[unread:]
    row_tiles, per_block = tiles_ref.shape[:2]
    shares = lax.axis_size("col")
    me = lax.axis_index("col")
    per_share = row_tiles // shares
    terms = row_tiles * per_block * RHS
    if first:
        pairs, (term_ref, lower_ref) = refs[: shares // 2], refs[shares // 2 :]
        squares, sources = [], []
        for e, pair in enumerate(pairs):
            squares.append(pair[2 * per_share])
            for h in range(2):
                blocks = [pair[h * per_share + b] for b in range(per_share)]
                owner = jnp.bitwise_xor(me, 2 * e + h)
                sources.append((owner, packed(blocks, max(16, 4 * per_share))))
    else:
        done_ref, own_ref, other_ref, term_ref = refs
        squares = [read_squares(half[-16:, :LANES]) for half in (own_ref, other_ref)]
        sources = half_sources(other_ref, 1)
        at = 0
        for slot in range(shares // 2):
            for g in range(per_share // 2):
                i = (2 * slot + me % 2) * per_share + 2 * g
                term_ref[pl.ds(pl.multiple_of(8 * i, 16), 16), :] = done_ref[at : at + 16]
                at += 16
    squares = tree_sum(squares)
    pieces = jnp.concatenate(in_two(squares), axis=1)
    extra = jnp.zeros_like(pieces)
    if first:
        keys = keys_ref[...]
        coarse = jnp.floor(keys * (1.0 / 64))
        extra = jnp.where(low_half(2 * LANES), coarse, keys - 64 * coarse)
    term_ref[terms:] = jnp.concatenate([pieces, extra], axis=0).astype(jnp.bfloat16)
    for owner, rays in sources:
        for g in range(per_share // 2):
            value, at = adjoint_rows(rays, tiles_ref, owner, per_share, g)
            upper = value.astype(jnp.bfloat16)
            term_ref[pl.ds(at, 16), :] = upper
            if first:
                lower_ref[pl.ds(at, 16), :] = (value - upper.astype(jnp.float32)).astype(jnp.bfloat16)


def voxel_kernel(first, rows, tiles_ref, *refs):
    terms, refs = refs[:rows], list(refs[rows:])
    if first:
        lhs_ref, acc_ref, other_ref, beta_ref, all_ref, raw_ref, equal_ref, weight_ref, keys_ref = refs
    else:
        equal_ref, weight_ref, right_ref, alpha_ref = refs[:4]
        lhs_ref, acc_ref, other_ref, beta_ref, all_ref, raw_ref = refs[-6:]
    my_row = lax.axis_index("row")
    row_tiles, per_block = tiles_ref.shape[:2]
    per_row = row_tiles * per_block * RHS
    low = low_half(2 * LANES)
    squares = []
    for d in range(rows):
        slot = jnp.bitwise_xor(my_row, d)
        at = pl.ds(pl.multiple_of(slot * per_row, per_row), per_row)
        all_ref[at, :] = terms[d][:per_row]
        extra = terms[d][per_row:].astype(jnp.float32)
        squares.append(extra[:8, :LANES] + extra[:8, LANES:])
        if first:
            pieces = jnp.where(low, extra[8:] * 64, extra[8:])
            keys_ref[slot] = pieces + pltpu.roll(pieces, 4, 0)
    if first:
        fill_equal(keys_ref, equal_ref, weight_ref)
    beta = norm_of(tree_sum(squares))
    beta_ref[...] = beta
    wide_scale = jnp.concatenate([1.0 / beta] * 2, axis=1)
    if not first:
        wide_right = jnp.concatenate([beta / alpha_ref[...]] * 2, axis=1)
    acc = jnp.zeros((8, LANES), jnp.float32)
    for s in range(rows):
        same = equal_ref[s * per_row : (s + 1) * per_row, :]
        summed = jnp.dot(same, all_ref[...], preferred_element_type=jnp.float32)
        for m in range(per_row // 8):
            at = s * per_row + 8 * m
            raw = summed[8 * m : 8 * m + 8] * wide_scale
            if not first:
                raw = raw - right_ref[at : at + 8] * wide_right
            raw_ref[at : at + 8] = raw
            square = raw * raw
            acc = acc + (square[:, :LANES] + square[:, LANES:]) * weight_ref[at : at + 8]
    lhs_ref[...] = raw_ref[pl.ds(pl.multiple_of(my_row * per_row, 16), per_row), :].astype(jnp.bfloat16)
    forward_half(1, tiles_ref, lhs_ref, other_ref)
    other_ref[other_ref.shape[0] - 1] = acc
    acc_ref[...] = acc


def forward_half(half, tiles_ref, lhs_ref, out_ref):
    shares = lax.axis_size("col")
    per_share = tiles_ref.shape[0] // shares
    low = low_half(2 * LANES)
    core = lax.axis_index("col") % 2
    for slot in range(shares // 2):
        c = 2 * slot + jnp.bitwise_xor(core, half)
        for g in range(per_share // 2):
            i = c * per_share + 2 * g
            lhs = lhs_ref[pl.ds(pl.multiple_of(8 * i, 16), 16), :]
            wide = [
                lax.dot_general(
                    lhs, tiles_ref[i + e, k], (((1,), (1,)), ((), ())), preferred_element_type=jnp.float32
                )[8 * e : 8 * e + 8]
                for e in range(2)
                for k in range(2)
            ]
            value = jnp.where(low, wide[0], wide[3]) + pltpu.roll(jnp.where(low, wide[2], wide[1]), 4, 0)
            at = slot * per_share + 2 * g
            out_ref[at] = value[:, :LANES]
            out_ref[at + 1] = value[:, LANES:]


def forward_kernel(tiles_ref, lhs_ref, acc_ref, own_ref):
    forward_half(0, tiles_ref, lhs_ref, own_ref)
    own_ref[own_ref.shape[0] - 1] = acc_ref[...]


def pair_kernel(narrow, own_ref, other_ref, *refs):
    passed = len(refs) // 2
    out_ref = refs[passed]
    for i in range(passed):
        refs[1 + passed + i][...] = refs[i][...]
    if not narrow:
        out_ref[...] = own_ref[...] + other_ref[...]
        return
    count = own_ref.shape[0] - 1
    for b in range(0, count, 2):
        two = [own_ref[b + i] + other_ref[b + i] for i in range(2)]
        out_ref[8 * b : 8 * b + 16, :] = jnp.concatenate(two, axis=0).astype(jnp.bfloat16)
    out_ref[8 * count :, :] = packed_squares(own_ref[count] + other_ref[count])


def sum_kernel(*refs):
    refs[-1][...] = refs[-3][...] + refs[-2][...]


def half_ray_kernel(peers, first, narrow, update, unread, *refs):
    refs = refs[unread:]
    parts, refs = refs[:peers], refs[peers:]
    if update:
        lefts, (beta_ref, alpha_ref, raw_ref, half_ref) = refs[:-4], refs[-4:]
        rows = (half_ref.shape[0] - 16) // peers
    else:
        lefts, (beta_ref, alpha_ref, acc_ref) = refs[:-3], refs[-3:]
    if narrow:
        count = (parts[0].shape[0] - 16) // 8
        squares = [read_squares(p[8 * count :, :]) for p in parts]
    else:
        count = parts[0].shape[0] - 1
        squares = [p[count] for p in parts]
    per_share = count // peers
    alpha = norm_of(tree_sum(squares))
    alpha_ref[...] = alpha
    alpha_inv = 1.0 / alpha
    left_scale = alpha / beta_ref[...]
    squares = []
    for e in range(peers):
        slot = jnp.bitwise_xor(lax.axis_index("col") // 2, e)
        if narrow:
            at = pl.ds(pl.multiple_of(slot * per_share * 8, 16), per_share * 8)
            whole = tree_sum([p[at, :].astype(jnp.float32) for p in parts])
            totals = [whole[8 * b : 8 * b + 8] for b in range(per_share)]
        else:
            totals = [tree_sum([p[slot * per_share + b] for p in parts]) for b in range(per_share)]
        blocks = []
        for b in range(per_share):
            at = slot * per_share + b
            left = lefts[e][b] if first else lefts[0][at]
            blocks.append(totals[b] * alpha_inv - left * left_scale)
            if update:
                raw_ref[at] = blocks[-1]
        if update:
            half_ref[pl.ds(pl.multiple_of(slot * rows, 16), rows), :] = packed(blocks, rows)
        squares.append(tree_sum([b * b for b in blocks]))
    acc = tree_sum(squares)
    if update:
        pieces = packed_squares(acc)
        half_ref[peers * rows :, :LANES] = pieces
        half_ref[peers * rows :, LANES:] = jnp.zeros_like(pieces)
    else:
        acc_ref[...] = acc


def share_kernel(remainders, *refs):
    pick_ref, all_ref = refs[:2]
    lower_terms, out_ref = refs[2 : 2 + remainders], refs[2 + remainders]
    values = [all_ref]
    if remainders:
        held = refs[-1]
        per_row = lower_terms[0].shape[0]
        for d, term in enumerate(lower_terms):
            slot = jnp.bitwise_xor(lax.axis_index("row"), d)
            held[pl.ds(pl.multiple_of(slot * per_row, per_row), per_row), :] = term[...]
        values.append(held)
    step = 128
    for at in range(0, out_ref.shape[0], step):
        pick = pick_ref[at : at + step, :]
        out_ref[at : at + step, :] = tree_sum(
            [jnp.dot(pick, v[...], preferred_element_type=jnp.float32) for v in values]
        )


def pick_kernel(unread_ref, keys_ref, pick_ref):
    fill_pick(keys_ref, pick_ref)


def final_kernel(rows, iters, *refs):
    refs = list(refs)
    last = [refs.pop(0) for _ in range(rows)]
    betas = [refs.pop(0) for _ in range(iters)]
    alphas = [refs.pop(0) for _ in range(iters)]
    products = [refs.pop(0) for _ in range(iters)]
    out_ref, ratio_ref = refs
    beta = [b[...] for b in betas] + [norm_of(tree_sum([p[...] for p in last]))]
    alpha = [a[...] for a in alphas]
    phibar, rhobar = beta[0], alpha[0]
    direction = [1.0 / alpha[0]] + [jnp.zeros_like(phibar)] * (iters - 1)
    weights = [jnp.zeros_like(phibar)] * iters
    for i in range(iters):
        rho = jnp.sqrt(rhobar * rhobar + beta[i + 1] * beta[i + 1])
        cosine, sine = rhobar / rho, beta[i + 1] / rho
        phi = cosine * phibar
        phibar = sine * phibar
        weights = [w + (phi / rho) * d for w, d in zip(weights, direction)]
        if i + 1 < iters:
            theta = sine * alpha[i + 1]
            rhobar = -cosine * alpha[i + 1]
            direction = [-(theta / rho) * d for d in direction]
            direction[i + 1] = direction[i + 1] + 1.0 / alpha[i + 1]
    ratio = phibar / beta[0]
    for n in range(RHS):
        ratio_ref[n] = jnp.max(ratio[n : n + 1])
    scales = []
    carried = jnp.zeros_like(phibar)
    for i in reversed(range(iters)):
        carried = weights[i] - carried
        scales.insert(0, jnp.concatenate([carried / beta[i]] * 2, axis=1))
        if i > 0:
            carried = carried * (beta[i] / alpha[i - 1])
    unroll = 4

    @pl.loop(0, products[0].shape[0] // (8 * unroll))
    def _(step):
        for u in range(unroll):
            m = step * unroll + u
            at = pl.ds(pl.multiple_of(m * 8, 8), 8)
            both = tree_sum([p[at, :] * s for p, s in zip(products, scales)])
            lane = pl.multiple_of(m * 4 * LANES, 4 * LANES)
            out_ref[:, pl.ds(lane, 2 * LANES)] = both[:4]
            out_ref[:, pl.ds(lane + 2 * LANES, 2 * LANES)] = both[4:]


def f32(*shape):
    return jax.ShapeDtypeStruct(shape, jnp.float32)


def bf16(*shape):
    return jax.ShapeDtypeStruct(shape, jnp.bfloat16)


def from_peer(value, axis, d):
    return lax.ppermute(value, axis, [(i, i ^ d) for i in range(lax.axis_size(axis))])


def exchange(value, axis, step=1):
    return [value] + [from_peer(value, axis, d) for d in range(step, lax.axis_size(axis), step)]


def local(observed, tile_values, tile_cols):
    row_tiles, per_block, tile_size = tile_values.shape[:3]
    rows, shares = lax.axis_size("row"), lax.axis_size("col")
    col_tiles = N // (tile_size * shares)
    per_share = row_tiles // shares
    per_row = row_tiles * per_block * RHS
    share_rows = col_tiles // rows * RHS
    ray_rows = max(16, RHS * per_share)
    half_shares = shares // 2
    half_blocks = half_shares * per_share
    def call(kernel, name, out_shape, args, in_specs=None, scratch=(), flops=None):
        return pl.pallas_call(
            kernel,
            out_shape=out_shape,
            in_specs=in_specs or [VMEM] * len(args),
            out_specs=jax.tree.map(lambda _: VMEM, out_shape),
            scratch_shapes=list(scratch),
            compiler_params=PARAMS,
            cost_estimate=flops and pl.CostEstimate(flops=flops, bytes_accessed=0, transcendentals=0),
            name=name,
        )(*args)

    def adjoint(payloads, first, after):
        out_shape = [bf16(per_row + 16, tile_size)] + [bf16(per_row, tile_size)] * first
        args = [keys, tile_values, *after, *payloads]
        specs = [VMEM] * 2 + [ANY] * len(after) + [VMEM] * len(payloads)
        return call(functools.partial(adjoint_kernel, first, len(after)), "adjoint", out_shape, args, specs)

    def voxel(term_list, previous, keep):
        first = not previous
        out_shape = [bf16(per_row, tile_size), f32(8, LANES), f32(half_blocks + 1, 8, LANES)]
        out_shape += [f32(8, LANES), bf16(rows * per_row, tile_size)]
        raw_shape = (rows * per_row, tile_size)
        out_shape += [f32(*raw_shape)] * keep
        if first:
            out_shape += [
                bf16(rows * per_row, rows * per_row),
                f32(rows * per_row, LANES),
                f32(rows, 8, per_row),
            ]
        args = [tile_values, *term_list, *previous]
        scratch = [pltpu.VMEM(raw_shape, jnp.float32)] * (not keep)
        lhs, acc, other, *rest = call(
            functools.partial(voxel_kernel, first, rows), "voxel", out_shape, args, None, scratch
        )
        own = call(forward_kernel, "forward", f32(half_blocks + 1, 8, LANES), [tile_values, lhs, acc])
        return own, other, *rest

    def pair(own, other, passed, narrow):
        args = [own, from_peer(other, "col", 1), *passed]
        out_shape = [jax.ShapeDtypeStruct(x.shape, x.dtype) for x in [own, *passed]]
        if narrow:
            out_shape[0] = bf16(8 * half_blocks + 16, LANES)
        return call(functools.partial(pair_kernel, narrow), "pair", out_shape, args)

    def half_ray(parts, lefts, beta, after, narrow, update):
        out_shape = [f32(8, LANES)]
        if update:
            out_shape += [f32(half_blocks, 8, LANES), bf16(half_shares * ray_rows + 16, 2 * LANES)]
        else:
            out_shape += [f32(8, LANES)]
        kernel = functools.partial(half_ray_kernel, half_shares, len(lefts) > 1, narrow, update, len(after))
        args = [*after, *parts, *lefts, beta]
        specs = [ANY] * len(after) + [VMEM] * (len(args) - len(after))
        return call(kernel, "half_ray", out_shape, args, specs, (), 2 * 10**9)

    def share(selector, all_terms, lower_terms):
        scratch = [pltpu.VMEM((rows * per_row, tile_size), jnp.bfloat16)] * (len(lower_terms) > 0)
        kernel = functools.partial(share_kernel, len(lower_terms))
        args = [selector, all_terms, *lower_terms]
        return call(kernel, "share", f32(share_rows, tile_size), args, None, scratch)

    far = pltpu.with_memory_space_constraint(tile_values, pltpu.HBM)
    blocks = call(pack_kernel, "pack", f32(per_share + 1, 8, LANES), [observed, far], [VMEM, HBM])
    keys = call(keys_kernel, "keys", f32(8, per_row), [blocks, tile_cols.T], [ANY, SMEM])
    both = call(join_kernel, "join", f32(2 * per_share + 1, 8, LANES), [blocks, from_peer(blocks, "col", 1)])
    lefts = exchange(both, "col", 2)
    terms, remainder = adjoint(lefts, True, [])
    terms = exchange(terms, "row")
    own, other, beta, upper_terms, right_raw, equal, weight, all_keys = voxel(terms, [], True)
    betas, alphas, combined = [], [], []
    remainders = [None] * rows
    for iteration in range(ITERS):
        last = iteration == ITERS - 1
        betas.append(beta)
        combined.append(upper_terms)
        late = range(rows // 2, rows - 1)
        crossing = [d for d in range(1, rows) if d not in late] if iteration == 0 else late if last else []
        summed, *passed = pair(own, other, [remainder] * (len(crossing) > 0), last)
        gathered = exchange(summed, "col", 2)
        for d in crossing:
            remainders[d] = from_peer(passed[0], "row", d)
        after = [remainders[d] for d in crossing]
        if last:
            alpha, squares = half_ray(gathered, lefts, beta, [], True, False)
            _, left_raw, half = half_ray(gathered, lefts, beta, [], True, True)
        else:
            alpha, left_raw, half = half_ray(gathered, lefts, beta, [], False, True)
        alphas.append(alpha)
        lefts = [left_raw]
        other_half = from_peer(half, "col", 1)
        done = call(own_adjoint_kernel, "own_adjoint", bf16(per_row // 2, tile_size), [tile_values, half])
        (new_terms,) = adjoint([done, half, other_half], False, after)
        if iteration == 0:
            selector = call(pick_kernel, "pick", bf16(share_rows, rows * per_row), [new_terms, all_keys], [ANY, VMEM])
        new_terms = exchange(new_terms, "row")
        fixed = [equal, weight, right_raw, alpha]
        own, other, beta, upper_terms = voxel(new_terms, fixed, False)
        right_raw = voxel(new_terms, fixed, True)[4]
    remainders[0] = remainder
    products = [share(selector, c, [] if i else remainders) for i, c in enumerate(combined)]
    squares = call(
        sum_kernel, "sum", f32(8, LANES), [*after, squares, from_peer(squares, "col", 1)], [ANY] * len(after) + [VMEM] * 2
    )
    result, ratio = pl.pallas_call(
        functools.partial(final_kernel, rows, ITERS),
        out_shape=[f32(RHS, col_tiles // rows * tile_size), f32(RHS)],
        in_specs=[VMEM] * (rows + 3 * ITERS),
        out_specs=[VMEM, SMEM],
        compiler_params=PARAMS,
        name="final",
    )(*exchange(squares, "row"), *betas, *alphas, *products)
    return result, ratio


def solution(mesh):
    in_specs = (P(None, ("row", "col")), P("row", "col", None, None), P("row", "col"))
    out_specs = (P(None, ("col", "row")), P())
    return jax.shard_map(local, mesh=mesh, in_specs=in_specs, out_specs=out_specs, check_vma=False)
```

```python
import functools

import jax
import jax.numpy as jnp
from jax import lax
from jax.experimental import pallas as pl
from jax.experimental.pallas import tpu as pltpu
from jax.sharding import PartitionSpec as P

ITERS = 2
N = 1048576
epsilon_sq = 1e-06
LANES = 128
RHS = 4
VMEM = pl.BlockSpec(memory_space=pltpu.VMEM)
SMEM = pl.BlockSpec(memory_space=pltpu.SMEM)
HBM = pl.BlockSpec(memory_space=pltpu.HBM)
ANY = pl.BlockSpec(memory_space=pl.ANY)
PARAMS = pltpu.CompilerParams(vmem_limit_bytes=32 * 1024 * 1024)


def tree_sum(parts):
    while len(parts) > 1:
        paired = [parts[i] + parts[i + 1] for i in range(0, len(parts) - 1, 2)]
        parts = paired + parts[2 * len(paired) :]
    return parts[0]


def norm_of(acc):
    rows = jnp.broadcast_to(jnp.sum(acc, axis=1, keepdims=True), acc.shape)
    return jnp.sqrt(rows + pltpu.roll(rows, 4, 0) + epsilon_sq)


def low_half(width):
    return lax.broadcasted_iota(jnp.int32, (8, width), 0) < 4


def in_two(acc):
    upper = acc.astype(jnp.bfloat16).astype(jnp.float32)
    return upper, acc - upper


def packed(blocks, rows):
    blank = [jnp.zeros((8, LANES), jnp.float32)] * (rows // 8)
    halves = [jnp.concatenate((blocks[h::2] + blank)[: rows // 8], axis=0) for h in range(2)]
    return jnp.concatenate(halves, axis=1).astype(jnp.bfloat16)


def packed_squares(acc):
    return jnp.concatenate(in_two(acc), axis=0).astype(jnp.bfloat16)


def read_squares(both):
    both = both.astype(jnp.float32)
    return both[:8] + both[8:16]


def ray_blocks(obs_ref, count):
    obs = obs_ref[...]
    blocks = []
    for b in range(count):
        at = (b // 2) * 4 * LANES + (b % 2) * LANES
        blocks.append(jnp.concatenate([obs[:, at : at + LANES], obs[:, at + 2 * LANES : at + 3 * LANES]], axis=0))
    return blocks


def pack_kernel(obs_ref, unread_ref, blocks_ref):
    count = blocks_ref.shape[0] - 1
    blocks = ray_blocks(obs_ref, count)
    for b, block in enumerate(blocks):
        blocks_ref[b] = block
    blocks_ref[count] = tree_sum([b * b for b in blocks])


def join_kernel(own_ref, other_ref, both_ref):
    count = own_ref.shape[0] - 1
    both_ref[:count] = own_ref[:count]
    both_ref[count : 2 * count] = other_ref[:count]
    both_ref[2 * count] = own_ref[count] + other_ref[count]


def keys_kernel(unread_ref, cols_ref, keys_ref):
    keys_ref[...] = key_row(cols_ref)


def key_row(cols_ref):
    per_block, row_tiles = cols_ref.shape
    width = per_block * row_tiles * RHS
    lane = lax.broadcasted_iota(jnp.int32, (8, width), 1)
    keys = jnp.zeros((8, width), jnp.int32)
    for i in range(row_tiles):
        for k in range(per_block):
            keys = jnp.where(lane // RHS == i * per_block + k, cols_ref[k, i], keys)
    return (keys * RHS + lane % RHS).astype(jnp.float32)


def fill_equal(keys_ref, equal_ref, weight_ref):
    rows, _, per_row = keys_ref.shape

    @pl.loop(0, rows)
    def _(s):
        down = jnp.broadcast_to(keys_ref[s][:1], (LANES, per_row)).T
        at = pl.ds(pl.multiple_of(s * per_row, per_row), per_row)
        count = jnp.zeros((per_row, LANES), jnp.float32)
        for other in range(rows):
            for h in range(per_row // LANES):
                across = keys_ref[other, :1, h * LANES : (h + 1) * LANES]
                same = jnp.where(down == across, 1.0, 0.0)
                count = count + same
                lane = other * per_row + h * LANES
                equal_ref[at, lane : lane + LANES] = same.astype(jnp.bfloat16)
        weight_ref[at, :] = jnp.broadcast_to(1.0 / jnp.sum(count, axis=1, keepdims=True), (per_row, LANES))


def fill_pick(keys_ref, pick_ref):
    rows, _, per_row = keys_ref.shape
    wanted = pick_ref.shape[0]
    step_rows = 128
    start = lax.axis_index("row") * wanted

    @pl.loop(0, wanted // step_rows)
    def _(step):
        down = lax.broadcasted_iota(jnp.int32, (step_rows, LANES), 0) + (start + step * step_rows)
        down = down.astype(jnp.float32)
        at = pl.ds(pl.multiple_of(step * step_rows, step_rows), step_rows)
        for other in range(rows):
            for h in range(per_row // LANES):
                across = keys_ref[other, :1, h * LANES : (h + 1) * LANES]
                lane = other * per_row + h * LANES
                pick_ref[at, lane : lane + LANES] = jnp.where(down == across, 1.0, 0.0).astype(jnp.bfloat16)


def adjoint_rows(rays, tiles_ref, owner, per_share, g):
    low = low_half(2 * LANES)
    i = owner * per_share + 2 * g
    wide = [
        jnp.dot(rays, tiles_ref[i + e, k], preferred_element_type=jnp.float32)[8 * g : 8 * g + 8]
        for e in range(2)
        for k in range(2)
    ]
    value = jnp.concatenate(
        [
            jnp.where(low, wide[0], pltpu.roll(wide[1], 4, 0)),
            jnp.where(low, pltpu.roll(wide[2], 4, 0), wide[3]),
        ],
        axis=0,
    )
    return value, pl.multiple_of(8 * i, 16)


def half_sources(half_ref, half):
    peers = lax.axis_size("col") // 2
    rows = (half_ref.shape[0] - 16) // peers
    core = jnp.bitwise_xor(lax.axis_index("col") % 2, half)
    return [(2 * slot + core, half_ref[slot * rows : (slot + 1) * rows]) for slot in range(peers)]


def own_adjoint_kernel(tiles_ref, half_ref, out_ref):
    per_share = tiles_ref.shape[0] // lax.axis_size("col")
    at = 0
    for owner, rays in half_sources(half_ref, 0):
        for g in range(per_share // 2):
            value, _ = adjoint_rows(rays, tiles_ref, owner, per_share, g)
            out_ref[at : at + 16] = value.astype(jnp.bfloat16)
            at += 16


def adjoint_kernel(first, unread, keys_ref, tiles_ref, *refs):
    refs = refs[unread:]
    row_tiles, per_block = tiles_ref.shape[:2]
    shares = lax.axis_size("col")
    me = lax.axis_index("col")
    per_share = row_tiles // shares
    terms = row_tiles * per_block * RHS
    if first:
        pairs, (term_ref, lower_ref) = refs[: shares // 2], refs[shares // 2 :]
        squares, sources = [], []
        for e, pair in enumerate(pairs):
            squares.append(pair[2 * per_share])
            for h in range(2):
                blocks = [pair[h * per_share + b] for b in range(per_share)]
                owner = jnp.bitwise_xor(me, 2 * e + h)
                sources.append((owner, packed(blocks, max(16, 4 * per_share))))
    else:
        done_ref, own_ref, other_ref, term_ref = refs
        squares = [read_squares(half[-16:, :LANES]) for half in (own_ref, other_ref)]
        sources = half_sources(other_ref, 1)
        at = 0
        for slot in range(shares // 2):
            for g in range(per_share // 2):
                i = (2 * slot + me % 2) * per_share + 2 * g
                term_ref[pl.ds(pl.multiple_of(8 * i, 16), 16), :] = done_ref[at : at + 16]
                at += 16
    squares = tree_sum(squares)
    pieces = jnp.concatenate(in_two(squares), axis=1)
    extra = jnp.zeros_like(pieces)
    if first:
        keys = keys_ref[...]
        coarse = jnp.floor(keys * (1.0 / 64))
        extra = jnp.where(low_half(2 * LANES), coarse, keys - 64 * coarse)
    term_ref[terms:] = jnp.concatenate([pieces, extra], axis=0).astype(jnp.bfloat16)
    for owner, rays in sources:
        for g in range(per_share // 2):
            value, at = adjoint_rows(rays, tiles_ref, owner, per_share, g)
            upper = value.astype(jnp.bfloat16)
            term_ref[pl.ds(at, 16), :] = upper
            if first:
                lower_ref[pl.ds(at, 16), :] = (value - upper.astype(jnp.float32)).astype(jnp.bfloat16)


def voxel_kernel(first, rows, tiles_ref, *refs):
    terms, refs = refs[:rows], list(refs[rows:])
    if first:
        lhs_ref, acc_ref, other_ref, beta_ref, all_ref, raw_ref, equal_ref, weight_ref, keys_ref = refs
    else:
        equal_ref, weight_ref, right_ref, alpha_ref = refs[:4]
        lhs_ref, acc_ref, other_ref, beta_ref, all_ref, raw_ref = refs[-6:]
    my_row = lax.axis_index("row")
    row_tiles, per_block = tiles_ref.shape[:2]
    per_row = row_tiles * per_block * RHS
    low = low_half(2 * LANES)
    squares = []
    for d in range(rows):
        slot = jnp.bitwise_xor(my_row, d)
        at = pl.ds(pl.multiple_of(slot * per_row, per_row), per_row)
        all_ref[at, :] = terms[d][:per_row]
        extra = terms[d][per_row:].astype(jnp.float32)
        squares.append(extra[:8, :LANES] + extra[:8, LANES:])
        if first:
            pieces = jnp.where(low, extra[8:] * 64, extra[8:])
            keys_ref[slot] = pieces + pltpu.roll(pieces, 4, 0)
    if first:
        fill_equal(keys_ref, equal_ref, weight_ref)
    beta = norm_of(tree_sum(squares))
    beta_ref[...] = beta
    wide_scale = jnp.concatenate([1.0 / beta] * 2, axis=1)
    if not first:
        wide_right = jnp.concatenate([beta / alpha_ref[...]] * 2, axis=1)
    acc = jnp.zeros((8, LANES), jnp.float32)
    for s in range(rows):
        same = equal_ref[s * per_row : (s + 1) * per_row, :]
        summed = jnp.dot(same, all_ref[...], preferred_element_type=jnp.float32)
        for m in range(per_row // 8):
            at = s * per_row + 8 * m
            raw = summed[8 * m : 8 * m + 8] * wide_scale
            if not first:
                raw = raw - right_ref[at : at + 8] * wide_right
            raw_ref[at : at + 8] = raw
            square = raw * raw
            acc = acc + (square[:, :LANES] + square[:, LANES:]) * weight_ref[at : at + 8]
    lhs_ref[...] = raw_ref[pl.ds(pl.multiple_of(my_row * per_row, 16), per_row), :].astype(jnp.bfloat16)
    forward_half(1, tiles_ref, lhs_ref, other_ref)
    other_ref[other_ref.shape[0] - 1] = acc
    acc_ref[...] = acc


def forward_half(half, tiles_ref, lhs_ref, out_ref):
    shares = lax.axis_size("col")
    per_share = tiles_ref.shape[0] // shares
    low = low_half(2 * LANES)
    core = lax.axis_index("col") % 2
    for slot in range(shares // 2):
        c = 2 * slot + jnp.bitwise_xor(core, half)
        for g in range(per_share // 2):
            i = c * per_share + 2 * g
            lhs = lhs_ref[pl.ds(pl.multiple_of(8 * i, 16), 16), :]
            wide = [
                lax.dot_general(
                    lhs, tiles_ref[i + e, k], (((1,), (1,)), ((), ())), preferred_element_type=jnp.float32
                )[8 * e : 8 * e + 8]
                for e in range(2)
                for k in range(2)
            ]
            value = jnp.where(low, wide[0], wide[3]) + pltpu.roll(jnp.where(low, wide[2], wide[1]), 4, 0)
            at = slot * per_share + 2 * g
            out_ref[at] = value[:, :LANES]
            out_ref[at + 1] = value[:, LANES:]


def forward_kernel(tiles_ref, lhs_ref, acc_ref, own_ref):
    forward_half(0, tiles_ref, lhs_ref, own_ref)
    own_ref[own_ref.shape[0] - 1] = acc_ref[...]


def pair_kernel(narrow, own_ref, other_ref, *refs):
    passed = len(refs) // 2
    out_ref = refs[passed]
    for i in range(passed):
        refs[1 + passed + i][...] = refs[i][...]
    if not narrow:
        out_ref[...] = own_ref[...] + other_ref[...]
        return
    count = own_ref.shape[0] - 1
    for b in range(0, count, 2):
        two = [own_ref[b + i] + other_ref[b + i] for i in range(2)]
        out_ref[8 * b : 8 * b + 16, :] = jnp.concatenate(two, axis=0).astype(jnp.bfloat16)
    out_ref[8 * count :, :] = packed_squares(own_ref[count] + other_ref[count])


def sum_kernel(own_ref, other_ref, out_ref):
    out_ref[...] = own_ref[...] + other_ref[...]


def half_ray_kernel(peers, first, narrow, update, unread, *refs):
    refs = refs[unread:]
    parts, refs = refs[:peers], refs[peers:]
    if update:
        lefts, (beta_ref, alpha_ref, raw_ref, half_ref) = refs[:-4], refs[-4:]
        rows = (half_ref.shape[0] - 16) // peers
    else:
        lefts, (beta_ref, alpha_ref, acc_ref) = refs[:-3], refs[-3:]
    if narrow:
        count = (parts[0].shape[0] - 16) // 8
        squares = [read_squares(p[8 * count :, :]) for p in parts]
    else:
        count = parts[0].shape[0] - 1
        squares = [p[count] for p in parts]
    per_share = count // peers
    alpha = norm_of(tree_sum(squares))
    alpha_ref[...] = alpha
    alpha_inv = 1.0 / alpha
    left_scale = alpha / beta_ref[...]
    squares = []
    for e in range(peers):
        slot = jnp.bitwise_xor(lax.axis_index("col") // 2, e)
        if narrow:
            at = pl.ds(pl.multiple_of(slot * per_share * 8, 16), per_share * 8)
            whole = tree_sum([p[at, :].astype(jnp.float32) for p in parts])
            totals = [whole[8 * b : 8 * b + 8] for b in range(per_share)]
        else:
            totals = [tree_sum([p[slot * per_share + b] for p in parts]) for b in range(per_share)]
        blocks = []
        for b in range(per_share):
            at = slot * per_share + b
            left = lefts[e][b] if first else lefts[0][at]
            blocks.append(totals[b] * alpha_inv - left * left_scale)
            if update:
                raw_ref[at] = blocks[-1]
        if update:
            half_ref[pl.ds(pl.multiple_of(slot * rows, 16), rows), :] = packed(blocks, rows)
        squares.append(tree_sum([b * b for b in blocks]))
    acc = tree_sum(squares)
    if update:
        pieces = packed_squares(acc)
        half_ref[peers * rows :, :LANES] = pieces
        half_ref[peers * rows :, LANES:] = jnp.zeros_like(pieces)
    else:
        acc_ref[...] = acc


def share_kernel(remainders, *refs):
    pick_ref, all_ref = refs[:2]
    lower_terms, out_ref = refs[2 : 2 + remainders], refs[2 + remainders]
    values = [all_ref]
    if remainders:
        held = refs[-1]
        per_row = lower_terms[0].shape[0]
        for d, term in enumerate(lower_terms):
            slot = jnp.bitwise_xor(lax.axis_index("row"), d)
            held[pl.ds(pl.multiple_of(slot * per_row, per_row), per_row), :] = term[...]
        values.append(held)
    step = 128
    for at in range(0, out_ref.shape[0], step):
        pick = pick_ref[at : at + step, :]
        out_ref[at : at + step, :] = tree_sum(
            [jnp.dot(pick, v[...], preferred_element_type=jnp.float32) for v in values]
        )


def pick_kernel(unread_ref, keys_ref, pick_ref):
    fill_pick(keys_ref, pick_ref)


def final_kernel(rows, iters, *refs):
    refs = list(refs)
    last = [refs.pop(0) for _ in range(rows)]
    betas = [refs.pop(0) for _ in range(iters)]
    alphas = [refs.pop(0) for _ in range(iters)]
    products = [refs.pop(0) for _ in range(iters)]
    out_ref, ratio_ref = refs
    beta = [b[...] for b in betas] + [norm_of(tree_sum([p[...] for p in last]))]
    alpha = [a[...] for a in alphas]
    phibar, rhobar = beta[0], alpha[0]
    direction = [1.0 / alpha[0]] + [jnp.zeros_like(phibar)] * (iters - 1)
    weights = [jnp.zeros_like(phibar)] * iters
    for i in range(iters):
        rho = jnp.sqrt(rhobar * rhobar + beta[i + 1] * beta[i + 1])
        cosine, sine = rhobar / rho, beta[i + 1] / rho
        phi = cosine * phibar
        phibar = sine * phibar
        weights = [w + (phi / rho) * d for w, d in zip(weights, direction)]
        if i + 1 < iters:
            theta = sine * alpha[i + 1]
            rhobar = -cosine * alpha[i + 1]
            direction = [-(theta / rho) * d for d in direction]
            direction[i + 1] = direction[i + 1] + 1.0 / alpha[i + 1]
    ratio = phibar / beta[0]
    for n in range(RHS):
        ratio_ref[n] = jnp.max(ratio[n : n + 1])
    scales = []
    carried = jnp.zeros_like(phibar)
    for i in reversed(range(iters)):
        carried = weights[i] - carried
        scales.insert(0, jnp.concatenate([carried / beta[i]] * 2, axis=1))
        if i > 0:
            carried = carried * (beta[i] / alpha[i - 1])
    unroll = 4

    @pl.loop(0, products[0].shape[0] // (8 * unroll))
    def _(step):
        for u in range(unroll):
            m = step * unroll + u
            at = pl.ds(pl.multiple_of(m * 8, 8), 8)
            both = tree_sum([p[at, :] * s for p, s in zip(products, scales)])
            lane = pl.multiple_of(m * 4 * LANES, 4 * LANES)
            out_ref[:, pl.ds(lane, 2 * LANES)] = both[:4]
            out_ref[:, pl.ds(lane + 2 * LANES, 2 * LANES)] = both[4:]


def f32(*shape):
    return jax.ShapeDtypeStruct(shape, jnp.float32)


def bf16(*shape):
    return jax.ShapeDtypeStruct(shape, jnp.bfloat16)


def from_peer(value, axis, d):
    return lax.ppermute(value, axis, [(i, i ^ d) for i in range(lax.axis_size(axis))])


def exchange(value, axis, step=1):
    return [value] + [from_peer(value, axis, d) for d in range(step, lax.axis_size(axis), step)]


def local(observed, tile_values, tile_cols):
    row_tiles, per_block, tile_size = tile_values.shape[:3]
    rows, shares = lax.axis_size("row"), lax.axis_size("col")
    col_tiles = N // (tile_size * shares)
    per_share = row_tiles // shares
    per_row = row_tiles * per_block * RHS
    share_rows = col_tiles // rows * RHS
    ray_rows = max(16, RHS * per_share)
    half_shares = shares // 2
    half_blocks = half_shares * per_share
    def call(kernel, name, out_shape, args, in_specs=None, scratch=(), flops=None):
        return pl.pallas_call(
            kernel,
            out_shape=out_shape,
            in_specs=in_specs or [VMEM] * len(args),
            out_specs=jax.tree.map(lambda _: VMEM, out_shape),
            scratch_shapes=list(scratch),
            compiler_params=PARAMS,
            cost_estimate=flops and pl.CostEstimate(flops=flops, bytes_accessed=0, transcendentals=0),
            name=name,
        )(*args)

    def adjoint(payloads, first, after):
        out_shape = [bf16(per_row + 16, tile_size)] + [bf16(per_row, tile_size)] * first
        args = [keys, tile_values, *after, *payloads]
        specs = [VMEM] * 2 + [ANY] * len(after) + [VMEM] * len(payloads)
        return call(functools.partial(adjoint_kernel, first, len(after)), "adjoint", out_shape, args, specs)

    def voxel(term_list, previous, keep):
        first = not previous
        out_shape = [bf16(per_row, tile_size), f32(8, LANES), f32(half_blocks + 1, 8, LANES)]
        out_shape += [f32(8, LANES), bf16(rows * per_row, tile_size)]
        raw_shape = (rows * per_row, tile_size)
        out_shape += [f32(*raw_shape)] * keep
        if first:
            out_shape += [
                bf16(rows * per_row, rows * per_row),
                f32(rows * per_row, LANES),
                f32(rows, 8, per_row),
            ]
        args = [tile_values, *term_list, *previous]
        scratch = [pltpu.VMEM(raw_shape, jnp.float32)] * (not keep)
        lhs, acc, other, *rest = call(
            functools.partial(voxel_kernel, first, rows), "voxel", out_shape, args, None, scratch
        )
        own = call(forward_kernel, "forward", f32(half_blocks + 1, 8, LANES), [tile_values, lhs, acc])
        return own, other, *rest

    def pair(own, other, passed, narrow):
        args = [own, from_peer(other, "col", 1), *passed]
        out_shape = [jax.ShapeDtypeStruct(x.shape, x.dtype) for x in [own, *passed]]
        if narrow:
            out_shape[0] = bf16(8 * half_blocks + 16, LANES)
        return call(functools.partial(pair_kernel, narrow), "pair", out_shape, args)

    def half_ray(parts, lefts, beta, after, narrow, update):
        out_shape = [f32(8, LANES)]
        if update:
            out_shape += [f32(half_blocks, 8, LANES), bf16(half_shares * ray_rows + 16, 2 * LANES)]
        else:
            out_shape += [f32(8, LANES)]
        kernel = functools.partial(half_ray_kernel, half_shares, len(lefts) > 1, narrow, update, len(after))
        args = [*after, *parts, *lefts, beta]
        specs = [ANY] * len(after) + [VMEM] * (len(args) - len(after))
        return call(kernel, "half_ray", out_shape, args, specs, (), 2 * 10**9)

    def share(selector, all_terms, lower_terms):
        scratch = [pltpu.VMEM((rows * per_row, tile_size), jnp.bfloat16)] * (len(lower_terms) > 0)
        kernel = functools.partial(share_kernel, len(lower_terms))
        args = [selector, all_terms, *lower_terms]
        return call(kernel, "share", f32(share_rows, tile_size), args, None, scratch)

    far = pltpu.with_memory_space_constraint(tile_values, pltpu.HBM)
    blocks = call(pack_kernel, "pack", f32(per_share + 1, 8, LANES), [observed, far], [VMEM, HBM])
    keys = call(keys_kernel, "keys", f32(8, per_row), [blocks, tile_cols.T], [ANY, SMEM])
    both = call(join_kernel, "join", f32(2 * per_share + 1, 8, LANES), [blocks, from_peer(blocks, "col", 1)])
    lefts = exchange(both, "col", 2)
    terms, remainder = adjoint(lefts, True, [])
    terms = exchange(terms, "row")
    own, other, beta, upper_terms, right_raw, equal, weight, all_keys = voxel(terms, [], True)
    betas, alphas, combined = [], [], []
    remainders = [None] * rows
    for iteration in range(ITERS):
        last = iteration == ITERS - 1
        betas.append(beta)
        combined.append(upper_terms)
        crossing = range(1, rows // 2 + 1) if iteration == 0 else range(rows // 2 + 1, rows) if last else []
        summed, *passed = pair(own, other, [remainder] * (len(crossing) > 0), last)
        gathered = exchange(summed, "col", 2)
        for d in crossing:
            remainders[d] = from_peer(passed[0], "row", d)
        after = [remainders[d] for d in crossing]
        if last:
            alpha, squares = half_ray(gathered, lefts, beta, [], True, False)
            _, left_raw, half = half_ray(gathered, lefts, beta, [], True, True)
        else:
            alpha, left_raw, half = half_ray(gathered, lefts, beta, [], False, True)
        alphas.append(alpha)
        lefts = [left_raw]
        other_half = from_peer(half, "col", 1)
        done = call(own_adjoint_kernel, "own_adjoint", bf16(per_row // 2, tile_size), [tile_values, half])
        (new_terms,) = adjoint([done, half, other_half], False, after)
        if iteration == 0:
            selector = call(pick_kernel, "pick", bf16(share_rows, rows * per_row), [new_terms, all_keys], [ANY, VMEM])
        new_terms = exchange(new_terms, "row")
        fixed = [equal, weight, right_raw, alpha]
        own, other, beta, upper_terms = voxel(new_terms, fixed, False)
        right_raw = voxel(new_terms, fixed, True)[4]
    remainders[0] = remainder
    products = [share(selector, c, [] if i else remainders) for i, c in enumerate(combined)]
    squares = call(sum_kernel, "sum", f32(8, LANES), [squares, from_peer(squares, "col", 1)])
    result, ratio = pl.pallas_call(
        functools.partial(final_kernel, rows, ITERS),
        out_shape=[f32(RHS, col_tiles // rows * tile_size), f32(RHS)],
        in_specs=[VMEM] * (rows + 3 * ITERS),
        out_specs=[VMEM, SMEM],
        compiler_params=PARAMS,
        name="final",
    )(*exchange(squares, "row"), *betas, *alphas, *products)
    return result, ratio


def solution(mesh):
    in_specs = (P(None, ("row", "col")), P("row", "col", None, None), P("row", "col"))
    out_specs = (P(None, ("col", "row")), P())
    return jax.shard_map(local, mesh=mesh, in_specs=in_specs, out_specs=out_specs, check_vma=False)
```

```python
import functools

import jax
import jax.numpy as jnp
from jax import lax
from jax.experimental import pallas as pl
from jax.experimental.pallas import tpu as pltpu
from jax.sharding import PartitionSpec as P

ITERS = 2
N = 1048576
epsilon_sq = 1e-06
LANES = 128
RHS = 4
VMEM = pl.BlockSpec(memory_space=pltpu.VMEM)
SMEM = pl.BlockSpec(memory_space=pltpu.SMEM)
HBM = pl.BlockSpec(memory_space=pltpu.HBM)
ANY = pl.BlockSpec(memory_space=pl.ANY)
PARAMS = pltpu.CompilerParams(vmem_limit_bytes=32 * 1024 * 1024)


def tree_sum(parts):
    while len(parts) > 1:
        paired = [parts[i] + parts[i + 1] for i in range(0, len(parts) - 1, 2)]
        parts = paired + parts[2 * len(paired) :]
    return parts[0]


def norm_of(acc):
    rows = jnp.broadcast_to(jnp.sum(acc, axis=1, keepdims=True), acc.shape)
    return jnp.sqrt(rows + pltpu.roll(rows, 4, 0) + epsilon_sq)


def low_half(width):
    return lax.broadcasted_iota(jnp.int32, (8, width), 0) < 4


def in_two(acc):
    upper = acc.astype(jnp.bfloat16).astype(jnp.float32)
    return upper, acc - upper


def packed(blocks, rows):
    blank = [jnp.zeros((8, LANES), jnp.float32)] * (rows // 8)
    halves = [jnp.concatenate((blocks[h::2] + blank)[: rows // 8], axis=0) for h in range(2)]
    return jnp.concatenate(halves, axis=1).astype(jnp.bfloat16)


def packed_squares(acc):
    return jnp.concatenate(in_two(acc), axis=0).astype(jnp.bfloat16)


def read_squares(both):
    both = both.astype(jnp.float32)
    return both[:8] + both[8:16]


def ray_blocks(obs_ref, count):
    obs = obs_ref[...]
    blocks = []
    for b in range(count):
        at = (b // 2) * 4 * LANES + (b % 2) * LANES
        blocks.append(jnp.concatenate([obs[:, at : at + LANES], obs[:, at + 2 * LANES : at + 3 * LANES]], axis=0))
    return blocks


def pack_kernel(obs_ref, blocks_ref):
    count = blocks_ref.shape[0] - 1
    blocks = ray_blocks(obs_ref, count)
    for b, block in enumerate(blocks):
        blocks_ref[b] = block
    blocks_ref[count] = tree_sum([b * b for b in blocks])


def join_kernel(own_ref, other_ref, unread_ref, both_ref):
    count = own_ref.shape[0] - 1
    both_ref[:count] = own_ref[:count]
    both_ref[count : 2 * count] = other_ref[:count]
    both_ref[2 * count] = own_ref[count] + other_ref[count]


def keys_kernel(unread_ref, cols_ref, keys_ref):
    keys_ref[...] = key_row(cols_ref)


def key_row(cols_ref):
    per_block, row_tiles = cols_ref.shape
    width = per_block * row_tiles * RHS
    lane = lax.broadcasted_iota(jnp.int32, (8, width), 1)
    keys = jnp.zeros((8, width), jnp.int32)
    for i in range(row_tiles):
        for k in range(per_block):
            keys = jnp.where(lane // RHS == i * per_block + k, cols_ref[k, i], keys)
    return (keys * RHS + lane % RHS).astype(jnp.float32)


def fill_equal(keys_ref, equal_ref, weight_ref):
    rows, _, per_row = keys_ref.shape

    @pl.loop(0, rows)
    def _(s):
        down = jnp.broadcast_to(keys_ref[s][:1], (LANES, per_row)).T
        at = pl.ds(pl.multiple_of(s * per_row, per_row), per_row)
        count = jnp.zeros((per_row, LANES), jnp.float32)
        for other in range(rows):
            for h in range(per_row // LANES):
                across = keys_ref[other, :1, h * LANES : (h + 1) * LANES]
                same = jnp.where(down == across, 1.0, 0.0)
                count = count + same
                lane = other * per_row + h * LANES
                equal_ref[at, lane : lane + LANES] = same.astype(jnp.bfloat16)
        weight_ref[at, :] = jnp.broadcast_to(1.0 / jnp.sum(count, axis=1, keepdims=True), (per_row, LANES))


def fill_pick(keys_ref, pick_ref):
    rows, _, per_row = keys_ref.shape
    wanted = pick_ref.shape[0]
    step_rows = 128
    start = lax.axis_index("row") * wanted

    @pl.loop(0, wanted // step_rows)
    def _(step):
        down = lax.broadcasted_iota(jnp.int32, (step_rows, LANES), 0) + (start + step * step_rows)
        down = down.astype(jnp.float32)
        at = pl.ds(pl.multiple_of(step * step_rows, step_rows), step_rows)
        for other in range(rows):
            for h in range(per_row // LANES):
                across = keys_ref[other, :1, h * LANES : (h + 1) * LANES]
                lane = other * per_row + h * LANES
                pick_ref[at, lane : lane + LANES] = jnp.where(down == across, 1.0, 0.0).astype(jnp.bfloat16)


def adjoint_rows(rays, tiles_ref, owner, per_share, g):
    low = low_half(2 * LANES)
    i = owner * per_share + 2 * g
    wide = [
        jnp.dot(rays, tiles_ref[i + e, k], preferred_element_type=jnp.float32)[8 * g : 8 * g + 8]
        for e in range(2)
        for k in range(2)
    ]
    value = jnp.concatenate(
        [
            jnp.where(low, wide[0], pltpu.roll(wide[1], 4, 0)),
            jnp.where(low, pltpu.roll(wide[2], 4, 0), wide[3]),
        ],
        axis=0,
    )
    return value, pl.multiple_of(8 * i, 16)


def half_sources(half_ref, half):
    peers = lax.axis_size("col") // 2
    rows = (half_ref.shape[0] - 16) // peers
    core = jnp.bitwise_xor(lax.axis_index("col") % 2, half)
    return [(2 * slot + core, half_ref[slot * rows : (slot + 1) * rows]) for slot in range(peers)]


def own_adjoint_kernel(tiles_ref, half_ref, out_ref):
    per_share = tiles_ref.shape[0] // lax.axis_size("col")
    at = 0
    for owner, rays in half_sources(half_ref, 0):
        for g in range(per_share // 2):
            value, _ = adjoint_rows(rays, tiles_ref, owner, per_share, g)
            out_ref[at : at + 16] = value.astype(jnp.bfloat16)
            at += 16


def pair_sources(pair, e, per_share):
    me = lax.axis_index("col")
    sources = []
    for h in range(2):
        blocks = [pair[h * per_share + b] for b in range(per_share)]
        sources.append((jnp.bitwise_xor(me, 2 * e + h), packed(blocks, max(16, 4 * per_share))))
    return sources


def pair_adjoint_kernel(tiles_ref, pair_ref, upper_ref, lower_ref):
    per_share = tiles_ref.shape[0] // lax.axis_size("col")
    at = 0
    for owner, rays in pair_sources(pair_ref, 0, per_share):
        for g in range(per_share // 2):
            value, _ = adjoint_rows(rays, tiles_ref, owner, per_share, g)
            upper = value.astype(jnp.bfloat16)
            upper_ref[at : at + 16] = upper
            lower_ref[at : at + 16] = (value - upper.astype(jnp.float32)).astype(jnp.bfloat16)
            at += 16


def adjoint_kernel(first, unread, keys_ref, tiles_ref, *refs):
    refs = refs[unread:]
    row_tiles, per_block = tiles_ref.shape[:2]
    shares = lax.axis_size("col")
    me = lax.axis_index("col")
    per_share = row_tiles // shares
    terms = row_tiles * per_block * RHS
    if first:
        done_ref, done_lower_ref = refs[:2]
        pairs, (term_ref, lower_ref) = refs[2:-2], refs[-2:]
        squares = [pair[2 * per_share] for pair in pairs]
        sources = [x for e in range(1, shares // 2) for x in pair_sources(pairs[e], e, per_share)]
        at = 0
        for h in range(2):
            for g in range(per_share // 2):
                i = jnp.bitwise_xor(me, h) * per_share + 2 * g
                to = pl.ds(pl.multiple_of(8 * i, 16), 16)
                term_ref[to, :] = done_ref[at : at + 16]
                lower_ref[to, :] = done_lower_ref[at : at + 16]
                at += 16
    else:
        done_ref, own_ref, other_ref, term_ref = refs
        squares = [read_squares(half[-16:, :LANES]) for half in (own_ref, other_ref)]
        sources = half_sources(other_ref, 1)
        at = 0
        for slot in range(shares // 2):
            for g in range(per_share // 2):
                i = (2 * slot + me % 2) * per_share + 2 * g
                term_ref[pl.ds(pl.multiple_of(8 * i, 16), 16), :] = done_ref[at : at + 16]
                at += 16
    squares = tree_sum(squares)
    pieces = jnp.concatenate(in_two(squares), axis=1)
    extra = jnp.zeros_like(pieces)
    if first:
        keys = keys_ref[...]
        coarse = jnp.floor(keys * (1.0 / 64))
        extra = jnp.where(low_half(2 * LANES), coarse, keys - 64 * coarse)
    term_ref[terms:] = jnp.concatenate([pieces, extra], axis=0).astype(jnp.bfloat16)
    for owner, rays in sources:
        for g in range(per_share // 2):
            value, at = adjoint_rows(rays, tiles_ref, owner, per_share, g)
            upper = value.astype(jnp.bfloat16)
            term_ref[pl.ds(at, 16), :] = upper
            if first:
                lower_ref[pl.ds(at, 16), :] = (value - upper.astype(jnp.float32)).astype(jnp.bfloat16)


def voxel_kernel(first, rows, tiles_ref, *refs):
    terms, refs = refs[:rows], list(refs[rows:])
    if first:
        lhs_ref, acc_ref, other_ref, beta_ref, all_ref, raw_ref, equal_ref, weight_ref, keys_ref = refs
    else:
        equal_ref, weight_ref, right_ref, alpha_ref = refs[:4]
        lhs_ref, acc_ref, other_ref, beta_ref, all_ref, raw_ref = refs[-6:]
    my_row = lax.axis_index("row")
    row_tiles, per_block = tiles_ref.shape[:2]
    per_row = row_tiles * per_block * RHS
    low = low_half(2 * LANES)
    squares = []
    for d in range(rows):
        slot = jnp.bitwise_xor(my_row, d)
        at = pl.ds(pl.multiple_of(slot * per_row, per_row), per_row)
        all_ref[at, :] = terms[d][:per_row]
        extra = terms[d][per_row:].astype(jnp.float32)
        squares.append(extra[:8, :LANES] + extra[:8, LANES:])
        if first:
            pieces = jnp.where(low, extra[8:] * 64, extra[8:])
            keys_ref[slot] = pieces + pltpu.roll(pieces, 4, 0)
    if first:
        fill_equal(keys_ref, equal_ref, weight_ref)
    beta = norm_of(tree_sum(squares))
    beta_ref[...] = beta
    wide_scale = jnp.concatenate([1.0 / beta] * 2, axis=1)
    if not first:
        wide_right = jnp.concatenate([beta / alpha_ref[...]] * 2, axis=1)
    acc = jnp.zeros((8, LANES), jnp.float32)
    for s in range(rows):
        same = equal_ref[s * per_row : (s + 1) * per_row, :]
        summed = jnp.dot(same, all_ref[...], preferred_element_type=jnp.float32)
        for m in range(per_row // 8):
            at = s * per_row + 8 * m
            raw = summed[8 * m : 8 * m + 8] * wide_scale
            if not first:
                raw = raw - right_ref[at : at + 8] * wide_right
            raw_ref[at : at + 8] = raw
            square = raw * raw
            acc = acc + (square[:, :LANES] + square[:, LANES:]) * weight_ref[at : at + 8]
    lhs_ref[...] = raw_ref[pl.ds(pl.multiple_of(my_row * per_row, 16), per_row), :].astype(jnp.bfloat16)
    forward_half(1, tiles_ref, lhs_ref, other_ref)
    other_ref[other_ref.shape[0] - 1] = acc
    acc_ref[...] = acc


def forward_half(half, tiles_ref, lhs_ref, out_ref):
    shares = lax.axis_size("col")
    per_share = tiles_ref.shape[0] // shares
    low = low_half(2 * LANES)
    core = lax.axis_index("col") % 2
    for slot in range(shares // 2):
        c = 2 * slot + jnp.bitwise_xor(core, half)
        for g in range(per_share // 2):
            i = c * per_share + 2 * g
            lhs = lhs_ref[pl.ds(pl.multiple_of(8 * i, 16), 16), :]
            wide = [
                lax.dot_general(
                    lhs, tiles_ref[i + e, k], (((1,), (1,)), ((), ())), preferred_element_type=jnp.float32
                )[8 * e : 8 * e + 8]
                for e in range(2)
                for k in range(2)
            ]
            value = jnp.where(low, wide[0], wide[3]) + pltpu.roll(jnp.where(low, wide[2], wide[1]), 4, 0)
            at = slot * per_share + 2 * g
            out_ref[at] = value[:, :LANES]
            out_ref[at + 1] = value[:, LANES:]


def forward_kernel(tiles_ref, lhs_ref, acc_ref, own_ref):
    forward_half(0, tiles_ref, lhs_ref, own_ref)
    own_ref[own_ref.shape[0] - 1] = acc_ref[...]


def pair_kernel(narrow, own_ref, other_ref, *refs):
    passed = len(refs) // 2
    out_ref = refs[passed]
    for i in range(passed):
        refs[1 + passed + i][...] = refs[i][...]
    if not narrow:
        out_ref[...] = own_ref[...] + other_ref[...]
        return
    count = own_ref.shape[0] - 1
    for b in range(0, count, 2):
        two = [own_ref[b + i] + other_ref[b + i] for i in range(2)]
        out_ref[8 * b : 8 * b + 16, :] = jnp.concatenate(two, axis=0).astype(jnp.bfloat16)
    out_ref[8 * count :, :] = packed_squares(own_ref[count] + other_ref[count])


def sum_kernel(own_ref, other_ref, out_ref):
    out_ref[...] = own_ref[...] + other_ref[...]


def half_ray_kernel(peers, first, narrow, update, unread, *refs):
    refs = refs[unread:]
    parts, refs = refs[:peers], refs[peers:]
    if update:
        lefts, (beta_ref, alpha_ref, raw_ref, half_ref) = refs[:-4], refs[-4:]
        rows = (half_ref.shape[0] - 16) // peers
    else:
        lefts, (beta_ref, alpha_ref, acc_ref) = refs[:-3], refs[-3:]
    if narrow:
        count = (parts[0].shape[0] - 16) // 8
        squares = [read_squares(p[8 * count :, :]) for p in parts]
    else:
        count = parts[0].shape[0] - 1
        squares = [p[count] for p in parts]
    per_share = count // peers
    alpha = norm_of(tree_sum(squares))
    alpha_ref[...] = alpha
    alpha_inv = 1.0 / alpha
    left_scale = alpha / beta_ref[...]
    squares = []
    for e in range(peers):
        slot = jnp.bitwise_xor(lax.axis_index("col") // 2, e)
        if narrow:
            at = pl.ds(pl.multiple_of(slot * per_share * 8, 16), per_share * 8)
            whole = tree_sum([p[at, :].astype(jnp.float32) for p in parts])
            totals = [whole[8 * b : 8 * b + 8] for b in range(per_share)]
        else:
            totals = [tree_sum([p[slot * per_share + b] for p in parts]) for b in range(per_share)]
        blocks = []
        for b in range(per_share):
            at = slot * per_share + b
            left = lefts[e][b] if first else lefts[0][at]
            blocks.append(totals[b] * alpha_inv - left * left_scale)
            if update:
                raw_ref[at] = blocks[-1]
        if update:
            half_ref[pl.ds(pl.multiple_of(slot * rows, 16), rows), :] = packed(blocks, rows)
        squares.append(tree_sum([b * b for b in blocks]))
    acc = tree_sum(squares)
    if update:
        pieces = packed_squares(acc)
        half_ref[peers * rows :, :LANES] = pieces
        half_ref[peers * rows :, LANES:] = jnp.zeros_like(pieces)
    else:
        acc_ref[...] = acc


def share_kernel(remainders, *refs):
    pick_ref, all_ref = refs[:2]
    lower_terms, out_ref = refs[2 : 2 + remainders], refs[2 + remainders]
    values = [all_ref]
    if remainders:
        held = refs[-1]
        per_row = lower_terms[0].shape[0]
        for d, term in enumerate(lower_terms):
            slot = jnp.bitwise_xor(lax.axis_index("row"), d)
            held[pl.ds(pl.multiple_of(slot * per_row, per_row), per_row), :] = term[...]
        values.append(held)
    step = 128
    for at in range(0, out_ref.shape[0], step):
        pick = pick_ref[at : at + step, :]
        out_ref[at : at + step, :] = tree_sum(
            [jnp.dot(pick, v[...], preferred_element_type=jnp.float32) for v in values]
        )


def pick_kernel(unread_ref, keys_ref, pick_ref):
    fill_pick(keys_ref, pick_ref)


def final_kernel(rows, iters, *refs):
    refs = list(refs)
    last = [refs.pop(0) for _ in range(rows)]
    betas = [refs.pop(0) for _ in range(iters)]
    alphas = [refs.pop(0) for _ in range(iters)]
    products = [refs.pop(0) for _ in range(iters)]
    out_ref, ratio_ref = refs
    beta = [b[...] for b in betas] + [norm_of(tree_sum([p[...] for p in last]))]
    alpha = [a[...] for a in alphas]
    phibar, rhobar = beta[0], alpha[0]
    direction = [1.0 / alpha[0]] + [jnp.zeros_like(phibar)] * (iters - 1)
    weights = [jnp.zeros_like(phibar)] * iters
    for i in range(iters):
        rho = jnp.sqrt(rhobar * rhobar + beta[i + 1] * beta[i + 1])
        cosine, sine = rhobar / rho, beta[i + 1] / rho
        phi = cosine * phibar
        phibar = sine * phibar
        weights = [w + (phi / rho) * d for w, d in zip(weights, direction)]
        if i + 1 < iters:
            theta = sine * alpha[i + 1]
            rhobar = -cosine * alpha[i + 1]
            direction = [-(theta / rho) * d for d in direction]
            direction[i + 1] = direction[i + 1] + 1.0 / alpha[i + 1]
    ratio = phibar / beta[0]
    for n in range(RHS):
        ratio_ref[n] = jnp.max(ratio[n : n + 1])
    scales = []
    carried = jnp.zeros_like(phibar)
    for i in reversed(range(iters)):
        carried = weights[i] - carried
        scales.insert(0, jnp.concatenate([carried / beta[i]] * 2, axis=1))
        if i > 0:
            carried = carried * (beta[i] / alpha[i - 1])
    unroll = 4

    @pl.loop(0, products[0].shape[0] // (8 * unroll))
    def _(step):
        for u in range(unroll):
            m = step * unroll + u
            at = pl.ds(pl.multiple_of(m * 8, 8), 8)
            both = tree_sum([p[at, :] * s for p, s in zip(products, scales)])
            lane = pl.multiple_of(m * 4 * LANES, 4 * LANES)
            out_ref[:, pl.ds(lane, 2 * LANES)] = both[:4]
            out_ref[:, pl.ds(lane + 2 * LANES, 2 * LANES)] = both[4:]


def f32(*shape):
    return jax.ShapeDtypeStruct(shape, jnp.float32)


def bf16(*shape):
    return jax.ShapeDtypeStruct(shape, jnp.bfloat16)


def from_peer(value, axis, d):
    return lax.ppermute(value, axis, [(i, i ^ d) for i in range(lax.axis_size(axis))])


def exchange(value, axis, step=1):
    return [value] + [from_peer(value, axis, d) for d in range(step, lax.axis_size(axis), step)]


def local(observed, tile_values, tile_cols):
    row_tiles, per_block, tile_size = tile_values.shape[:3]
    rows, shares = lax.axis_size("row"), lax.axis_size("col")
    col_tiles = N // (tile_size * shares)
    per_share = row_tiles // shares
    per_row = row_tiles * per_block * RHS
    share_rows = col_tiles // rows * RHS
    ray_rows = max(16, RHS * per_share)
    half_shares = shares // 2
    half_blocks = half_shares * per_share
    def call(kernel, name, out_shape, args, in_specs=None, scratch=(), flops=None):
        return pl.pallas_call(
            kernel,
            out_shape=out_shape,
            in_specs=in_specs or [VMEM] * len(args),
            out_specs=jax.tree.map(lambda _: VMEM, out_shape),
            scratch_shapes=list(scratch),
            compiler_params=PARAMS,
            cost_estimate=flops and pl.CostEstimate(flops=flops, bytes_accessed=0, transcendentals=0),
            name=name,
        )(*args)

    def adjoint(payloads, first, after):
        out_shape = [bf16(per_row + 16, tile_size)] + [bf16(per_row, tile_size)] * first
        args = [keys, tile_values, *after, *payloads]
        specs = [VMEM] * 2 + [ANY] * len(after) + [VMEM] * len(payloads)
        return call(functools.partial(adjoint_kernel, first, len(after)), "adjoint", out_shape, args, specs)

    def voxel(term_list, previous, keep):
        first = not previous
        out_shape = [bf16(per_row, tile_size), f32(8, LANES), f32(half_blocks + 1, 8, LANES)]
        out_shape += [f32(8, LANES), bf16(rows * per_row, tile_size)]
        raw_shape = (rows * per_row, tile_size)
        out_shape += [f32(*raw_shape)] * keep
        if first:
            out_shape += [
                bf16(rows * per_row, rows * per_row),
                f32(rows * per_row, LANES),
                f32(rows, 8, per_row),
            ]
        args = [tile_values, *term_list, *previous]
        scratch = [pltpu.VMEM(raw_shape, jnp.float32)] * (not keep)
        lhs, acc, other, *rest = call(
            functools.partial(voxel_kernel, first, rows), "voxel", out_shape, args, None, scratch
        )
        own = call(forward_kernel, "forward", f32(half_blocks + 1, 8, LANES), [tile_values, lhs, acc])
        return own, other, *rest

    def pair(own, other, passed, narrow):
        args = [own, from_peer(other, "col", 1), *passed]
        out_shape = [jax.ShapeDtypeStruct(x.shape, x.dtype) for x in [own, *passed]]
        if narrow:
            out_shape[0] = bf16(8 * half_blocks + 16, LANES)
        return call(functools.partial(pair_kernel, narrow), "pair", out_shape, args)

    def half_ray(parts, lefts, beta, after, narrow, update):
        out_shape = [f32(8, LANES)]
        if update:
            out_shape += [f32(half_blocks, 8, LANES), bf16(half_shares * ray_rows + 16, 2 * LANES)]
        else:
            out_shape += [f32(8, LANES)]
        kernel = functools.partial(half_ray_kernel, half_shares, len(lefts) > 1, narrow, update, len(after))
        args = [*after, *parts, *lefts, beta]
        specs = [ANY] * len(after) + [VMEM] * (len(args) - len(after))
        return call(kernel, "half_ray", out_shape, args, specs, (), 2 * 10**9)

    def share(selector, all_terms, lower_terms):
        scratch = [pltpu.VMEM((rows * per_row, tile_size), jnp.bfloat16)] * (len(lower_terms) > 0)
        kernel = functools.partial(share_kernel, len(lower_terms))
        args = [selector, all_terms, *lower_terms]
        return call(kernel, "share", f32(share_rows, tile_size), args, None, scratch)

    far = pltpu.with_memory_space_constraint(tile_values, pltpu.HBM)
    blocks = call(pack_kernel, "pack", f32(per_share + 1, 8, LANES), [observed])
    keys = call(keys_kernel, "keys", f32(8, per_row), [blocks, tile_cols.T], [ANY, SMEM])
    both = call(
        join_kernel,
        "join",
        f32(2 * per_share + 1, 8, LANES),
        [blocks, from_peer(blocks, "col", 1), far],
        [VMEM, VMEM, HBM],
    )
    lefts = exchange(both, "col", 2)
    done = call(pair_adjoint_kernel, "pair_adjoint", [bf16(2 * per_share * 8, tile_size)] * 2, [tile_values, both])
    terms, remainder = adjoint([*done, *lefts], True, [])
    terms = exchange(terms, "row")
    own, other, beta, upper_terms, right_raw, equal, weight, all_keys = voxel(terms, [], True)
    betas, alphas, combined = [], [], []
    remainders = [None] * rows
    for iteration in range(ITERS):
        last = iteration == ITERS - 1
        betas.append(beta)
        combined.append(upper_terms)
        crossing = range(1, rows // 2 + 1) if iteration == 0 else range(rows // 2 + 1, rows) if last else []
        summed, *passed = pair(own, other, [remainder] * (len(crossing) > 0), last)
        gathered = exchange(summed, "col", 2)
        for d in crossing:
            remainders[d] = from_peer(passed[0], "row", d)
        after = [remainders[d] for d in crossing]
        if last:
            alpha, squares = half_ray(gathered, lefts, beta, [], True, False)
            _, left_raw, half = half_ray(gathered, lefts, beta, [], True, True)
        else:
            alpha, left_raw, half = half_ray(gathered, lefts, beta, [], False, True)
        alphas.append(alpha)
        lefts = [left_raw]
        other_half = from_peer(half, "col", 1)
        done = call(own_adjoint_kernel, "own_adjoint", bf16(per_row // 2, tile_size), [tile_values, half])
        (new_terms,) = adjoint([done, half, other_half], False, after)
        if iteration == 0:
            selector = call(pick_kernel, "pick", bf16(share_rows, rows * per_row), [new_terms, all_keys], [ANY, VMEM])
        new_terms = exchange(new_terms, "row")
        fixed = [equal, weight, right_raw, alpha]
        own, other, beta, upper_terms = voxel(new_terms, fixed, False)
        right_raw = voxel(new_terms, fixed, True)[4]
    remainders[0] = remainder
    products = [share(selector, c, [] if i else remainders) for i, c in enumerate(combined)]
    squares = call(sum_kernel, "sum", f32(8, LANES), [squares, from_peer(squares, "col", 1)])
    result, ratio = pl.pallas_call(
        functools.partial(final_kernel, rows, ITERS),
        out_shape=[f32(RHS, col_tiles // rows * tile_size), f32(RHS)],
        in_specs=[VMEM] * (rows + 3 * ITERS),
        out_specs=[VMEM, SMEM],
        compiler_params=PARAMS,
        name="final",
    )(*exchange(squares, "row"), *betas, *alphas, *products)
    return result, ratio


def solution(mesh):
    in_specs = (P(None, ("row", "col")), P("row", "col", None, None), P("row", "col"))
    out_specs = (P(None, ("col", "row")), P())
    return jax.shard_map(local, mesh=mesh, in_specs=in_specs, out_specs=out_specs, check_vma=False)
```
